32 devices in a mesh: dp: 4 (over x, core), expert: 8 (over z, y).
Axes of the slice: x: 2, y: 2, z: 4, core: 2. Of those that a mesh axis runs over, the one named last changes fastest.
Arguments:
- events: bfloat16 [64, 1024], P(('dp', 'expert')), may hold values from -6 to 6
- labels: int32 [64, 4], P(('dp', 'expert')), may hold values 0 or 1
- w_in: bfloat16 [8, 1024, 4096], P('expert', None, 'dp'), may hold values from -0.1875 to 0.1875
- w_out: bfloat16 [8, 4096, 1024], P('expert', 'dp'), may hold values from -0.09375 to 0.09375
- gate_weight: bfloat16 [4, 1024, 8], replicated, may hold values from -4 to 4
- tower_in: bfloat16 [4, 1024, 256], replicated, may hold values from -0.1875 to 0.1875
- tower_bias: float32 [4, 256], replicated, may hold values from -3 to 3
- tower_out: float32 [4, 256], replicated, may hold values from -0.75 to 0.75
- tower_out_bias: float32 [4], replicated, may hold values from -3 to 3
Outputs:
- grad_in: bfloat16 [8, 1024, 4096], P('expert', None, 'dp')
- grad_out: bfloat16 [8, 4096, 1024], P('expert', 'dp')
- grad_gate: float32 [4, 1024, 8], P(None, None, 'expert')
The draws below stay inside these ranges and needn't reach their ends.
All inputs are finite; a program needn't handle non-finite values. No bound on the sum of `labels` on one device may be relied on, other than what follows from the above.
Results may differ from the reference program's by a relative error of at most 0.035.
Values may be sent and summed in bfloat16 or wider, within the bound.
No kernel may reach another device: no remote copies, remote signals or barrier semaphores. Data moves between devices by JAX's collectives and lax.ppermute only.
A program may use at most 64 MiB of HBM per device.

```python
import jax
import jax.numpy as jnp
from jax import lax

D = 1024
H = 4096
TASKS = 4
TW = 256
E = 8
ROWS = 64
N_DP = 4


def draw_gate_weight(key, part):
    key = jax.random.fold_in(key, 5)
    first = jax.random.fold_in(key, 0)
    values = jax.random.normal(first, (TASKS, D, E), jnp.float32) * (2.0 / D ** 0.5)
    return jnp.clip(values, -4.0, 4.0).astype(jnp.bfloat16)


def set_ends(values, rng, smallest, high):
    longest = values.shape.index(max(values.shape))
    spots = []
    for shift in (0, 1):
        where = [jax.random.randint(jax.random.fold_in(rng, axis), (), 0, length) for axis, length in enumerate(values.shape)]
        where[longest] = (where[longest] + shift) % values.shape[longest]
        spots.append(tuple(where))
    return values.at[spots[0]].set(smallest).at[spots[1]].set(high)


def shard_levels(rng, dims, shards, least, top_value):
    level = 1.0
    for axis_at, shards_of in shards:
        heights = jax.random.uniform(jax.random.fold_in(jax.random.fold_in(rng, 6), axis_at), (shards_of,), jnp.float32, least / len(shards), top_value / len(shards))
        level = level * jnp.repeat(jnp.exp(heights), dims[axis_at] // shards_of).reshape((-1,) + (1,) * (len(dims) - 1 - axis_at))
    return level


def normal_values(key, dims, scale, reach, cuts=(), held_as=jnp.bfloat16):
    array = scale * jax.random.normal(key, dims, jnp.float32)
    if cuts:
        array = array * shard_levels(key, dims, cuts, -0.22, 0.18)
    return jnp.clip(array, -reach, reach).astype(held_as)


def setup_inputs(seed: int = 0) -> dict:
    seeds = jax.random.split(jax.random.key(seed), 10)
    return {
        "events": normal_values(seeds[0], (ROWS, D), 1.0, 6.0, ((0, 32),)),
        "labels": set_ends((jax.random.randint(seeds[1], (ROWS, TASKS), 0, 2) < 1).astype(jnp.int32), jax.random.fold_in(seeds[1], 1), 0, 1),
        "w_in": normal_values(seeds[2], (E, D, H), D ** -0.5, 0.1875, ((0, 8), (2, 4))),
        "w_out": normal_values(seeds[3], (E, H, D), H ** -0.5, 0.09375, ((0, 8), (1, 4))),
        "gate_weight": draw_gate_weight(jax.random.fold_in(seeds[9], 71), 0),
        "tower_in": normal_values(seeds[5], (TASKS, D, TW), D ** -0.5, 0.1875),
        "tower_bias": normal_values(seeds[6], (TASKS, TW), 0.5, 3.0, (), jnp.float32),
        "tower_out": normal_values(seeds[7], (TASKS, TW), (TW // 4) ** -0.5, 0.75, (), jnp.float32),
        "tower_out_bias": normal_values(seeds[8], (TASKS,), 1.0, 3.0, (), jnp.float32),
    }


def gelu_tanh(value):
    return jax.nn.gelu(value, approximate=True)

def tower_apply(mixed, tower_in, tower_bias, tower_out, tower_out_bias):
    tower_pre = jnp.einsum('trd,tdk->trk', mixed, tower_in.astype(jnp.float32), precision=lax.Precision.HIGHEST) + tower_bias[:, None, :]
    return lax.optimization_barrier(jnp.sum(gelu_tanh(tower_pre) * tower_out[:, None, :], -1)) + tower_out_bias[:, None]

def reference(events, labels, w_in, w_out, gate_weight, tower_in, tower_bias, tower_out, tower_out_bias):
    rows = events.shape[0]
    blocks = N_DP
    width = w_in.shape[2] // blocks

    def forward(pair):
        weight_in, weight_out = pair
        pre = jnp.dot(events, weight_in, preferred_element_type=jnp.float32)
        hidden = gelu_tanh(pre).astype(jnp.bfloat16)
        parts = jnp.einsum('rjk,jkd->jrd', hidden.reshape(rows, blocks, width).astype(jnp.float32), weight_out.reshape(blocks, width, -1).astype(jnp.float32), precision=lax.Precision.HIGHEST)
        rounded = lax.optimization_barrier(parts.astype(jnp.bfloat16)).astype(jnp.float32)
        return lax.optimization_barrier(jnp.sum(rounded, 0)).astype(jnp.bfloat16)
    expert_out = lax.map(forward, (w_in, w_out))
    events_wide = events.astype(jnp.float32)
    gate_logits = jnp.einsum('rd,tde->tre', events_wide, gate_weight.astype(jnp.float32), precision=lax.Precision.HIGHEST)
    probs = jax.nn.softmax(gate_logits, axis=-1)
    outs_wide = expert_out.astype(jnp.float32)
    mixed = jnp.einsum('tre,erd->trd', probs, outs_wide, precision=lax.Precision.HIGHEST).astype(jnp.bfloat16)
    targets = labels.T.astype(jnp.float32)

    def tower_of(value):
        return tower_apply(value, tower_in, tower_bias, tower_out, tower_out_bias)
    logit, tower_back = jax.vjp(tower_of, mixed.astype(jnp.float32))
    dmixed = tower_back(jax.nn.sigmoid(logit) - targets)[0].astype(jnp.bfloat16)
    dmixed_wide = lax.optimization_barrier(dmixed).astype(jnp.float32)
    dprob = jnp.einsum('trd,erd->tre', dmixed_wide, outs_wide, precision=lax.Precision.HIGHEST)
    dgate = probs * (dprob - lax.optimization_barrier(jnp.sum(probs * dprob, -1, keepdims=True)))
    grad_gate = jnp.einsum('rd,tre->tde', events_wide, dgate, precision=lax.Precision.HIGHEST)
    dexpert = jnp.einsum('tre,trd->erd', probs, dmixed_wide, precision=lax.Precision.HIGHEST).astype(jnp.bfloat16)

    def backward(triple):
        weight_in, weight_out, grad_rows = triple
        pre = jnp.dot(events, weight_in, preferred_element_type=jnp.float32)
        hidden = gelu_tanh(pre).astype(jnp.bfloat16)
        dhidden = jnp.dot(grad_rows, weight_out.T, preferred_element_type=jnp.float32)
        gelu_back = jax.vjp(gelu_tanh, pre)[1]
        dpre = gelu_back(dhidden)[0].astype(jnp.bfloat16)
        grad_second = jnp.dot(hidden.T, grad_rows, preferred_element_type=jnp.float32).astype(jnp.bfloat16)
        grad_first = jnp.dot(events.T, dpre, preferred_element_type=jnp.float32).astype(jnp.bfloat16)
        return (grad_first, grad_second)
    grad_in, grad_out = lax.map(backward, (w_in, w_out, dexpert))
    return (grad_in, grad_out, grad_gate)
```

```python
import jax
import jax.numpy as jnp
from jax import lax
from jax.sharding import PartitionSpec as P

BOTH = ("dp", "expert")


def gelu_tanh(value):
    return jax.nn.gelu(value, approximate=True)


def pieces_of(value):
    high = value.astype(jnp.bfloat16)
    rest = value - high.astype(jnp.float32)
    middle = rest.astype(jnp.bfloat16)
    low = (rest - middle.astype(jnp.float32)).astype(jnp.bfloat16)
    return high, middle, low


def per_device(
    events, labels, w_in, w_out, gate_weight, tower_in, tower_bias, tower_out, tower_out_bias
):
    dp = lax.axis_size("dp")
    experts = lax.axis_size("expert")
    devices = dp * experts
    own, width = events.shape
    tasks = tower_in.shape[0]
    rows = devices * own

    gate_logits = jnp.einsum(
        "rd,tde->tre", events, gate_weight, preferred_element_type=jnp.float32
    )
    probs = jax.nn.softmax(gate_logits, axis=-1)

    every = lax.all_to_all(
        jnp.broadcast_to(events[None], (devices, own, width)), BOTH, 0, 0, tiled=True
    ).reshape(rows, width)
    pre = jnp.dot(every, w_in[0], preferred_element_type=jnp.float32)
    hidden = gelu_tanh(pre).astype(jnp.bfloat16)
    part = jnp.dot(hidden, w_out[0], preferred_element_type=jnp.float32).astype(jnp.bfloat16)

    parts = lax.all_to_all(part.reshape(devices, own, width), BOTH, 0, 0, tiled=True)
    parts = parts.reshape(dp, experts, own, width).astype(jnp.float32)
    outs = jnp.sum(parts, 0).astype(jnp.bfloat16)
    outs_wide = outs.astype(jnp.float32)
    mixed = jnp.sum(
        jnp.transpose(probs, (0, 2, 1))[..., None] * outs_wide[None], 1
    ).astype(jnp.bfloat16)
    tower_pre = (
        jnp.einsum("trd,tdk->trk", mixed, tower_in, preferred_element_type=jnp.float32)
        + tower_bias[:, None, :]
    )
    active, gelu_back = jax.vjp(gelu_tanh, tower_pre)
    logit = jnp.sum(active * tower_out[:, None, :], -1) + tower_out_bias[:, None]
    dlogit = jax.nn.sigmoid(logit) - labels.T.astype(jnp.float32)
    dtower = gelu_back(dlogit[..., None] * tower_out[:, None, :])[0]
    stacked = jnp.concatenate(pieces_of(dtower), 1)
    dmixed = jnp.einsum("trk,tdk->trd", stacked, tower_in, preferred_element_type=jnp.float32)
    dmixed = jnp.sum(dmixed.reshape(tasks, 3, own, width), 1).astype(jnp.bfloat16)
    dmixed_wide = dmixed.astype(jnp.float32)
    dprob = jnp.sum(dmixed_wide[:, None] * outs_wide[None], -1)
    probs_ter = jnp.transpose(probs, (0, 2, 1))
    dgate = probs_ter * (dprob - jnp.sum(probs_ter * dprob, 1, keepdims=True))
    dexpert = jnp.sum(probs_ter[..., None] * dmixed_wide[:, None], 0).astype(jnp.bfloat16)

    packed = jnp.transpose(jnp.concatenate(pieces_of(dgate), 0), (1, 2, 0))
    packed = jnp.pad(packed, ((0, 0), (0, 0), (0, 128 - 3 * tasks)))
    message = jnp.concatenate([dexpert, packed], -1)
    message = jnp.broadcast_to(message[None], (dp, experts, own, width + 128))
    message = message.reshape(devices, own, width + 128)
    arrived = lax.all_to_all(message, BOTH, 0, 0, tiled=True).reshape(rows, width + 128)
    all_grads = arrived[:, :width]
    gate_rows = arrived[:, width : width + 3 * tasks]

    dhidden = lax.dot_general(
        all_grads, w_out[0], (((1,), (1,)), ((), ())), preferred_element_type=jnp.float32
    )
    dpre = jax.vjp(gelu_tanh, pre)[1](dhidden)[0].astype(jnp.bfloat16)
    grad_second = lax.dot_general(
        hidden, all_grads, (((0,), (0,)), ((), ())), preferred_element_type=jnp.float32
    ).astype(jnp.bfloat16)
    grad_first = lax.dot_general(
        every, dpre, (((0,), (0,)), ((), ())), preferred_element_type=jnp.float32
    ).astype(jnp.bfloat16)
    grad_gate = lax.dot_general(
        gate_rows, every, (((0,), (0,)), ((), ())), preferred_element_type=jnp.float32
    )
    grad_gate = jnp.sum(grad_gate.reshape(3, tasks, width), 0)
    return (grad_first[None], grad_second[None], grad_gate[:, :, None])


def solution(mesh):
    placed = (
        P(BOTH, None),
        P(BOTH, None),
        P("expert", None, "dp"),
        P("expert", "dp", None),
        P(),
        P(),
        P(),
        P(),
        P(),
    )
    return jax.shard_map(
        per_device,
        mesh=mesh,
        in_specs=placed,
        out_specs=(P("expert", None, "dp"), P("expert", "dp", None), P(None, None, "expert")),
        check_vma=False,
    )
```

```python
import jax
import jax.numpy as jnp
from jax import lax
from jax.sharding import PartitionSpec as P

BOTH = ("dp", "expert")


def gelu_tanh(value):
    return jax.nn.gelu(value, approximate=True)


def pieces_of(value):
    high = value.astype(jnp.bfloat16)
    rest = value - high.astype(jnp.float32)
    middle = rest.astype(jnp.bfloat16)
    low = (rest - middle.astype(jnp.float32)).astype(jnp.bfloat16)
    return high, middle, low


def per_device(
    events, labels, w_in, w_out, gate_weight, tower_in, tower_bias, tower_out, tower_out_bias
):
    dp = lax.axis_size("dp")
    experts = lax.axis_size("expert")
    devices = dp * experts
    own, width = events.shape
    tasks = tower_in.shape[0]
    rows = devices * own

    gate_logits = jnp.einsum(
        "rd,tde->tre", events, gate_weight, preferred_element_type=jnp.float32
    )
    probs = jax.nn.softmax(gate_logits, axis=-1)

    block = experts * own
    every = lax.all_to_all(
        jnp.broadcast_to(events[None], (experts, own, width)), "expert", 0, 0, tiled=True
    ).reshape(block, width)
    every = lax.all_to_all(
        jnp.broadcast_to(every[None], (dp, block, width)), "dp", 0, 0, tiled=True
    ).reshape(rows, width)
    pre = jnp.dot(every, w_in[0], preferred_element_type=jnp.float32)
    hidden = gelu_tanh(pre).astype(jnp.bfloat16)
    part = jnp.dot(hidden, w_out[0], preferred_element_type=jnp.float32).astype(jnp.bfloat16)

    parts = lax.all_to_all(part.reshape(dp, block, width), "dp", 0, 0, tiled=True)
    outs = jnp.sum(parts.astype(jnp.float32), 0).astype(jnp.bfloat16)
    outs = lax.all_to_all(outs.reshape(experts, own, width), "expert", 0, 0, tiled=True)
    outs_wide = outs.astype(jnp.float32)
    mixed = jnp.sum(
        jnp.transpose(probs, (0, 2, 1))[..., None] * outs_wide[None], 1
    ).astype(jnp.bfloat16)
    tower_pre = (
        jnp.einsum("trd,tdk->trk", mixed, tower_in, preferred_element_type=jnp.float32)
        + tower_bias[:, None, :]
    )
    active, gelu_back = jax.vjp(gelu_tanh, tower_pre)
    logit = jnp.sum(active * tower_out[:, None, :], -1) + tower_out_bias[:, None]
    dlogit = jax.nn.sigmoid(logit) - labels.T.astype(jnp.float32)
    dtower = gelu_back(dlogit[..., None] * tower_out[:, None, :])[0]
    stacked = jnp.concatenate(pieces_of(dtower), 1)
    dmixed = jnp.einsum("trk,tdk->trd", stacked, tower_in, preferred_element_type=jnp.float32)
    dmixed = jnp.sum(dmixed.reshape(tasks, 3, own, width), 1).astype(jnp.bfloat16)
    dmixed_wide = dmixed.astype(jnp.float32)
    dprob = jnp.sum(dmixed_wide[:, None] * outs_wide[None], -1)
    probs_ter = jnp.transpose(probs, (0, 2, 1))
    dgate = probs_ter * (dprob - jnp.sum(probs_ter * dprob, 1, keepdims=True))
    dexpert = jnp.sum(probs_ter[..., None] * dmixed_wide[:, None], 0).astype(jnp.bfloat16)

    packed = jnp.transpose(jnp.concatenate(pieces_of(dgate), 0), (1, 2, 0))
    packed = jnp.pad(packed, ((0, 0), (0, 0), (0, 128 - 3 * tasks)))
    message = jnp.concatenate([dexpert, packed], -1)
    arrived = lax.all_to_all(message, "expert", 0, 0, tiled=True)
    arrived = arrived.reshape(block, width + 128)
    arrived = lax.all_to_all(
        jnp.broadcast_to(arrived[None], (dp, block, width + 128)), "dp", 0, 0, tiled=True
    ).reshape(rows, width + 128)
    all_grads = arrived[:, :width]
    gate_rows = arrived[:, width : width + 3 * tasks]

    dhidden = lax.dot_general(
        all_grads, w_out[0], (((1,), (1,)), ((), ())), preferred_element_type=jnp.float32
    )
    dpre = jax.vjp(gelu_tanh, pre)[1](dhidden)[0].astype(jnp.bfloat16)
    grad_second = lax.dot_general(
        hidden, all_grads, (((0,), (0,)), ((), ())), preferred_element_type=jnp.float32
    ).astype(jnp.bfloat16)
    grad_first = lax.dot_general(
        every, dpre, (((0,), (0,)), ((), ())), preferred_element_type=jnp.float32
    ).astype(jnp.bfloat16)
    grad_gate = lax.dot_general(
        gate_rows, every, (((0,), (0,)), ((), ())), preferred_element_type=jnp.float32
    )
    grad_gate = jnp.sum(grad_gate.reshape(3, tasks, width), 0)
    return (grad_first[None], grad_second[None], grad_gate[:, :, None])


def solution(mesh):
    placed = (
        P(BOTH, None),
        P(BOTH, None),
        P("expert", None, "dp"),
        P("expert", "dp", None),
        P(),
        P(),
        P(),
        P(),
        P(),
    )
    return jax.shard_map(
        per_device,
        mesh=mesh,
        in_specs=placed,
        out_specs=(P("expert", None, "dp"), P("expert", "dp", None), P(None, None, "expert")),
        check_vma=False,
    )
```

```python
import jax
import jax.numpy as jnp
from jax import lax
from jax.sharding import PartitionSpec as P

BOTH = ("dp", "expert")


def gelu_tanh(value):
    return jax.nn.gelu(value, approximate=True)


def pieces_of(value):
    high = value.astype(jnp.bfloat16)
    rest = value - high.astype(jnp.float32)
    middle = rest.astype(jnp.bfloat16)
    low = (rest - middle.astype(jnp.float32)).astype(jnp.bfloat16)
    return high, middle, low


def partners(value, axis):
    size = lax.axis_size(axis)
    got = [value[0]]
    for k in range(1, size):
        got.append(lax.ppermute(value[k], axis, [(i, i ^ k) for i in range(size)]))
    return got


def per_device(
    events, labels, w_in, w_out, gate_weight, tower_in, tower_bias, tower_out, tower_out_bias
):
    dp = lax.axis_size("dp")
    experts = lax.axis_size("expert")
    own, width = events.shape
    tasks = tower_in.shape[0]

    gate_logits = jnp.einsum(
        "rd,tde->tre", events, gate_weight, preferred_element_type=jnp.float32
    )
    probs = jax.nn.softmax(gate_logits, axis=-1)

    slots = jnp.arange(experts) ^ lax.axis_index("expert")
    probs = jnp.take(probs, slots, axis=2)

    every = jnp.concatenate(partners([events] * experts, "expert"), 0)
    every = jnp.concatenate(partners([every] * dp, "dp"), 0)
    pre = jnp.dot(every, w_in[0], preferred_element_type=jnp.float32)
    hidden = gelu_tanh(pre).astype(jnp.bfloat16)
    part = jnp.dot(hidden, w_out[0], preferred_element_type=jnp.float32).astype(jnp.bfloat16)

    parts = partners(part.reshape(dp, experts * own, width), "dp")
    outs = sum(piece.astype(jnp.float32) for piece in parts).astype(jnp.bfloat16)
    outs = jnp.stack(partners(outs.reshape(experts, own, width), "expert"), 0)
    outs_wide = outs.astype(jnp.float32)
    mixed = jnp.sum(
        jnp.transpose(probs, (0, 2, 1))[..., None] * outs_wide[None], 1
    ).astype(jnp.bfloat16)
    tower_pre = (
        jnp.einsum("trd,tdk->trk", mixed, tower_in, preferred_element_type=jnp.float32)
        + tower_bias[:, None, :]
    )
    active, gelu_back = jax.vjp(gelu_tanh, tower_pre)
    logit = jnp.sum(active * tower_out[:, None, :], -1) + tower_out_bias[:, None]
    dlogit = jax.nn.sigmoid(logit) - labels.T.astype(jnp.float32)
    dtower = gelu_back(dlogit[..., None] * tower_out[:, None, :])[0]
    stacked = jnp.concatenate(pieces_of(dtower), 1)
    dmixed = jnp.einsum("trk,tdk->trd", stacked, tower_in, preferred_element_type=jnp.float32)
    dmixed = jnp.sum(dmixed.reshape(tasks, 3, own, width), 1).astype(jnp.bfloat16)
    dmixed_wide = dmixed.astype(jnp.float32)
    dprob = jnp.sum(dmixed_wide[:, None] * outs_wide[None], -1)
    probs_ter = jnp.transpose(probs, (0, 2, 1))
    dgate = probs_ter * (dprob - jnp.sum(probs_ter * dprob, 1, keepdims=True))
    dexpert = jnp.sum(probs_ter[..., None] * dmixed_wide[:, None], 0).astype(jnp.bfloat16)

    packed = jnp.transpose(jnp.concatenate(pieces_of(dgate), 0), (1, 2, 0))
    packed = jnp.pad(packed, ((0, 0), (0, 0), (0, 128 - 3 * tasks)))
    message = jnp.concatenate([dexpert, packed], -1)
    arrived = jnp.concatenate(partners(message, "expert"), 0)
    arrived = jnp.concatenate(partners([arrived] * dp, "dp"), 0)
    all_grads = arrived[:, :width]
    gate_rows = arrived[:, width : width + 3 * tasks]

    dhidden = lax.dot_general(
        all_grads, w_out[0], (((1,), (1,)), ((), ())), preferred_element_type=jnp.float32
    )
    dpre = jax.vjp(gelu_tanh, pre)[1](dhidden)[0].astype(jnp.bfloat16)
    grad_second = lax.dot_general(
        hidden, all_grads, (((0,), (0,)), ((), ())), preferred_element_type=jnp.float32
    ).astype(jnp.bfloat16)
    grad_first = lax.dot_general(
        every, dpre, (((0,), (0,)), ((), ())), preferred_element_type=jnp.float32
    ).astype(jnp.bfloat16)
    grad_gate = lax.dot_general(
        gate_rows, every, (((0,), (0,)), ((), ())), preferred_element_type=jnp.float32
    )
    grad_gate = jnp.sum(grad_gate.reshape(3, tasks, width), 0)
    return (grad_first[None], grad_second[None], grad_gate[:, :, None])


def solution(mesh):
    placed = (
        P(BOTH, None),
        P(BOTH, None),
        P("expert", None, "dp"),
        P("expert", "dp", None),
        P(),
        P(),
        P(),
        P(),
        P(),
    )
    return jax.shard_map(
        per_device,
        mesh=mesh,
        in_specs=placed,
        out_specs=(P("expert", None, "dp"), P("expert", "dp", None), P(None, None, "expert")),
        check_vma=False,
    )
```

```python
import functools

import jax
import jax.numpy as jnp
from jax import lax
from jax.experimental import pallas as pl
from jax.experimental.pallas import tpu as pltpu
from jax.sharding import PartitionSpec as P

BOTH = ("dp", "expert")
LANES = 128
TILE = 256
GELU_C = 0.7978845608028654
GELU_A = 0.044715
VMEM_LIMIT = 40 * 1024 * 1024


def gelu_tanh(value):
    return jax.nn.gelu(value, approximate=True)


def gelu_slope(value):
    square = value * value
    bend = jnp.tanh(GELU_C * (value + GELU_A * value * square))
    inner = GELU_C * (1.0 + 3.0 * GELU_A * square)
    return 0.5 * (1.0 + bend) + 0.5 * value * (1.0 - bend * bend) * inner


def pieces_of(value):
    high = value.astype(jnp.bfloat16)
    rest = value - high.astype(jnp.float32)
    middle = rest.astype(jnp.bfloat16)
    low = (rest - middle.astype(jnp.float32)).astype(jnp.bfloat16)
    return high, middle, low


def dot(left, right, over):
    return lax.dot_general(
        left, right, ((over[:1], over[1:]), ((), ())), preferred_element_type=jnp.float32
    )


def steps(count, flat, body):
    if flat:
        for step in range(count):
            body(step)
    else:
        lax.fori_loop(0, count, lambda step, none: (body(step), none)[1], None)


def span(step, size):
    return pl.ds(pl.multiple_of(step * size, size), size)


def params():
    return pltpu.CompilerParams(vmem_limit_bytes=VMEM_LIMIT)


def cost(flops, moved):
    return pl.CostEstimate(flops=flops, bytes_accessed=moved, transcendentals=0)


def spread_kernel(row_ref, out_ref):
    for step in range(out_ref.shape[0]):
        out_ref[step] = row_ref[...]


def spread(value, devices):
    return pl.pallas_call(
        spread_kernel,
        out_shape=jax.ShapeDtypeStruct((devices, *value.shape), value.dtype),
        compiler_params=params(),
        name="spread",
    )(value)


def fetch_kernel(*refs):
    count = (len(refs) - 1) // 2
    sems = refs[-1]
    copies = [
        pltpu.make_async_copy(refs[at], refs[count + at], sems.at[at]) for at in range(count)
    ]
    for copy in copies:
        copy.start()
    for copy in copies:
        copy.wait()


def fetch(*arrays):
    moved = sum(array.size * array.dtype.itemsize for array in arrays)
    return pl.pallas_call(
        fetch_kernel,
        in_specs=[pl.BlockSpec(memory_space=pl.ANY)] * len(arrays),
        out_specs=[pl.BlockSpec(memory_space=pltpu.VMEM)] * len(arrays),
        out_shape=[pltpu.VMEM(array.shape, array.dtype) for array in arrays],
        scratch_shapes=[pltpu.SemaphoreType.DMA((len(arrays),))],
        compiler_params=params(),
        cost_estimate=cost(0, 2 * moved),
        name="fetch",
    )(*(pltpu.with_memory_space_constraint(array, pltpu.HBM) for array in arrays))


def forward_kernel(own, every_ref, first_ref, second_ref, part_ref, pre_ref, hidden_ref):
    rows = every_ref.shape[0]
    chunk = min(rows, 64)

    def body(step):
        here = span(step, chunk)
        pre = dot(every_ref[here, :], first_ref[...], (1, 0))
        hidden = gelu_tanh(pre).astype(jnp.bfloat16)
        part = dot(hidden, second_ref[...], (1, 0)).astype(jnp.bfloat16)
        for at in range(chunk // own):
            part_ref[step * (chunk // own) + at] = part[at * own : (at + 1) * own]
        pre_ref[here, :] = pre
        hidden_ref[here, :] = hidden

    steps(rows // chunk, rows == chunk, body)


def forward(every, first, second, own):
    rows, width = every.shape
    units = first.shape[1]
    return pl.pallas_call(
        functools.partial(forward_kernel, own),
        out_shape=[
            jax.ShapeDtypeStruct((rows // own, own, width), jnp.bfloat16),
            pltpu.VMEM((rows, units), jnp.float32),
            pltpu.VMEM((rows, units), jnp.bfloat16),
        ],
        compiler_params=params(),
        cost_estimate=cost(4 * rows * width * units, 4 * width * units),
        name="forward",
    )(every, first, second)


def backward_kernel(
    tasks,
    arrived_ref,
    every_ref,
    hidden_ref,
    pre_ref,
    second_ref,
    grad_first_ref,
    grad_second_ref,
    grad_gate_ref,
    dpre_ref,
    first_buf,
    second_buf,
    sems,
):
    rows, width = every_ref.shape
    units = hidden_ref.shape[1]
    flat = rows <= 64
    across, down = units // TILE, width // TILE

    def second_copy(step):
        here = span(step, TILE)
        return pltpu.make_async_copy(
            second_buf.at[here, :], grad_second_ref.at[here, :], sems.at[step]
        )

    def first_copy(step):
        here = span(step, TILE)
        return pltpu.make_async_copy(
            first_buf.at[here, :], grad_first_ref.at[here, :], sems.at[across + step]
        )

    def second_step(step):
        here = span(step, TILE)
        second_buf[here, :] = dot(
            hidden_ref[:, here], arrived_ref[:, :width], (0, 0)
        ).astype(jnp.bfloat16)
        second_copy(step).start()

    def dpre_step(step):
        here = span(step, TILE)
        dhidden = dot(arrived_ref[:, :width], second_ref[here, :], (1, 1))
        dpre_ref[:, here] = (gelu_slope(pre_ref[:, here]) * dhidden).astype(jnp.bfloat16)

    def first_step(step):
        here = span(step, TILE)
        first_buf[here, :] = dot(every_ref[:, here], dpre_ref[...], (0, 0)).astype(jnp.bfloat16)
        first_copy(step).start()

    steps(across, flat, second_step)
    steps(across, flat, dpre_step)
    steps(down, flat, first_step)
    gate = dot(arrived_ref[:, width:], every_ref[...], (0, 0))
    total = gate[:tasks] + gate[tasks : 2 * tasks] + gate[2 * tasks : 3 * tasks]
    for task in range(tasks):
        grad_gate_ref[task] = total[task : task + 1]
    steps(across, flat, lambda step: second_copy(step).wait())
    steps(down, flat, lambda step: first_copy(step).wait())


def backward(arrived, every, hidden, pre, second, tasks):
    rows, width = every.shape
    units = hidden.shape[1]
    anywhere = pl.BlockSpec(memory_space=pl.ANY)
    inside = pl.BlockSpec(memory_space=pltpu.VMEM)
    return pl.pallas_call(
        functools.partial(backward_kernel, tasks),
        out_shape=[
            jax.ShapeDtypeStruct((width, units), jnp.bfloat16),
            jax.ShapeDtypeStruct((units, width), jnp.bfloat16),
            jax.ShapeDtypeStruct((tasks, 1, width), jnp.float32),
        ],
        in_specs=[inside] * 5,
        out_specs=[anywhere, anywhere, inside],
        scratch_shapes=[
            pltpu.VMEM((rows, units), jnp.bfloat16),
            pltpu.VMEM((width, units), jnp.bfloat16),
            pltpu.VMEM((units, width), jnp.bfloat16),
            pltpu.SemaphoreType.DMA((units // TILE + width // TILE,)),
        ],
        compiler_params=params(),
        cost_estimate=cost(6 * rows * width * units, 6 * width * units),
        name="backward",
    )(arrived, every, hidden, pre, second)


def per_device(
    events, labels, w_in, w_out, gate_weight, tower_in, tower_bias, tower_out, tower_out_bias
):
    dp = lax.axis_size("dp")
    experts = lax.axis_size("expert")
    devices = dp * experts
    own, width = events.shape
    tasks = tower_in.shape[0]
    rows = devices * own

    gate_logits = jnp.einsum(
        "rd,tde->tre", events, gate_weight, preferred_element_type=jnp.float32
    )
    probs = jax.nn.softmax(gate_logits, axis=-1)

    every = lax.all_to_all(spread(events, devices), BOTH, 0, 0, tiled=True).reshape(rows, width)
    first, second, tower_in = fetch(w_in[0], w_out[0], tower_in)
    part, pre, hidden = forward(every, first, second, own)

    parts = lax.all_to_all(part, BOTH, 0, 0, tiled=True)
    parts = parts.reshape(dp, experts, own, width).astype(jnp.float32)
    outs = jnp.sum(parts, 0).astype(jnp.bfloat16)
    outs_wide = outs.astype(jnp.float32)
    mixed = jnp.sum(
        jnp.transpose(probs, (0, 2, 1))[..., None] * outs_wide[None], 1
    ).astype(jnp.bfloat16)
    tower_pre = (
        jnp.einsum("trd,tdk->trk", mixed, tower_in, preferred_element_type=jnp.float32)
        + tower_bias[:, None, :]
    )
    active, gelu_back = jax.vjp(gelu_tanh, tower_pre)
    logit = jnp.sum(active * tower_out[:, None, :], -1) + tower_out_bias[:, None]
    dlogit = jax.nn.sigmoid(logit) - labels.T.astype(jnp.float32)
    dtower = gelu_back(dlogit[..., None] * tower_out[:, None, :])[0]
    stacked = jnp.concatenate(pieces_of(dtower), 1)
    dmixed = jnp.einsum("trk,tdk->trd", stacked, tower_in, preferred_element_type=jnp.float32)
    dmixed = jnp.sum(dmixed.reshape(tasks, 3, own, width), 1).astype(jnp.bfloat16)
    dmixed_wide = dmixed.astype(jnp.float32)
    dprob = jnp.sum(dmixed_wide[:, None] * outs_wide[None], -1)
    probs_ter = jnp.transpose(probs, (0, 2, 1))
    dgate = probs_ter * (dprob - jnp.sum(probs_ter * dprob, 1, keepdims=True))
    dexpert = jnp.sum(probs_ter[..., None] * dmixed_wide[:, None], 0).astype(jnp.bfloat16)

    packed = jnp.transpose(jnp.concatenate(pieces_of(dgate), 0), (1, 2, 0))
    packed = jnp.pad(packed, ((0, 0), (0, 0), (0, LANES - 3 * tasks)))
    message = jnp.concatenate([dexpert, packed], -1)
    message = jnp.broadcast_to(message[None], (dp, experts, own, width + LANES))
    message = message.reshape(devices, own, width + LANES)
    arrived = lax.all_to_all(message, BOTH, 0, 0, tiled=True).reshape(rows, width + LANES)
    grad_first, grad_second, grad_gate = backward(arrived, every, hidden, pre, second, tasks)
    return (grad_first[None], grad_second[None], jnp.transpose(grad_gate, (0, 2, 1)))


def solution(mesh):
    placed = (
        P(BOTH, None),
        P(BOTH, None),
        P("expert", None, "dp"),
        P("expert", "dp", None),
        P(),
        P(),
        P(),
        P(),
        P(),
    )
    return jax.shard_map(
        per_device,
        mesh=mesh,
        in_specs=placed,
        out_specs=(P("expert", None, "dp"), P("expert", "dp", None), P(None, None, "expert")),
        check_vma=False,
    )
```

```python
import functools

import jax
import jax.numpy as jnp
from jax import lax
from jax.experimental import pallas as pl
from jax.experimental.pallas import tpu as pltpu
from jax.sharding import PartitionSpec as P

BOTH = ("dp", "expert")
LANES = 128
TILE = 256
GELU_C = 0.7978845608028654
GELU_A = 0.044715
VMEM_LIMIT = 40 * 1024 * 1024


def gelu_tanh(value):
    return jax.nn.gelu(value, approximate=True)


def gelu_slope(value):
    square = value * value
    bend = jnp.tanh(GELU_C * (value + GELU_A * value * square))
    inner = GELU_C * (1.0 + 3.0 * GELU_A * square)
    return 0.5 * (1.0 + bend) + 0.5 * value * (1.0 - bend * bend) * inner


def pieces_of(value):
    high = value.astype(jnp.bfloat16)
    rest = value - high.astype(jnp.float32)
    middle = rest.astype(jnp.bfloat16)
    low = (rest - middle.astype(jnp.float32)).astype(jnp.bfloat16)
    return high, middle, low


def dot(left, right, over):
    return lax.dot_general(
        left, right, ((over[:1], over[1:]), ((), ())), preferred_element_type=jnp.float32
    )


def steps(count, flat, body):
    if flat:
        for step in range(count):
            body(step)
    else:
        lax.fori_loop(0, count, lambda step, none: (body(step), none)[1], None)


def span(step, size):
    return pl.ds(pl.multiple_of(step * size, size), size)


def params():
    return pltpu.CompilerParams(vmem_limit_bytes=VMEM_LIMIT)


def cost(flops, moved):
    return pl.CostEstimate(flops=flops, bytes_accessed=moved, transcendentals=0)


def in_hbm(value):
    return pltpu.with_memory_space_constraint(value, pltpu.HBM)


def spread_kernel(row_ref, out_ref, sem):
    def body(step):
        pltpu.make_async_copy(row_ref, out_ref.at[step], sem).start()

    steps(out_ref.shape[0], True, body)
    pltpu.make_async_copy(out_ref, out_ref, sem).wait()


def spread(value, devices):
    return pl.pallas_call(
        spread_kernel,
        in_specs=[pl.BlockSpec(memory_space=pl.ANY)],
        out_specs=pl.BlockSpec(memory_space=pl.ANY),
        out_shape=pltpu.HBM((devices, *value.shape), value.dtype),
        scratch_shapes=[pltpu.SemaphoreType.DMA],
        compiler_params=params(),
        name="spread",
    )(in_hbm(value))


def fetch_kernel(*refs):
    count = (len(refs) - 1) // 2
    sems = refs[-1]
    copies = [
        pltpu.make_async_copy(refs[at], refs[count + at], sems.at[at]) for at in range(count)
    ]
    for copy in copies:
        copy.start()
    for copy in copies:
        copy.wait()


def fetch(*arrays):
    moved = sum(array.size * array.dtype.itemsize for array in arrays)
    return pl.pallas_call(
        fetch_kernel,
        in_specs=[pl.BlockSpec(memory_space=pl.ANY)] * len(arrays),
        out_specs=[pl.BlockSpec(memory_space=pltpu.VMEM)] * len(arrays),
        out_shape=[pltpu.VMEM(array.shape, array.dtype) for array in arrays],
        scratch_shapes=[pltpu.SemaphoreType.DMA((len(arrays),))],
        compiler_params=params(),
        cost_estimate=cost(0, 2 * moved),
        name="fetch",
    )(*(in_hbm(array) for array in arrays))


def streamed(source, target, sems):
    def block(step):
        here = span(step, TILE)
        return pltpu.make_async_copy(source.at[here, :], target.at[here, :], sems.at[step])

    return block


def forward_kernel(
    own, every_ref, first_ref, second_ref, part_ref, pre_ref, hidden_ref, second_buf, sems
):
    rows = every_ref.shape[0]
    chunk = min(rows, 64)
    blocks = second_ref.shape[0] // TILE
    block = streamed(second_ref, second_buf, sems)
    for at in range(blocks):
        block(at).start()

    def body(step):
        here = span(step, chunk)
        pre = dot(every_ref[here, :], first_ref[...], (1, 0))
        pre_ref[here, :] = pre
        hidden_ref[here, :] = gelu_tanh(pre).astype(jnp.bfloat16)

    steps(rows // chunk, rows == chunk, body)
    for at in range(blocks):
        block(at).wait()

    def finish(step):
        here = span(step, chunk)
        part = dot(hidden_ref[here, :], second_buf[...], (1, 0)).astype(jnp.bfloat16)
        for at in range(chunk // own):
            part_ref[step * (chunk // own) + at] = part[at * own : (at + 1) * own]

    steps(rows // chunk, rows == chunk, finish)


def forward(every, first, second, own):
    rows, width = every.shape
    units = first.shape[1]
    inside = pl.BlockSpec(memory_space=pltpu.VMEM)
    return pl.pallas_call(
        functools.partial(forward_kernel, own),
        out_shape=[
            jax.ShapeDtypeStruct((rows // own, own, width), jnp.bfloat16),
            pltpu.VMEM((rows, units), jnp.float32),
            pltpu.VMEM((rows, units), jnp.bfloat16),
        ],
        in_specs=[inside, inside, pl.BlockSpec(memory_space=pl.ANY)],
        out_specs=[inside] * 3,
        scratch_shapes=[
            pltpu.VMEM(second.shape, second.dtype),
            pltpu.SemaphoreType.DMA((units // TILE,)),
        ],
        compiler_params=params(),
        cost_estimate=cost(4 * rows * width * units, 4 * width * units),
        name="forward",
    )(every, first, in_hbm(second))


def middle_kernel(
    shape,
    parts_ref,
    probs_ref,
    tower_in_ref,
    bias_ref,
    weight_ref,
    shift_ref,
    target_ref,
    message_ref,
):
    dp, experts, own = shape
    tasks = tower_in_ref.shape[0]
    width = parts_ref.shape[1]
    slots = experts * own
    rows = tasks * own
    total = parts_ref[:slots, :].astype(jnp.float32)
    for at in range(1, dp):
        total = total + parts_ref[at * slots : (at + 1) * slots, :].astype(jnp.float32)
    outs = total.astype(jnp.bfloat16)
    probs = probs_ref[...]
    share = jnp.concatenate([piece.astype(jnp.float32) for piece in pieces_of(probs)], 0)
    share = share.astype(jnp.bfloat16)

    def fold(value):
        return value[:rows] + value[rows : 2 * rows] + value[2 * rows :]

    def only(value, task):
        at = lax.broadcasted_iota(jnp.int32, value.shape, 0)
        return jnp.where(lax.rem(at, rows) // own == task, value, 0.0).astype(jnp.bfloat16)

    mixed = fold(dot(share, outs, (1, 0))).astype(jnp.bfloat16).astype(jnp.float32)
    tower = bias_ref[...]
    for task in range(tasks):
        tower = tower + dot(only(mixed, task), tower_in_ref[task], (1, 0))
    weight = weight_ref[...]
    logit = jnp.sum(gelu_tanh(tower) * weight, -1, keepdims=True) + shift_ref[...]
    dlogit = jax.nn.sigmoid(logit) - target_ref[...]
    dtower = gelu_slope(tower) * (dlogit * weight)
    stack = jnp.concatenate([piece.astype(jnp.float32) for piece in pieces_of(dtower)], 0)
    wide = dot(only(stack, 0), tower_in_ref[0], (1, 1))
    for task in range(1, tasks):
        wide = wide + dot(only(stack, task), tower_in_ref[task], (1, 1))
    dmixed = fold(wide).astype(jnp.bfloat16)
    dprob = dot(dmixed, outs, (1, 1))
    dgate = probs * (dprob - jnp.sum(probs * dprob, -1, keepdims=True))
    twice = dmixed.astype(jnp.float32)
    twice = jnp.concatenate([twice, twice, twice], 0).astype(jnp.bfloat16)
    dexpert = dot(share, twice, (0, 0)).astype(jnp.bfloat16)
    lanes = jnp.concatenate([piece.astype(jnp.float32) for piece in pieces_of(dgate)], 0)
    unit = lax.broadcasted_iota(jnp.int32, (3 * rows, LANES), 0) == lax.broadcasted_iota(
        jnp.int32, (3 * rows, LANES), 1
    )
    lanes = dot(lanes.astype(jnp.bfloat16), unit.astype(jnp.bfloat16), (0, 0))
    lanes = lanes.astype(jnp.bfloat16)
    for expert in range(experts):
        here = slice(expert * own, (expert + 1) * own)
        for at in range(dp):
            message_ref[at * experts + expert, :, :width] = dexpert[here]
            message_ref[at * experts + expert, :, width:] = lanes[here]


def middle(shape, parts, probs, tower_in, bias, weight, shift, target):
    dp, experts, own = shape
    width = parts.shape[1]
    return pl.pallas_call(
        functools.partial(middle_kernel, shape),
        out_shape=jax.ShapeDtypeStruct((dp * experts, own, width + LANES), jnp.bfloat16),
        compiler_params=params(),
        cost_estimate=cost(4 * 8 * tower_in.size, 2 * tower_in.size),
        name="middle",
    )(parts, probs, tower_in, bias, weight, shift, target)


def backward_kernel(
    tasks,
    own,
    arrived_ref,
    every_ref,
    hidden_ref,
    pre_ref,
    second_ref,
    grad_first_ref,
    grad_second_ref,
    grad_gate_ref,
    dpre_ref,
    first_buf,
    second_buf,
    weight_buf,
    sems,
    weight_sems,
):
    rows, width = every_ref.shape
    units = hidden_ref.shape[1]
    flat = rows <= 64
    across, down = units // TILE, width // TILE
    block = streamed(second_ref, weight_buf, weight_sems)
    for at in range(across):
        block(at).start()

    def second_copy(step):
        here = span(step, TILE)
        return pltpu.make_async_copy(
            second_buf.at[here, :], grad_second_ref.at[here, :], sems.at[step]
        )

    def first_copy(step):
        here = span(step, TILE)
        return pltpu.make_async_copy(
            first_buf.at[here, :], grad_first_ref.at[here, :], sems.at[across + step]
        )

    def second_step(step):
        here = span(step, TILE)
        second_buf[here, :] = dot(
            hidden_ref[:, here], arrived_ref[:, :width], (0, 0)
        ).astype(jnp.bfloat16)
        second_copy(step).start()

    def dpre_step(step):
        here = span(step, TILE)
        block(step).wait()
        dhidden = dot(arrived_ref[:, :width], weight_buf[here, :], (1, 1))
        dpre_ref[:, here] = (gelu_slope(pre_ref[:, here]) * dhidden).astype(jnp.bfloat16)

    def first_step(step):
        here = span(step, TILE)
        first_buf[here, :] = dot(every_ref[:, here], dpre_ref[...], (0, 0)).astype(jnp.bfloat16)
        first_copy(step).start()

    steps(across, flat, second_step)
    steps(across, flat, dpre_step)
    steps(down, flat, first_step)
    gate = dot(arrived_ref[:, width:], every_ref[...], (0, 0))
    for task in range(tasks):
        lanes = [(at * tasks + task) * own + row for at in range(3) for row in range(own)]
        grad_gate_ref[task] = sum(gate[lane : lane + 1] for lane in lanes)
    steps(across, flat, lambda step: second_copy(step).wait())
    steps(down, flat, lambda step: first_copy(step).wait())


def backward(arrived, every, hidden, pre, second, tasks, own):
    rows, width = every.shape
    units = hidden.shape[1]
    anywhere = pl.BlockSpec(memory_space=pl.ANY)
    inside = pl.BlockSpec(memory_space=pltpu.VMEM)
    return pl.pallas_call(
        functools.partial(backward_kernel, tasks, own),
        out_shape=[
            jax.ShapeDtypeStruct((width, units), jnp.bfloat16),
            jax.ShapeDtypeStruct((units, width), jnp.bfloat16),
            jax.ShapeDtypeStruct((tasks, 1, width), jnp.float32),
        ],
        in_specs=[inside] * 4 + [anywhere],
        out_specs=[anywhere, anywhere, inside],
        scratch_shapes=[
            pltpu.VMEM((rows, units), jnp.bfloat16),
            pltpu.VMEM((width, units), jnp.bfloat16),
            pltpu.VMEM((units, width), jnp.bfloat16),
            pltpu.VMEM((units, width), jnp.bfloat16),
            pltpu.SemaphoreType.DMA((units // TILE + width // TILE,)),
            pltpu.SemaphoreType.DMA((units // TILE,)),
        ],
        compiler_params=params(),
        cost_estimate=cost(6 * rows * width * units, 6 * width * units),
        name="backward",
    )(arrived, every, hidden, pre, in_hbm(second))


def per_device(
    events, labels, w_in, w_out, gate_weight, tower_in, tower_bias, tower_out, tower_out_bias
):
    dp = lax.axis_size("dp")
    experts = lax.axis_size("expert")
    devices = dp * experts
    own, width = events.shape
    tasks = tower_in.shape[0]
    rows = devices * own

    gate_logits = jnp.einsum(
        "rd,tde->tre", events, gate_weight, preferred_element_type=jnp.float32
    )
    probs = jax.nn.softmax(gate_logits, axis=-1)
    probs = probs[..., None] * jnp.eye(own, dtype=jnp.float32)[None, :, None, :]
    probs = probs.reshape(tasks * own, experts * own)
    bias = jnp.repeat(tower_bias, own, 0)
    weight = jnp.repeat(tower_out, own, 0)
    shift = jnp.repeat(tower_out_bias, own)[:, None]
    target = labels.T.astype(jnp.float32).reshape(tasks * own, 1)

    every = lax.all_to_all(spread(events, devices), BOTH, 0, 0, tiled=True).reshape(rows, width)
    (first,) = fetch(w_in[0])
    part, pre, hidden = forward(every, first, w_out[0], own)

    parts = lax.all_to_all(part, BOTH, 0, 0, tiled=True).reshape(rows, width)
    (tower_here,) = fetch(tower_in)
    message = middle(
        (dp, experts, own), parts, probs, tower_here, bias, weight, shift, target
    )

    arrived = lax.all_to_all(message, BOTH, 0, 0, tiled=True).reshape(rows, width + LANES)
    grad_first, grad_second, grad_gate = backward(
        arrived, every, hidden, pre, w_out[0], tasks, own
    )
    return (grad_first[None], grad_second[None], jnp.transpose(grad_gate, (0, 2, 1)))


def solution(mesh):
    placed = (
        P(BOTH, None),
        P(BOTH, None),
        P("expert", None, "dp"),
        P("expert", "dp", None),
        P(),
        P(),
        P(),
        P(),
        P(),
    )
    return jax.shard_map(
        per_device,
        mesh=mesh,
        in_specs=placed,
        out_specs=(P("expert", None, "dp"), P("expert", "dp", None), P(None, None, "expert")),
        check_vma=False,
    )
```

```python
import functools

import jax
import jax.numpy as jnp
from jax import lax
from jax.experimental import pallas as pl
from jax.experimental.pallas import tpu as pltpu
from jax.sharding import PartitionSpec as P

BOTH = ("dp", "expert")
LANES = 128
TILE = 256
GELU_C = 0.7978845608028654
GELU_A = 0.044715
VMEM_LIMIT = 40 * 1024 * 1024


def gelu_tanh(value):
    return jax.nn.gelu(value, approximate=True)


def gelu_slope(value):
    square = value * value
    bend = jnp.tanh(GELU_C * (value + GELU_A * value * square))
    inner = GELU_C * (1.0 + 3.0 * GELU_A * square)
    return 0.5 * (1.0 + bend) + 0.5 * value * (1.0 - bend * bend) * inner


def pieces_of(value):
    high = value.astype(jnp.bfloat16)
    rest = value - high.astype(jnp.float32)
    middle = rest.astype(jnp.bfloat16)
    low = (rest - middle.astype(jnp.float32)).astype(jnp.bfloat16)
    return high, middle, low


def dot(left, right, over):
    return lax.dot_general(
        left, right, ((over[:1], over[1:]), ((), ())), preferred_element_type=jnp.float32
    )


def steps(count, flat, body):
    if flat:
        for step in range(count):
            body(step)
    else:
        lax.fori_loop(0, count, lambda step, none: (body(step), none)[1], None)


def span(step, size):
    return pl.ds(pl.multiple_of(step * size, size), size)


def params():
    return pltpu.CompilerParams(vmem_limit_bytes=VMEM_LIMIT)


def cost(flops, moved):
    return pl.CostEstimate(flops=flops, bytes_accessed=moved, transcendentals=0)


def in_hbm(value):
    return pltpu.with_memory_space_constraint(value, pltpu.HBM)


def spread_kernel(row_ref, out_ref):
    for step in range(out_ref.shape[0]):
        out_ref[step] = row_ref[...]


def spread(value, devices):
    return pl.pallas_call(
        spread_kernel,
        out_shape=jax.ShapeDtypeStruct((devices, *value.shape), value.dtype),
        compiler_params=params(),
        name="spread",
    )(value)


def fetch_kernel(count, cuts, *refs):
    sources, targets, sems = refs[:count], refs[-1 - count : -1], refs[-1]
    copies = []
    for at in range(count):
        size = targets[at].shape[0] // cuts
        for cut in range(cuts):
            here = pl.ds(cut * size, size)
            copies.append(
                pltpu.make_async_copy(
                    sources[at].at[here], targets[at].at[here], sems.at[at, cut]
                )
            )
    for copy in copies:
        copy.start()
    for copy in copies:
        copy.wait()


def fetch(*arrays, sizes=None, after=(), cuts=4):
    sizes = sizes or [array.shape[0] for array in arrays]
    shapes = [(size, *array.shape[1:]) for size, array in zip(sizes, arrays)]
    moved = sum(array.size * array.dtype.itemsize for array in arrays)
    return pl.pallas_call(
        functools.partial(fetch_kernel, len(arrays), cuts),
        in_specs=[pl.BlockSpec(memory_space=pl.ANY)] * (len(arrays) + len(after)),
        out_specs=[pl.BlockSpec(memory_space=pltpu.VMEM)] * len(arrays),
        out_shape=[pltpu.VMEM(shape, array.dtype) for shape, array in zip(shapes, arrays)],
        scratch_shapes=[pltpu.SemaphoreType.DMA((len(arrays), cuts))],
        compiler_params=params(),
        cost_estimate=cost(0, 2 * moved),
        name="fetch",
    )(*(in_hbm(array) for array in arrays), *after)


def streamed(source, target, sems):
    def block(step):
        here = span(step, TILE)
        return pltpu.make_async_copy(source.at[here, :], target.at[here, :], sems.at[step])

    return block


def forward_kernel(
    own, every_ref, first_ref, upper_ref, second_ref, part_ref, pre_ref, hidden_ref, lower_buf, sems
):
    rows = every_ref.shape[0]
    chunk = min(rows, 64)
    half = upper_ref.shape[0]
    block = streamed(second_ref.at[pl.ds(half, half), :], lower_buf, sems)
    for at in range(half // TILE):
        block(at).start()

    def begin(step):
        here = span(step, chunk)
        pre = dot(every_ref[here, :], first_ref[...], (1, 0))
        pre_ref[here, :] = pre
        hidden_ref[here, :] = gelu_tanh(pre).astype(jnp.bfloat16)

    def finish(step):
        here = span(step, chunk)
        part = dot(hidden_ref[here, :half], upper_ref[...], (1, 0))
        if rows == chunk:
            arrive()
        part = part + dot(hidden_ref[here, half:], lower_buf[...], (1, 0))
        part = part.astype(jnp.bfloat16)
        for at in range(chunk // own):
            part_ref[step * (chunk // own) + at] = part[at * own : (at + 1) * own]

    def arrive():
        for at in range(half // TILE):
            block(at).wait()

    steps(rows // chunk, rows == chunk, begin)
    if rows != chunk:
        arrive()
    steps(rows // chunk, rows == chunk, finish)


def forward(every, first, upper, second, own):
    rows, width = every.shape
    units = first.shape[1]
    inside = pl.BlockSpec(memory_space=pltpu.VMEM)
    return pl.pallas_call(
        functools.partial(forward_kernel, own),
        out_shape=[
            jax.ShapeDtypeStruct((rows // own, own, width), jnp.bfloat16),
            pltpu.VMEM((rows, units), jnp.float32),
            pltpu.VMEM((rows, units), jnp.bfloat16),
        ],
        in_specs=[inside] * 3 + [pl.BlockSpec(memory_space=pl.ANY)],
        out_specs=[inside] * 3,
        scratch_shapes=[
            pltpu.VMEM(upper.shape, upper.dtype),
            pltpu.SemaphoreType.DMA((upper.shape[0] // TILE,)),
        ],
        compiler_params=params(),
        cost_estimate=cost(4 * rows * width * units, 4 * width * units),
        name="forward",
    )(every, first, upper, in_hbm(second))


def middle_kernel(
    shape,
    parts_ref,
    probs_ref,
    tower_in_ref,
    bias_ref,
    weight_ref,
    shift_ref,
    target_ref,
    message_ref,
):
    dp, experts, own = shape
    tasks = tower_in_ref.shape[0]
    width = parts_ref.shape[1]
    slots = experts * own
    rows = tasks * own
    total = parts_ref[:slots, :].astype(jnp.float32)
    for at in range(1, dp):
        total = total + parts_ref[at * slots : (at + 1) * slots, :].astype(jnp.float32)
    outs = total.astype(jnp.bfloat16)
    probs = probs_ref[...]
    share = jnp.concatenate([piece.astype(jnp.float32) for piece in pieces_of(probs)], 0)
    share = share.astype(jnp.bfloat16)

    def fold(value):
        return value[:rows] + value[rows : 2 * rows] + value[2 * rows :]

    def only(value, task):
        at = lax.broadcasted_iota(jnp.int32, value.shape, 0)
        return jnp.where(lax.rem(at, rows) // own == task, value, 0.0).astype(jnp.bfloat16)

    mixed = fold(dot(share, outs, (1, 0))).astype(jnp.bfloat16).astype(jnp.float32)
    tower = bias_ref[...]
    for task in range(tasks):
        tower = tower + dot(only(mixed, task), tower_in_ref[task], (1, 0))
    weight = weight_ref[...]
    logit = jnp.sum(gelu_tanh(tower) * weight, -1, keepdims=True) + shift_ref[...]
    dlogit = jax.nn.sigmoid(logit) - target_ref[...]
    dtower = gelu_slope(tower) * (dlogit * weight)
    stack = jnp.concatenate([piece.astype(jnp.float32) for piece in pieces_of(dtower)], 0)
    wide = dot(only(stack, 0), tower_in_ref[0], (1, 1))
    for task in range(1, tasks):
        wide = wide + dot(only(stack, task), tower_in_ref[task], (1, 1))
    dmixed = fold(wide).astype(jnp.bfloat16)
    dprob = dot(dmixed, outs, (1, 1))
    dgate = probs * (dprob - jnp.sum(probs * dprob, -1, keepdims=True))
    twice = dmixed.astype(jnp.float32)
    twice = jnp.concatenate([twice, twice, twice], 0).astype(jnp.bfloat16)
    dexpert = dot(share, twice, (0, 0)).astype(jnp.bfloat16)
    lanes = jnp.concatenate([piece.astype(jnp.float32) for piece in pieces_of(dgate)], 0)
    unit = lax.broadcasted_iota(jnp.int32, (3 * rows, LANES), 0) == lax.broadcasted_iota(
        jnp.int32, (3 * rows, LANES), 1
    )
    lanes = dot(lanes.astype(jnp.bfloat16), unit.astype(jnp.bfloat16), (0, 0))
    lanes = lanes.astype(jnp.bfloat16)
    for expert in range(experts):
        here = slice(expert * own, (expert + 1) * own)
        for at in range(dp):
            message_ref[at * experts + expert, :, :width] = dexpert[here]
            message_ref[at * experts + expert, :, width:] = lanes[here]


def middle(shape, parts, probs, tower_in, bias, weight, shift, target):
    dp, experts, own = shape
    width = parts.shape[1]
    return pl.pallas_call(
        functools.partial(middle_kernel, shape),
        out_shape=jax.ShapeDtypeStruct((dp * experts, own, width + LANES), jnp.bfloat16),
        compiler_params=params(),
        cost_estimate=cost(4 * 8 * tower_in.size, 2 * tower_in.size),
        name="middle",
    )(parts, probs, tower_in, bias, weight, shift, target)


def backward_kernel(
    tasks,
    own,
    arrived_ref,
    every_ref,
    hidden_ref,
    pre_ref,
    second_ref,
    grad_first_ref,
    grad_second_ref,
    grad_gate_ref,
    dpre_ref,
    first_buf,
    second_buf,
    sems,
):
    rows, width = every_ref.shape
    units = hidden_ref.shape[1]
    flat = rows <= 64
    across, down = units // TILE, width // TILE

    def second_copy(step):
        here = span(step, TILE)
        return pltpu.make_async_copy(
            second_buf.at[here, :], grad_second_ref.at[here, :], sems.at[step]
        )

    def first_copy(step):
        here = span(step, TILE)
        return pltpu.make_async_copy(
            first_buf.at[here, :], grad_first_ref.at[here, :], sems.at[across + step]
        )

    def second_step(step):
        here = span(step, TILE)
        second_buf[here, :] = dot(
            hidden_ref[:, here], arrived_ref[:, :width], (0, 0)
        ).astype(jnp.bfloat16)
        second_copy(step).start()

    def dpre_step(step):
        here = span(step, TILE)
        dhidden = dot(arrived_ref[:, :width], second_ref[here, :], (1, 1))
        dpre_ref[:, here] = (gelu_slope(pre_ref[:, here]) * dhidden).astype(jnp.bfloat16)

    def first_step(step):
        here = span(step, TILE)
        first_buf[here, :] = dot(every_ref[:, here], dpre_ref[...], (0, 0)).astype(jnp.bfloat16)
        first_copy(step).start()

    steps(across, flat, second_step)
    steps(across, flat, dpre_step)
    steps(down, flat, first_step)
    gate = dot(arrived_ref[:, width:], every_ref[...], (0, 0))
    for task in range(tasks):
        lanes = [(at * tasks + task) * own + row for at in range(3) for row in range(own)]
        grad_gate_ref[task] = sum(gate[lane : lane + 1] for lane in lanes)
    steps(across, flat, lambda step: second_copy(step).wait())
    steps(down, flat, lambda step: first_copy(step).wait())


def backward(arrived, every, hidden, pre, second, tasks, own):
    rows, width = every.shape
    units = hidden.shape[1]
    anywhere = pl.BlockSpec(memory_space=pl.ANY)
    inside = pl.BlockSpec(memory_space=pltpu.VMEM)
    return pl.pallas_call(
        functools.partial(backward_kernel, tasks, own),
        out_shape=[
            jax.ShapeDtypeStruct((width, units), jnp.bfloat16),
            jax.ShapeDtypeStruct((units, width), jnp.bfloat16),
            jax.ShapeDtypeStruct((tasks, 1, width), jnp.float32),
        ],
        in_specs=[inside] * 5,
        out_specs=[anywhere, anywhere, inside],
        scratch_shapes=[
            pltpu.VMEM((rows, units), jnp.bfloat16),
            pltpu.VMEM((width, units), jnp.bfloat16),
            pltpu.VMEM((units, width), jnp.bfloat16),
            pltpu.SemaphoreType.DMA((units // TILE + width // TILE,)),
        ],
        compiler_params=params(),
        cost_estimate=cost(6 * rows * width * units, 6 * width * units),
        name="backward",
    )(arrived, every, hidden, pre, second)


def per_device(
    events, labels, w_in, w_out, gate_weight, tower_in, tower_bias, tower_out, tower_out_bias
):
    dp = lax.axis_size("dp")
    experts = lax.axis_size("expert")
    devices = dp * experts
    own, width = events.shape
    tasks = tower_in.shape[0]
    rows = devices * own

    gate_logits = jnp.einsum(
        "rd,tde->tre", events, gate_weight, preferred_element_type=jnp.float32
    )
    probs = jax.nn.softmax(gate_logits, axis=-1)
    probs = probs[..., None] * jnp.eye(own, dtype=jnp.float32)[None, :, None, :]
    probs = probs.reshape(tasks * own, experts * own)
    bias = jnp.repeat(tower_bias, own, 0)
    weight = jnp.repeat(tower_out, own, 0)
    shift = jnp.repeat(tower_out_bias, own)[:, None]
    target = labels.T.astype(jnp.float32).reshape(tasks * own, 1)

    every = lax.all_to_all(spread(events, devices), BOTH, 0, 0, tiled=True).reshape(rows, width)
    first, upper = fetch(w_in[0], w_out[0], sizes=(w_in.shape[1], w_out.shape[1] // 2))
    part, pre, hidden = forward(every, first, upper, w_out[0], own)

    parts = lax.all_to_all(part, BOTH, 0, 0, tiled=True).reshape(rows, width)
    (tower_here,) = fetch(tower_in, after=(part,))
    message = middle(
        (dp, experts, own), parts, probs, tower_here, bias, weight, shift, target
    )

    (second,) = fetch(w_out[0], after=(message,))
    arrived = lax.all_to_all(message, BOTH, 0, 0, tiled=True).reshape(rows, width + LANES)
    grad_first, grad_second, grad_gate = backward(
        arrived, every, hidden, pre, second, tasks, own
    )
    return (grad_first[None], grad_second[None], jnp.transpose(grad_gate, (0, 2, 1)))


def solution(mesh):
    placed = (
        P(BOTH, None),
        P(BOTH, None),
        P("expert", None, "dp"),
        P("expert", "dp", None),
        P(),
        P(),
        P(),
        P(),
        P(),
    )
    return jax.shard_map(
        per_device,
        mesh=mesh,
        in_specs=placed,
        out_specs=(P("expert", None, "dp"), P("expert", "dp", None), P(None, None, "expert")),
        check_vma=False,
    )
```

```python
import functools

import jax
import jax.numpy as jnp
from jax import lax
from jax.experimental import pallas as pl
from jax.experimental.pallas import tpu as pltpu
from jax.sharding import PartitionSpec as P

BOTH = ("dp", "expert")
LANES = 128
TILE = 256
GELU_C = 0.7978845608028654
GELU_A = 0.044715
AHEAD_FLOPS = 1 << 34
VMEM_LIMIT = 32 * 1024 * 1024


def gelu_tanh(value):
    return jax.nn.gelu(value, approximate=True)


def gelu_slope(value):
    square = value * value
    bend = jnp.tanh(GELU_C * (value + GELU_A * value * square))
    inner = GELU_C * (1.0 + 3.0 * GELU_A * square)
    return 0.5 * (1.0 + bend) + 0.5 * value * (1.0 - bend * bend) * inner


def pieces_of(value):
    high = value.astype(jnp.bfloat16)
    rest = value - high.astype(jnp.float32)
    middle = rest.astype(jnp.bfloat16)
    low = (rest - middle.astype(jnp.float32)).astype(jnp.bfloat16)
    return high, middle, low


def dot(left, right, over):
    return lax.dot_general(
        left, right, ((over[:1], over[1:]), ((), ())), preferred_element_type=jnp.float32
    )


def steps(count, flat, body):
    if flat:
        for step in range(count):
            body(step)
    else:
        lax.fori_loop(0, count, lambda step, none: (body(step), none)[1], None)


def span(step, size):
    return pl.ds(pl.multiple_of(step * size, size), size)


def params():
    return pltpu.CompilerParams(vmem_limit_bytes=VMEM_LIMIT)


def cost(flops, moved):
    return pl.CostEstimate(flops=flops, bytes_accessed=moved, transcendentals=0)


def in_vmem(value):
    return pltpu.with_memory_space_constraint(value, pltpu.VMEM)


def spread_kernel(row_ref, out_ref):
    for step in range(out_ref.shape[0]):
        out_ref[step] = row_ref[...]


def spread(value, devices):
    return pl.pallas_call(
        spread_kernel,
        out_shape=pltpu.VMEM((devices, *value.shape), value.dtype),
        compiler_params=params(),
        cost_estimate=cost(AHEAD_FLOPS, 0),
        name="spread",
    )(value)


def unpack(message_ref, rows_ref):
    own = message_ref.shape[1]
    for at in range(message_ref.shape[0]):
        rows_ref[at * own : (at + 1) * own, :] = message_ref[at].astype(jnp.float32)


def forward_kernel(
    got_ref, first_ref, second_ref, part_ref, every_ref, pre_ref, hidden_ref, wide_ref
):
    own = got_ref.shape[1]
    rows = every_ref.shape[0]
    chunk = min(rows, 64)
    unpack(got_ref, wide_ref)

    def body(step):
        here = span(step, chunk)
        every = wide_ref[here, :].astype(jnp.bfloat16)
        every_ref[here, :] = every
        pre = dot(every, first_ref[...], (1, 0))
        hidden = gelu_tanh(pre).astype(jnp.bfloat16)
        part = dot(hidden, second_ref[...], (1, 0)).astype(jnp.bfloat16)
        for at in range(chunk // own):
            part_ref[step * (chunk // own) + at] = part[at * own : (at + 1) * own]
        pre_ref[here, :] = pre
        hidden_ref[here, :] = hidden

    steps(rows // chunk, rows == chunk, body)


def forward(got, first, second):
    devices, own, width = got.shape
    rows = devices * own
    units = first.shape[1]
    return pl.pallas_call(
        forward_kernel,
        out_shape=[
            pltpu.VMEM(got.shape, jnp.bfloat16),
            pltpu.VMEM((rows, width), jnp.bfloat16),
            pltpu.VMEM((rows, units), jnp.float32),
            pltpu.VMEM((rows, units), jnp.bfloat16),
        ],
        scratch_shapes=[pltpu.VMEM((rows, width), jnp.float32)],
        compiler_params=params(),
        cost_estimate=cost(4 * rows * width * units, 4 * width * units),
        name="forward",
    )(got, in_vmem(first), in_vmem(second))


def middle_kernel(
    dp,
    parts_ref,
    events_ref,
    labels_ref,
    gate_ref,
    tower_in_ref,
    bias_ref,
    weight_ref,
    shift_ref,
    message_ref,
    outs_ref,
):
    devices, own, width = parts_ref.shape
    experts = devices // dp
    tasks = tower_in_ref.shape[0]
    slots = experts * own
    rows = tasks * own
    float32, bfloat16 = jnp.float32, jnp.bfloat16

    def iota(shape, axis):
        return lax.broadcasted_iota(jnp.int32, shape, axis)

    def spread_rows(value_of, wide, of_task):
        at = iota((rows, wide), 0)
        at = at // own if of_task else lax.rem(at, own)
        result = jnp.zeros((rows, wide), float32)
        for key in range(tasks if of_task else own):
            result = jnp.where(at == key, value_of(key), result)
        return result

    def split(value):
        return jnp.concatenate([piece.astype(float32) for piece in pieces_of(value)], 0)

    def fold(value):
        return value[:rows] + value[rows : 2 * rows] + value[2 * rows :]

    def only(value, task):
        at = lax.rem(iota(value.shape, 0), rows) // own
        return jnp.where(at == task, value, 0.0).astype(bfloat16)

    events = events_ref[...].astype(float32)
    events = spread_rows(lambda row: events[row : row + 1], width, False).astype(bfloat16)
    gates = spread_rows(lambda task: dot(events, gate_ref[task], (1, 1)), experts, True)
    gates = jnp.exp(gates - jnp.max(gates, -1, keepdims=True))
    gates = gates / jnp.sum(gates, -1, keepdims=True)
    place = (iota((experts, slots), 0) == iota((experts, slots), 1) // own).astype(bfloat16)
    same = lax.rem(iota((3 * rows, slots), 0), own) == lax.rem(iota((3 * rows, slots), 1), own)
    share = jnp.where(same, dot(split(gates).astype(bfloat16), place, (1, 0)), 0.0)
    probs = fold(share)
    share = share.astype(bfloat16)

    for expert in range(experts):
        total = parts_ref[expert].astype(float32)
        for at in range(1, dp):
            total = total + parts_ref[at * experts + expert].astype(float32)
        outs_ref[expert * own : (expert + 1) * own, :] = total
    outs = outs_ref[...].astype(bfloat16)

    mixed = fold(dot(share, outs, (1, 0))).astype(bfloat16).astype(float32)
    tower = spread_rows(lambda task: bias_ref[task : task + 1, :], bias_ref.shape[1], True)
    weight = spread_rows(lambda task: weight_ref[task : task + 1, :], bias_ref.shape[1], True)
    shift = spread_rows(lambda task: shift_ref[:, task : task + 1], 1, True)
    labels = labels_ref[...].astype(float32)
    labels = spread_rows(lambda row: labels[row : row + 1], tasks, False)
    pick = iota((rows, tasks), 0) // own == iota((rows, tasks), 1)
    target = jnp.sum(jnp.where(pick, labels, 0.0), -1, keepdims=True)
    for task in range(tasks):
        tower = tower + dot(only(mixed, task), tower_in_ref[task], (1, 0))
    logit = jnp.sum(gelu_tanh(tower) * weight, -1, keepdims=True) + shift
    dlogit = jax.nn.sigmoid(logit) - target
    stack = split(gelu_slope(tower) * (dlogit * weight))
    wide = dot(only(stack, 0), tower_in_ref[0], (1, 1))
    for task in range(1, tasks):
        wide = wide + dot(only(stack, task), tower_in_ref[task], (1, 1))
    dmixed = fold(wide).astype(bfloat16)
    dprob = dot(dmixed, outs, (1, 1))
    dgate = probs * (dprob - jnp.sum(probs * dprob, -1, keepdims=True))
    thrice = dmixed.astype(float32)
    thrice = jnp.concatenate([thrice, thrice, thrice], 0).astype(bfloat16)
    dexpert = dot(share, thrice, (0, 0)).astype(bfloat16)

    unit = (iota((3 * rows, LANES), 0) == iota((3 * rows, LANES), 1)).astype(bfloat16)
    lanes = dot(split(dgate).astype(bfloat16), unit, (0, 0)).astype(bfloat16)
    for expert in range(experts):
        here = slice(expert * own, (expert + 1) * own)
        for at in range(dp):
            message_ref[at * experts + expert, :, :width] = dexpert[here]
            message_ref[at * experts + expert, :, width:] = lanes[here]


def middle(dp, parts, events, labels, gate, tower_in, bias, weight, shift):
    devices, own, width = parts.shape
    return pl.pallas_call(
        functools.partial(middle_kernel, dp),
        out_shape=pltpu.VMEM((devices, own, width + LANES), jnp.bfloat16),
        scratch_shapes=[pltpu.VMEM((devices // dp * own, width), jnp.float32)],
        compiler_params=params(),
        cost_estimate=cost(4 * 8 * tower_in.size, 2 * tower_in.size),
        name="middle",
    )(parts, events, labels, gate, in_vmem(tower_in), bias, weight, shift)


def backward_kernel(
    tasks,
    got_ref,
    every_ref,
    hidden_ref,
    pre_ref,
    second_ref,
    grad_first_ref,
    grad_second_ref,
    grad_gate_ref,
    dpre_ref,
    first_buf,
    second_buf,
    arrived_ref,
    wide_ref,
    sems,
):
    rows, width = every_ref.shape
    own = got_ref.shape[1]
    units = hidden_ref.shape[1]
    flat = rows <= 64
    across, down = units // TILE, width // TILE

    def second_copy(step):
        here = span(step, TILE)
        return pltpu.make_async_copy(
            second_buf.at[here, :], grad_second_ref.at[here, :], sems.at[step]
        )

    def first_copy(step):
        here = span(step, TILE)
        return pltpu.make_async_copy(
            first_buf.at[here, :], grad_first_ref.at[here, :], sems.at[across + step]
        )

    def second_step(step):
        here = span(step, TILE)
        second_buf[here, :] = dot(
            hidden_ref[:, here], arrived_ref[:, :width], (0, 0)
        ).astype(jnp.bfloat16)
        second_copy(step).start()

    def dpre_step(step):
        here = span(step, TILE)
        dhidden = dot(arrived_ref[:, :width], second_ref[here, :], (1, 1))
        dpre_ref[:, here] = (gelu_slope(pre_ref[:, here]) * dhidden).astype(jnp.bfloat16)

    def first_step(step):
        here = span(step, TILE)
        first_buf[here, :] = dot(every_ref[:, here], dpre_ref[...], (0, 0)).astype(jnp.bfloat16)
        first_copy(step).start()

    unpack(got_ref, wide_ref)
    arrived_ref[...] = wide_ref[...].astype(jnp.bfloat16)
    steps(across, flat, second_step)
    steps(across, flat, dpre_step)
    steps(down, flat, first_step)
    gate = dot(arrived_ref[:, width:], every_ref[...], (0, 0))
    for task in range(tasks):
        lanes = [(at * tasks + task) * own + row for at in range(3) for row in range(own)]
        grad_gate_ref[task] = sum(gate[lane : lane + 1] for lane in lanes)
    steps(across, flat, lambda step: second_copy(step).wait())
    steps(down, flat, lambda step: first_copy(step).wait())


def backward(got, every, hidden, pre, second, tasks):
    rows, width = every.shape
    units = hidden.shape[1]
    anywhere = pl.BlockSpec(memory_space=pl.ANY)
    inside = pl.BlockSpec(memory_space=pltpu.VMEM)
    return pl.pallas_call(
        functools.partial(backward_kernel, tasks),
        out_shape=[
            jax.ShapeDtypeStruct((width, units), jnp.bfloat16),
            jax.ShapeDtypeStruct((units, width), jnp.bfloat16),
            jax.ShapeDtypeStruct((tasks, 1, width), jnp.float32),
        ],
        in_specs=[inside] * 5,
        out_specs=[anywhere, anywhere, inside],
        scratch_shapes=[
            pltpu.VMEM((rows, units), jnp.bfloat16),
            pltpu.VMEM((width, units), jnp.bfloat16),
            pltpu.VMEM((units, width), jnp.bfloat16),
            pltpu.VMEM((rows, width + LANES), jnp.bfloat16),
            pltpu.VMEM((rows, width + LANES), jnp.float32),
            pltpu.SemaphoreType.DMA((units // TILE + width // TILE,)),
        ],
        compiler_params=params(),
        cost_estimate=cost(6 * rows * width * units, 6 * width * units),
        name="backward",
    )(got, every, hidden, pre, in_vmem(second))


def per_device(
    events, labels, w_in, w_out, gate_weight, tower_in, tower_bias, tower_out, tower_out_bias
):
    dp = lax.axis_size("dp")
    devices = dp * lax.axis_size("expert")
    tasks = tower_in.shape[0]
    gate = jnp.transpose(gate_weight, (0, 2, 1))

    got = lax.all_to_all(spread(events, devices), BOTH, 0, 0, tiled=True)
    part, every, pre, hidden = forward(got, w_in[0], w_out[0])

    parts = lax.all_to_all(part, BOTH, 0, 0, tiled=True)
    message = middle(
        dp, parts, events, labels, gate, tower_in, tower_bias, tower_out, tower_out_bias[None]
    )

    got = lax.all_to_all(message, BOTH, 0, 0, tiled=True)
    grad_first, grad_second, grad_gate = backward(got, every, hidden, pre, w_out[0], tasks)
    return (grad_first[None], grad_second[None], jnp.transpose(grad_gate, (0, 2, 1)))


def solution(mesh):
    placed = (
        P(BOTH, None),
        P(BOTH, None),
        P("expert", None, "dp"),
        P("expert", "dp", None),
        P(),
        P(),
        P(),
        P(),
        P(),
    )
    return jax.shard_map(
        per_device,
        mesh=mesh,
        in_specs=placed,
        out_specs=(P("expert", None, "dp"), P("expert", "dp", None), P(None, None, "expert")),
        check_vma=False,
    )
```

```python
import functools

import jax
import jax.numpy as jnp
from jax import lax
from jax.experimental import pallas as pl
from jax.experimental.pallas import tpu as pltpu
from jax.sharding import PartitionSpec as P

BOTH = ("dp", "expert")
LANES = 128
TILE = 256
GELU_C = 0.7978845608028654
GELU_A = 0.044715
AHEAD_FLOPS = 1 << 34
VMEM_LIMIT = 32 * 1024 * 1024


def gelu_pair(value):
    square = value * value
    bend = jnp.tanh(GELU_C * (value + GELU_A * value * square))
    inner = GELU_C * (1.0 + 3.0 * GELU_A * square)
    half = 0.5 * (1.0 + bend)
    return value * half, half + 0.5 * value * (1.0 - bend * bend) * inner


def pieces_of(value):
    high = value.astype(jnp.bfloat16)
    rest = value - high.astype(jnp.float32)
    middle = rest.astype(jnp.bfloat16)
    low = (rest - middle.astype(jnp.float32)).astype(jnp.bfloat16)
    return high, middle, low


def dot(left, right, over):
    return lax.dot_general(
        left, right, ((over[:1], over[1:]), ((), ())), preferred_element_type=jnp.float32
    )


def steps(count, flat, body):
    if flat:
        for step in range(count):
            body(step)
    else:
        lax.fori_loop(0, count, lambda step, none: (body(step), none)[1], None)


def span(step, size):
    return pl.ds(pl.multiple_of(step * size, size), size)


def params():
    return pltpu.CompilerParams(vmem_limit_bytes=VMEM_LIMIT)


def cost(flops, moved):
    return pl.CostEstimate(flops=flops, bytes_accessed=moved, transcendentals=0)


def in_vmem(value):
    return pltpu.with_memory_space_constraint(value, pltpu.VMEM)


def spread_kernel(row_ref, out_ref):
    for step in range(out_ref.shape[0]):
        out_ref[step] = row_ref[...]


def spread(value, devices):
    return pl.pallas_call(
        spread_kernel,
        out_shape=pltpu.VMEM((devices, *value.shape), value.dtype),
        compiler_params=params(),
        cost_estimate=cost(AHEAD_FLOPS, 0),
        name="spread",
    )(value)


def unpack(message_ref, rows_ref):
    own = message_ref.shape[1]
    for at in range(message_ref.shape[0]):
        rows_ref[at * own : (at + 1) * own, :] = message_ref[at].astype(jnp.float32)


def iota(shape, axis):
    return lax.broadcasted_iota(jnp.int32, shape, axis)


def by_key(value_of, rows, wide, key_of_row, keys):
    key = key_of_row(iota((rows, wide), 0))
    result = jnp.zeros((rows, wide), jnp.float32)
    for at in range(keys):
        result = jnp.where(key == at, value_of(at), result)
    return result


def split(value):
    return jnp.concatenate([piece.astype(jnp.float32) for piece in pieces_of(value)], 0)


def forward_kernel(
    got_ref,
    events_ref,
    gate_ref,
    first_ref,
    second_ref,
    part_ref,
    every_ref,
    every_turned_ref,
    hidden_turned_ref,
    slope_ref,
    share_ref,
    share_turned_ref,
    wide_ref,
):
    own = got_ref.shape[1]
    rows, width = every_ref.shape
    chunk = min(rows, LANES)
    unpack(got_ref, wide_ref)

    def body(step):
        here = span(step, chunk)
        wide = wide_ref[here, :]
        every = wide.astype(jnp.bfloat16)
        every_ref[here, :] = every
        every_turned_ref[:, here] = wide.T.astype(jnp.bfloat16)
        pre = dot(every, first_ref[...], (1, 0))
        hidden, slope = gelu_pair(pre)
        part = dot(hidden.astype(jnp.bfloat16), second_ref[...], (1, 0)).astype(jnp.bfloat16)
        for at in range(chunk // own):
            part_ref[step * (chunk // own) + at] = part[at * own : (at + 1) * own]
        slope_ref[here, :] = slope
        hidden_turned_ref[:, here] = hidden.T.astype(jnp.bfloat16)

    steps(rows // chunk, rows == chunk, body)

    tasks, experts, _ = gate_ref.shape
    pairs, slots = tasks * own, experts * own
    events = events_ref[...].astype(jnp.float32)
    events = by_key(
        lambda row: events[row : row + 1], pairs, width, lambda at: lax.rem(at, own), own
    ).astype(jnp.bfloat16)
    gates = by_key(
        lambda task: dot(events, gate_ref[task], (1, 1)), pairs, experts, lambda at: at // own, tasks
    )
    gates = jnp.exp(gates - jnp.max(gates, -1, keepdims=True))
    gates = gates / jnp.sum(gates, -1, keepdims=True)
    gates = split(gates).astype(jnp.bfloat16)
    place = (iota((experts, slots), 0) == iota((experts, slots), 1) // own).astype(jnp.bfloat16)

    def same(shape):
        return lax.rem(iota(shape, 0), own) == lax.rem(iota(shape, 1), own)

    share_ref[...] = jnp.where(same((3 * pairs, slots)), dot(gates, place, (1, 0)), 0.0)
    share_turned_ref[...] = jnp.where(same((slots, 3 * pairs)), dot(place, gates, (0, 1)), 0.0)


def forward(got, events, gate, first, second):
    devices, own, width = got.shape
    rows = devices * own
    units = first.shape[1]
    pairs, slots = gate.shape[0] * own, gate.shape[1] * own
    return pl.pallas_call(
        forward_kernel,
        out_shape=[
            pltpu.VMEM(got.shape, jnp.bfloat16),
            pltpu.VMEM((rows, width), jnp.bfloat16),
            pltpu.VMEM((width, rows), jnp.bfloat16),
            pltpu.VMEM((units, rows), jnp.bfloat16),
            pltpu.VMEM((rows, units), jnp.float32),
            pltpu.VMEM((3 * pairs, slots), jnp.float32),
            pltpu.VMEM((slots, 3 * pairs), jnp.float32),
        ],
        scratch_shapes=[pltpu.VMEM((rows, width), jnp.float32)],
        compiler_params=params(),
        cost_estimate=cost(4 * rows * width * units, 4 * width * units),
        name="forward",
    )(got, events, gate, in_vmem(first), in_vmem(second))


def middle_kernel(
    dp,
    parts_ref,
    share_ref,
    share_turned_ref,
    labels_ref,
    tower_in_ref,
    bias_ref,
    weight_ref,
    shift_ref,
    message_ref,
    outs_ref,
):
    devices, own, width = parts_ref.shape
    experts = devices // dp
    tasks, _, units = tower_in_ref.shape
    pairs = tasks * own
    float32, bfloat16 = jnp.float32, jnp.bfloat16

    def of_task(value_of, wide):
        return by_key(value_of, pairs, wide, lambda at: at // own, tasks)

    def fold(value):
        return value[:pairs] + value[pairs : 2 * pairs] + value[2 * pairs :]

    def only(value, task):
        at = lax.rem(iota(value.shape, 0), pairs) // own
        return jnp.where(at == task, value, 0.0).astype(bfloat16)

    for expert in range(experts):
        total = parts_ref[expert].astype(float32)
        for at in range(1, dp):
            total = total + parts_ref[at * experts + expert].astype(float32)
        outs_ref[expert * own : (expert + 1) * own, :] = total
    outs = outs_ref[...].astype(bfloat16)

    share = share_ref[...].astype(bfloat16)
    mixed = fold(dot(share, outs, (1, 0))).astype(bfloat16).astype(float32)
    tower = of_task(lambda task: bias_ref[task : task + 1, :], units)
    weight = of_task(lambda task: weight_ref[task : task + 1, :], units)
    shift = of_task(lambda task: shift_ref[:, task : task + 1], 1)
    labels = labels_ref[...].astype(float32)
    labels = by_key(lambda row: labels[row : row + 1], pairs, tasks, lambda at: lax.rem(at, own), own)
    pick = iota((pairs, tasks), 0) // own == iota((pairs, tasks), 1)
    target = jnp.sum(jnp.where(pick, labels, 0.0), -1, keepdims=True)
    for task in range(tasks):
        tower = tower + dot(only(mixed, task), tower_in_ref[task], (1, 0))
    active, slope = gelu_pair(tower)
    logit = jnp.sum(active * weight, -1, keepdims=True) + shift
    dlogit = jax.nn.sigmoid(logit) - target
    stack = split(slope * weight * dlogit)
    wide = dot(only(stack, 0), tower_in_ref[0], (1, 1))
    for task in range(1, tasks):
        wide = wide + dot(only(stack, task), tower_in_ref[task], (1, 1))
    dmixed = fold(wide).astype(bfloat16).astype(float32)
    thrice = jnp.concatenate([dmixed, dmixed, dmixed], 0).astype(bfloat16)

    turned = share_turned_ref[...]
    dexpert = dot(turned.astype(bfloat16), thrice, (1, 0)).astype(bfloat16)
    dprob = dot(outs, thrice, (1, 1))
    probs = turned[:, :pairs] + turned[:, pairs : 2 * pairs] + turned[:, 2 * pairs :]
    probs = jnp.concatenate([probs, probs, probs], 1)
    dgate = probs * (dprob - jnp.sum(probs * dprob, 0, keepdims=True))
    high, middle, low = pieces_of(dgate)
    group = iota(dgate.shape, 1) // pairs
    lanes = jnp.where(group == 1, middle.astype(float32), low.astype(float32))
    lanes = jnp.where(group == 0, high.astype(float32), lanes)
    lanes = jnp.concatenate([lanes, jnp.zeros((lanes.shape[0], LANES - 3 * pairs), float32)], 1)
    lanes = lanes.astype(bfloat16)
    for expert in range(experts):
        here = slice(expert * own, (expert + 1) * own)
        for at in range(dp):
            message_ref[at * experts + expert, :, :width] = dexpert[here]
            message_ref[at * experts + expert, :, width:] = lanes[here]


def middle(dp, parts, share, share_turned, labels, tower_in, bias, weight, shift):
    devices, own, width = parts.shape
    return pl.pallas_call(
        functools.partial(middle_kernel, dp),
        out_shape=pltpu.VMEM((devices, own, width + LANES), jnp.bfloat16),
        scratch_shapes=[pltpu.VMEM((devices // dp * own, width), jnp.float32)],
        compiler_params=params(),
        cost_estimate=cost(4 * 8 * tower_in.size, 2 * tower_in.size),
        name="middle",
    )(parts, share, share_turned, labels, in_vmem(tower_in), bias, weight, shift)


def backward_kernel(
    tasks,
    got_ref,
    every_ref,
    every_turned_ref,
    hidden_turned_ref,
    slope_ref,
    second_ref,
    grad_first_ref,
    grad_second_ref,
    grad_gate_ref,
    dpre_ref,
    first_buf,
    second_buf,
    arrived_ref,
    wide_ref,
    sems,
):
    rows, width = every_ref.shape
    own = got_ref.shape[1]
    units = slope_ref.shape[1]
    flat = rows <= LANES
    across, down = units // TILE, width // TILE

    def second_copy(step):
        here = span(step, TILE)
        return pltpu.make_async_copy(
            second_buf.at[here, :], grad_second_ref.at[here, :], sems.at[step]
        )

    def first_copy(step):
        here = span(step, TILE)
        return pltpu.make_async_copy(
            first_buf.at[here, :], grad_first_ref.at[here, :], sems.at[across + step]
        )

    def second_step(step):
        here = span(step, TILE)
        second_buf[here, :] = dot(
            hidden_turned_ref[here, :], arrived_ref[:, :width], (1, 0)
        ).astype(jnp.bfloat16)
        second_copy(step).start()

    def dpre_step(step):
        here = span(step, TILE)
        dhidden = dot(arrived_ref[:, :width], second_ref[here, :], (1, 1))
        dpre_ref[:, here] = (slope_ref[:, here] * dhidden).astype(jnp.bfloat16)

    def first_step(step):
        here = span(step, TILE)
        first_buf[here, :] = dot(
            every_turned_ref[here, :], dpre_ref[...], (1, 0)
        ).astype(jnp.bfloat16)
        first_copy(step).start()

    unpack(got_ref, wide_ref)
    arrived_ref[...] = wide_ref[...].astype(jnp.bfloat16)
    steps(across, flat, second_step)
    steps(across, flat, dpre_step)
    steps(down, flat, first_step)
    gate = dot(arrived_ref[:, width:], every_ref[...], (0, 0))
    for task in range(tasks):
        lanes = [(at * tasks + task) * own + row for at in range(3) for row in range(own)]
        grad_gate_ref[task] = sum(gate[lane : lane + 1] for lane in lanes)
    steps(across, flat, lambda step: second_copy(step).wait())
    steps(down, flat, lambda step: first_copy(step).wait())


def backward(got, every, every_turned, hidden_turned, slope, second, tasks):
    rows, width = every.shape
    units = slope.shape[1]
    anywhere = pl.BlockSpec(memory_space=pl.ANY)
    inside = pl.BlockSpec(memory_space=pltpu.VMEM)
    return pl.pallas_call(
        functools.partial(backward_kernel, tasks),
        out_shape=[
            jax.ShapeDtypeStruct((width, units), jnp.bfloat16),
            jax.ShapeDtypeStruct((units, width), jnp.bfloat16),
            jax.ShapeDtypeStruct((tasks, 1, width), jnp.float32),
        ],
        in_specs=[inside] * 6,
        out_specs=[anywhere, anywhere, inside],
        scratch_shapes=[
            pltpu.VMEM((rows, units), jnp.bfloat16),
            pltpu.VMEM((width, units), jnp.bfloat16),
            pltpu.VMEM((units, width), jnp.bfloat16),
            pltpu.VMEM((rows, width + LANES), jnp.bfloat16),
            pltpu.VMEM((rows, width + LANES), jnp.float32),
            pltpu.SemaphoreType.DMA((units // TILE + width // TILE,)),
        ],
        compiler_params=params(),
        cost_estimate=cost(6 * rows * width * units, 6 * width * units),
        name="backward",
    )(got, every, every_turned, hidden_turned, slope, in_vmem(second))


def per_device(
    events, labels, w_in, w_out, gate_weight, tower_in, tower_bias, tower_out, tower_out_bias
):
    dp = lax.axis_size("dp")
    devices = dp * lax.axis_size("expert")
    tasks = tower_in.shape[0]
    gate = jnp.transpose(gate_weight, (0, 2, 1))

    got = lax.all_to_all(spread(events, devices), BOTH, 0, 0, tiled=True)
    part, every, every_turned, hidden_turned, slope, share, share_turned = forward(
        got, events, gate, w_in[0], w_out[0]
    )

    parts = lax.all_to_all(part, BOTH, 0, 0, tiled=True)
    message = middle(
        dp, parts, share, share_turned, labels, tower_in, tower_bias, tower_out, tower_out_bias[None]
    )

    got = lax.all_to_all(message, BOTH, 0, 0, tiled=True)
    grad_first, grad_second, grad_gate = backward(
        got, every, every_turned, hidden_turned, slope, w_out[0], tasks
    )
    return (grad_first[None], grad_second[None], jnp.transpose(grad_gate, (0, 2, 1)))


def solution(mesh):
    placed = (
        P(BOTH, None),
        P(BOTH, None),
        P("expert", None, "dp"),
        P("expert", "dp", None),
        P(),
        P(),
        P(),
        P(),
        P(),
    )
    return jax.shard_map(
        per_device,
        mesh=mesh,
        in_specs=placed,
        out_specs=(P("expert", None, "dp"), P("expert", "dp", None), P(None, None, "expert")),
        check_vma=False,
    )
```

```python
import functools

import jax
import jax.numpy as jnp
from jax import lax
from jax.experimental import pallas as pl
from jax.experimental.pallas import tpu as pltpu
from jax.sharding import PartitionSpec as P

BOTH = ("dp", "expert")
LANES = 128
TILE = 256
GELU_C = 0.7978845608028654
GELU_A = 0.044715
AHEAD_FLOPS = 1 << 34
VMEM_LIMIT = 32 * 1024 * 1024


def gelu_pair(value):
    square = value * value
    bend = jnp.tanh(GELU_C * (value + GELU_A * value * square))
    inner = GELU_C * (1.0 + 3.0 * GELU_A * square)
    half = 0.5 * (1.0 + bend)
    return value * half, half + 0.5 * value * (1.0 - bend * bend) * inner


def pieces_of(value):
    high = value.astype(jnp.bfloat16)
    rest = value - high.astype(jnp.float32)
    middle = rest.astype(jnp.bfloat16)
    low = (rest - middle.astype(jnp.float32)).astype(jnp.bfloat16)
    return high, middle, low


def dot(left, right, over):
    return lax.dot_general(
        left, right, ((over[:1], over[1:]), ((), ())), preferred_element_type=jnp.float32
    )


def steps(count, flat, body):
    if flat:
        for step in range(count):
            body(step)
    else:
        lax.fori_loop(0, count, lambda step, none: (body(step), none)[1], None)


def span(step, size):
    return pl.ds(pl.multiple_of(step * size, size), size)


def params():
    return pltpu.CompilerParams(vmem_limit_bytes=VMEM_LIMIT)


def cost(flops, moved):
    return pl.CostEstimate(flops=flops, bytes_accessed=moved, transcendentals=0)


def in_vmem(value):
    return pltpu.with_memory_space_constraint(value, pltpu.VMEM)


def spread_kernel(row_ref, out_ref):
    for step in range(out_ref.shape[0]):
        out_ref[step] = row_ref[...]


def spread(value, devices):
    return pl.pallas_call(
        spread_kernel,
        out_shape=pltpu.VMEM((devices, *value.shape), value.dtype),
        compiler_params=params(),
        cost_estimate=cost(AHEAD_FLOPS, 0),
        name="spread",
    )(value)


def unpack(message_ref, rows_ref):
    own = message_ref.shape[1]
    for at in range(message_ref.shape[0]):
        rows_ref[at * own : (at + 1) * own, :] = message_ref[at].astype(jnp.float32)


def iota(shape, axis):
    return lax.broadcasted_iota(jnp.int32, shape, axis)


def by_key(value_of, rows, wide, key_of_row, keys):
    key = key_of_row(iota((rows, wide), 0))
    result = jnp.zeros((rows, wide), jnp.float32)
    for at in range(keys):
        result = jnp.where(key == at, value_of(at), result)
    return result


def split(value):
    return jnp.concatenate([piece.astype(jnp.float32) for piece in pieces_of(value)], 0)


def forward_kernel(
    got_ref,
    events_ref,
    gate_ref,
    first_ref,
    second_ref,
    part_ref,
    every_ref,
    pre_ref,
    hidden_ref,
    share_ref,
    share_turned_ref,
    wide_ref,
):
    own = got_ref.shape[1]
    rows, width = every_ref.shape
    chunk = min(rows, 64)
    unpack(got_ref, wide_ref)

    def body(step):
        here = span(step, chunk)
        every = wide_ref[here, :].astype(jnp.bfloat16)
        every_ref[here, :] = every
        pre = dot(every, first_ref[...], (1, 0))
        hidden = gelu_pair(pre)[0].astype(jnp.bfloat16)
        part = dot(hidden, second_ref[...], (1, 0)).astype(jnp.bfloat16)
        for at in range(chunk // own):
            part_ref[step * (chunk // own) + at] = part[at * own : (at + 1) * own]
        pre_ref[here, :] = pre
        hidden_ref[here, :] = hidden

    steps(rows // chunk, rows == chunk, body)

    tasks, experts, _ = gate_ref.shape
    pairs, slots = tasks * own, experts * own
    events = events_ref[...].astype(jnp.float32)
    events = by_key(
        lambda row: events[row : row + 1], pairs, width, lambda at: lax.rem(at, own), own
    ).astype(jnp.bfloat16)
    gates = by_key(
        lambda task: dot(events, gate_ref[task], (1, 1)), pairs, experts, lambda at: at // own, tasks
    )
    gates = jnp.exp(gates - jnp.max(gates, -1, keepdims=True))
    gates = gates / jnp.sum(gates, -1, keepdims=True)
    gates = split(gates).astype(jnp.bfloat16)
    place = (iota((experts, slots), 0) == iota((experts, slots), 1) // own).astype(jnp.bfloat16)

    def same(shape):
        return lax.rem(iota(shape, 0), own) == lax.rem(iota(shape, 1), own)

    share_ref[...] = jnp.where(same((3 * pairs, slots)), dot(gates, place, (1, 0)), 0.0)
    share_turned_ref[...] = jnp.where(same((slots, 3 * pairs)), dot(place, gates, (0, 1)), 0.0)


def forward(got, events, gate, first, second):
    devices, own, width = got.shape
    rows = devices * own
    units = first.shape[1]
    pairs, slots = gate.shape[0] * own, gate.shape[1] * own
    return pl.pallas_call(
        forward_kernel,
        out_shape=[
            pltpu.VMEM(got.shape, jnp.bfloat16),
            pltpu.VMEM((rows, width), jnp.bfloat16),
            pltpu.VMEM((rows, units), jnp.float32),
            pltpu.VMEM((rows, units), jnp.bfloat16),
            pltpu.VMEM((3 * pairs, slots), jnp.float32),
            pltpu.VMEM((slots, 3 * pairs), jnp.float32),
        ],
        scratch_shapes=[pltpu.VMEM((rows, width), jnp.float32)],
        compiler_params=params(),
        cost_estimate=cost(4 * rows * width * units, 4 * width * units),
        name="forward",
    )(got, events, gate, in_vmem(first), in_vmem(second))


def middle_kernel(
    dp,
    parts_ref,
    share_ref,
    share_turned_ref,
    labels_ref,
    tower_in_ref,
    bias_ref,
    weight_ref,
    shift_ref,
    message_ref,
    outs_ref,
):
    devices, own, width = parts_ref.shape
    experts = devices // dp
    tasks, _, units = tower_in_ref.shape
    pairs = tasks * own
    float32, bfloat16 = jnp.float32, jnp.bfloat16

    def of_task(value_of, wide):
        return by_key(value_of, pairs, wide, lambda at: at // own, tasks)

    def fold(value):
        return value[:pairs] + value[pairs : 2 * pairs] + value[2 * pairs :]

    def only(value, task):
        at = lax.rem(iota(value.shape, 0), pairs) // own
        return jnp.where(at == task, value, 0.0).astype(bfloat16)

    for expert in range(experts):
        total = parts_ref[expert].astype(float32)
        for at in range(1, dp):
            total = total + parts_ref[at * experts + expert].astype(float32)
        outs_ref[expert * own : (expert + 1) * own, :] = total
    outs = outs_ref[...].astype(bfloat16)

    share = share_ref[...].astype(bfloat16)
    mixed = fold(dot(share, outs, (1, 0))).astype(bfloat16).astype(float32)
    tower = of_task(lambda task: bias_ref[task : task + 1, :], units)
    weight = of_task(lambda task: weight_ref[task : task + 1, :], units)
    shift = of_task(lambda task: shift_ref[:, task : task + 1], 1)
    labels = labels_ref[...].astype(float32)
    labels = by_key(lambda row: labels[row : row + 1], pairs, tasks, lambda at: lax.rem(at, own), own)
    pick = iota((pairs, tasks), 0) // own == iota((pairs, tasks), 1)
    target = jnp.sum(jnp.where(pick, labels, 0.0), -1, keepdims=True)
    for task in range(tasks):
        tower = tower + dot(only(mixed, task), tower_in_ref[task], (1, 0))
    active, slope = gelu_pair(tower)
    logit = jnp.sum(active * weight, -1, keepdims=True) + shift
    dlogit = jax.nn.sigmoid(logit) - target
    stack = split(slope * weight * dlogit)
    wide = dot(only(stack, 0), tower_in_ref[0], (1, 1))
    for task in range(1, tasks):
        wide = wide + dot(only(stack, task), tower_in_ref[task], (1, 1))
    dmixed = fold(wide).astype(bfloat16).astype(float32)
    thrice = jnp.concatenate([dmixed, dmixed, dmixed], 0).astype(bfloat16)

    turned = share_turned_ref[...]
    dexpert = dot(turned.astype(bfloat16), thrice, (1, 0)).astype(bfloat16)
    dprob = dot(outs, thrice, (1, 1))
    probs = turned[:, :pairs] + turned[:, pairs : 2 * pairs] + turned[:, 2 * pairs :]
    probs = jnp.concatenate([probs, probs, probs], 1)
    dgate = probs * (dprob - jnp.sum(probs * dprob, 0, keepdims=True))
    high, middle, low = pieces_of(dgate)
    group = iota(dgate.shape, 1) // pairs
    lanes = jnp.where(group == 1, middle.astype(float32), low.astype(float32))
    lanes = jnp.where(group == 0, high.astype(float32), lanes)
    lanes = jnp.concatenate([lanes, jnp.zeros((lanes.shape[0], LANES - 3 * pairs), float32)], 1)
    lanes = lanes.astype(bfloat16)
    for expert in range(experts):
        here = slice(expert * own, (expert + 1) * own)
        for at in range(dp):
            message_ref[at * experts + expert, :, :width] = dexpert[here]
            message_ref[at * experts + expert, :, width:] = lanes[here]


def middle(dp, parts, share, share_turned, labels, tower_in, bias, weight, shift):
    devices, own, width = parts.shape
    return pl.pallas_call(
        functools.partial(middle_kernel, dp),
        out_shape=pltpu.VMEM((devices, own, width + LANES), jnp.bfloat16),
        scratch_shapes=[pltpu.VMEM((devices // dp * own, width), jnp.float32)],
        compiler_params=params(),
        cost_estimate=cost(4 * 8 * tower_in.size, 2 * tower_in.size),
        name="middle",
    )(parts, share, share_turned, labels, in_vmem(tower_in), bias, weight, shift)


def backward_kernel(
    tasks,
    got_ref,
    every_ref,
    hidden_ref,
    pre_ref,
    second_ref,
    grad_first_ref,
    grad_second_ref,
    grad_gate_ref,
    dpre_ref,
    first_buf,
    second_buf,
    arrived_ref,
    wide_ref,
    sems,
):
    rows, width = every_ref.shape
    own = got_ref.shape[1]
    units = pre_ref.shape[1]
    flat = rows <= 64
    across, down = units // LANES, width // LANES

    def second_copy(step):
        here = span(step, LANES)
        return pltpu.make_async_copy(
            second_buf.at[here, :], grad_second_ref.at[here, :], sems.at[step]
        )

    def first_copy(step):
        here = span(step, LANES)
        return pltpu.make_async_copy(
            first_buf.at[here, :], grad_first_ref.at[here, :], sems.at[across + step]
        )

    def second_step(step):
        here = span(step, LANES)
        for at in range(width // TILE):
            there = span(at, TILE)
            tile = dot(hidden_ref[:, here], arrived_ref[:, there], (0, 0))
            second_buf[here, there] = tile.astype(jnp.bfloat16)
        second_copy(step).start()

    def dpre_step(step):
        here = span(step, TILE)
        dhidden = dot(arrived_ref[:, :width], second_ref[here, :], (1, 1))
        dpre_ref[:, here] = (gelu_pair(pre_ref[:, here])[1] * dhidden).astype(jnp.bfloat16)

    def first_step(step):
        here = span(step, LANES)
        for at in range(units // TILE):
            there = span(at, TILE)
            tile = dot(every_ref[:, here], dpre_ref[:, there], (0, 0))
            first_buf[here, there] = tile.astype(jnp.bfloat16)
        first_copy(step).start()

    unpack(got_ref, wide_ref)
    arrived_ref[...] = wide_ref[...].astype(jnp.bfloat16)
    steps(across, flat, second_step)
    steps(units // TILE, flat, dpre_step)
    steps(down, flat, first_step)
    gate = dot(arrived_ref[:, width:], every_ref[...], (0, 0))
    for task in range(tasks):
        lanes = [(at * tasks + task) * own + row for at in range(3) for row in range(own)]
        grad_gate_ref[task] = sum(gate[lane : lane + 1] for lane in lanes)
    steps(across, flat, lambda step: second_copy(step).wait())
    steps(down, flat, lambda step: first_copy(step).wait())


def backward(got, every, hidden, pre, second, tasks):
    rows, width = every.shape
    units = pre.shape[1]
    anywhere = pl.BlockSpec(memory_space=pl.ANY)
    inside = pl.BlockSpec(memory_space=pltpu.VMEM)
    return pl.pallas_call(
        functools.partial(backward_kernel, tasks),
        out_shape=[
            jax.ShapeDtypeStruct((width, units), jnp.bfloat16),
            jax.ShapeDtypeStruct((units, width), jnp.bfloat16),
            jax.ShapeDtypeStruct((tasks, 1, width), jnp.float32),
        ],
        in_specs=[inside] * 5,
        out_specs=[anywhere, anywhere, inside],
        scratch_shapes=[
            pltpu.VMEM((rows, units), jnp.bfloat16),
            pltpu.VMEM((width, units), jnp.bfloat16),
            pltpu.VMEM((units, width), jnp.bfloat16),
            pltpu.VMEM((rows, width + LANES), jnp.bfloat16),
            pltpu.VMEM((rows, width + LANES), jnp.float32),
            pltpu.SemaphoreType.DMA((units // LANES + width // LANES,)),
        ],
        compiler_params=params(),
        cost_estimate=cost(6 * rows * width * units, 6 * width * units),
        name="backward",
    )(got, every, hidden, pre, in_vmem(second))


def per_device(
    events, labels, w_in, w_out, gate_weight, tower_in, tower_bias, tower_out, tower_out_bias
):
    dp = lax.axis_size("dp")
    devices = dp * lax.axis_size("expert")
    tasks = tower_in.shape[0]
    gate = jnp.transpose(gate_weight, (0, 2, 1))

    got = lax.all_to_all(spread(events, devices), BOTH, 0, 0, tiled=True)
    part, every, pre, hidden, share, share_turned = forward(got, events, gate, w_in[0], w_out[0])

    parts = lax.all_to_all(part, BOTH, 0, 0, tiled=True)
    message = middle(
        dp, parts, share, share_turned, labels, tower_in, tower_bias, tower_out, tower_out_bias[None]
    )

    got = lax.all_to_all(message, BOTH, 0, 0, tiled=True)
    grad_first, grad_second, grad_gate = backward(got, every, hidden, pre, w_out[0], tasks)
    return (grad_first[None], grad_second[None], jnp.transpose(grad_gate, (0, 2, 1)))


def solution(mesh):
    placed = (
        P(BOTH, None),
        P(BOTH, None),
        P("expert", None, "dp"),
        P("expert", "dp", None),
        P(),
        P(),
        P(),
        P(),
        P(),
    )
    return jax.shard_map(
        per_device,
        mesh=mesh,
        in_specs=placed,
        out_specs=(P("expert", None, "dp"), P("expert", "dp", None), P(None, None, "expert")),
        check_vma=False,
    )
```

```python
import functools

import jax
import jax.numpy as jnp
from jax import lax
from jax.experimental import pallas as pl
from jax.experimental.pallas import tpu as pltpu
from jax.sharding import PartitionSpec as P

BOTH = ("dp", "expert")
LANES = 128
TILE = 256
GELU_C = 0.7978845608028654
GELU_A = 0.044715
AHEAD_FLOPS = 1 << 34
VMEM_LIMIT = 32 * 1024 * 1024


def gelu_pair(value):
    square = value * value
    bend = jnp.tanh(GELU_C * (value + GELU_A * value * square))
    inner = GELU_C * (1.0 + 3.0 * GELU_A * square)
    half = 0.5 * (1.0 + bend)
    return value * half, half + 0.5 * value * (1.0 - bend * bend) * inner


def pieces_of(value):
    high = value.astype(jnp.bfloat16)
    rest = value - high.astype(jnp.float32)
    middle = rest.astype(jnp.bfloat16)
    low = (rest - middle.astype(jnp.float32)).astype(jnp.bfloat16)
    return high, middle, low


def dot(left, right, over):
    return lax.dot_general(
        left, right, ((over[:1], over[1:]), ((), ())), preferred_element_type=jnp.float32
    )


def steps(count, flat, body):
    if flat:
        for step in range(count):
            body(step)
    else:
        lax.fori_loop(0, count, lambda step, none: (body(step), none)[1], None)


def span(step, size):
    return pl.ds(pl.multiple_of(step * size, size), size)


def params():
    return pltpu.CompilerParams(vmem_limit_bytes=VMEM_LIMIT)


def cost(flops, moved):
    return pl.CostEstimate(flops=flops, bytes_accessed=moved, transcendentals=0)


def in_vmem(value):
    return pltpu.with_memory_space_constraint(value, pltpu.VMEM)


def spread_kernel(row_ref, out_ref):
    for step in range(out_ref.shape[0]):
        out_ref[step] = row_ref[...]


def spread(value, devices):
    return pl.pallas_call(
        spread_kernel,
        out_shape=pltpu.VMEM((devices, *value.shape), value.dtype),
        compiler_params=params(),
        cost_estimate=cost(AHEAD_FLOPS, 0),
        name="spread",
    )(value)


def unpack(message_ref, rows_ref):
    own = message_ref.shape[1]
    for at in range(message_ref.shape[0]):
        rows_ref[at * own : (at + 1) * own, :] = message_ref[at].astype(jnp.float32)


def iota(shape, axis):
    return lax.broadcasted_iota(jnp.int32, shape, axis)


def by_row(value, count):
    own = value.shape[0]
    row = lax.rem(iota((count, value.shape[1]), 0), own)
    result = jnp.zeros(row.shape, jnp.float32)
    for at in range(own):
        result = jnp.where(row == at, value[at : at + 1].astype(jnp.float32), result)
    return result


def forward_kernel(
    got_ref,
    events_ref,
    gate_ref,
    first_ref,
    second_ref,
    part_ref,
    every_ref,
    pre_ref,
    hidden_ref,
    prob_ref,
    wide_ref,
):
    own = got_ref.shape[1]
    rows, width = every_ref.shape
    chunk = min(rows, 64)
    unpack(got_ref, wide_ref)

    def body(step):
        here = span(step, chunk)
        every = wide_ref[here, :].astype(jnp.bfloat16)
        every_ref[here, :] = every
        pre = dot(every, first_ref[...], (1, 0))
        hidden = gelu_pair(pre)[0].astype(jnp.bfloat16)
        part = dot(hidden, second_ref[...], (1, 0)).astype(jnp.bfloat16)
        for at in range(chunk // own):
            part_ref[step * (chunk // own) + at] = part[at * own : (at + 1) * own]
        pre_ref[here, :] = pre
        hidden_ref[here, :] = hidden

    steps(rows // chunk, rows == chunk, body)

    tasks, experts, _ = gate_ref.shape
    slots = experts * own
    events = by_row(events_ref[...], slots).astype(jnp.bfloat16)
    mine = iota((slots, experts), 0) // own == iota((slots, experts), 1)
    lane = iota((slots, LANES), 1)
    probs = jnp.zeros((slots, LANES), jnp.float32)
    for task in range(tasks):
        gates = dot(events, gate_ref[task], (1, 1))
        gates = jnp.exp(gates - jnp.max(gates, -1, keepdims=True))
        prob = jnp.sum(jnp.where(mine, gates, 0.0), -1, keepdims=True)
        probs = jnp.where(lane == task, prob / jnp.sum(gates, -1, keepdims=True), probs)
    prob_ref[...] = probs


def forward(got, events, gate, first, second):
    devices, own, width = got.shape
    rows = devices * own
    units = first.shape[1]
    return pl.pallas_call(
        forward_kernel,
        out_shape=[
            pltpu.VMEM(got.shape, jnp.bfloat16),
            pltpu.VMEM((rows, width), jnp.bfloat16),
            pltpu.VMEM((rows, units), jnp.float32),
            pltpu.VMEM((rows, units), jnp.bfloat16),
            pltpu.VMEM((gate.shape[1] * own, LANES), jnp.float32),
        ],
        scratch_shapes=[pltpu.VMEM((rows, width), jnp.float32)],
        compiler_params=params(),
        cost_estimate=cost(4 * rows * width * units, 4 * width * units),
        name="forward",
    )(got, events, gate, in_vmem(first), in_vmem(second))


def middle_kernel(
    dp,
    parts_ref,
    prob_ref,
    labels_ref,
    tower_in_ref,
    bias_ref,
    weight_ref,
    shift_ref,
    message_ref,
    outs_ref,
):
    devices, own, width = parts_ref.shape
    experts = devices // dp
    slots = experts * own
    tasks = tower_in_ref.shape[0]
    float32, bfloat16 = jnp.float32, jnp.bfloat16

    for expert in range(experts):
        total = parts_ref[expert].astype(float32)
        for at in range(1, dp):
            total = total + parts_ref[at * experts + expert].astype(float32)
        outs_ref[expert * own : (expert + 1) * own, :] = total
    outs = outs_ref[...].astype(bfloat16)
    labels = by_row(labels_ref[...], slots)
    lane = iota((slots, LANES), 1)
    lanes = jnp.zeros((slots, LANES), float32)
    dexpert = jnp.zeros((slots, width), float32)
    for task in range(tasks):
        prob = prob_ref[:, task : task + 1]
        weight = weight_ref[task : task + 1, :]
        single = dot(outs, tower_in_ref[task], (1, 0))
        linear = single * prob
        shift = own
        while shift < slots:
            linear = linear + pltpu.roll(linear, shift, 0)
            shift *= 2
        active, slope = gelu_pair(linear + bias_ref[task : task + 1, :])
        logit = jnp.sum(active * weight, -1, keepdims=True) + shift_ref[:, task : task + 1]
        dlogit = jax.nn.sigmoid(logit) - labels[:, task : task + 1]
        dtower = slope * weight * dlogit
        dgate = prob * jnp.sum(dtower * (single - linear), -1, keepdims=True)
        stack = [piece.astype(float32) for piece in pieces_of(dtower)[:2]]
        stack = jnp.concatenate(stack, 0).astype(bfloat16)
        turned = dot(stack, tower_in_ref[task], (1, 1))
        dmixed = (turned[:slots] + turned[slots:]).astype(bfloat16).astype(float32)
        dexpert = dexpert + prob * dmixed
        for at, piece in enumerate(pieces_of(dgate)):
            lanes = jnp.where(lane == at * tasks + task, piece.astype(float32), lanes)
    dexpert = dexpert.astype(bfloat16)
    lanes = lanes.astype(bfloat16)
    for expert in range(experts):
        here = slice(expert * own, (expert + 1) * own)
        for at in range(dp):
            message_ref[at * experts + expert, :, :width] = dexpert[here]
            message_ref[at * experts + expert, :, width:] = lanes[here]


def middle(dp, parts, prob, labels, tower_in, bias, weight, shift):
    devices, own, width = parts.shape
    return pl.pallas_call(
        functools.partial(middle_kernel, dp),
        out_shape=pltpu.VMEM((devices, own, width + LANES), jnp.bfloat16),
        scratch_shapes=[pltpu.VMEM((devices // dp * own, width), jnp.float32)],
        compiler_params=params(),
        cost_estimate=cost(4 * 8 * tower_in.size, 2 * tower_in.size),
        name="middle",
    )(parts, prob, labels, in_vmem(tower_in), bias, weight, shift)


def backward_kernel(
    tasks,
    got_ref,
    every_ref,
    hidden_ref,
    pre_ref,
    second_ref,
    grad_first_ref,
    grad_second_ref,
    grad_gate_ref,
    dpre_ref,
    first_buf,
    second_buf,
    gate_buf,
    arrived_ref,
    wide_ref,
    sems,
):
    rows, width = every_ref.shape
    units = pre_ref.shape[1]
    flat = rows <= 64
    across, down = units // TILE, width // TILE

    def second_copy(step):
        here = span(step, TILE)
        return pltpu.make_async_copy(
            second_buf.at[here, :], grad_second_ref.at[here, :], sems.at[step]
        )

    def first_copy(step):
        here = span(step, TILE)
        return pltpu.make_async_copy(
            first_buf.at[here, :], grad_first_ref.at[here, :], sems.at[across + step]
        )

    def second_step(step):
        here = span(step, TILE)
        second_buf[here, :] = dot(
            hidden_ref[:, here], arrived_ref[:, :width], (0, 0)
        ).astype(jnp.bfloat16)
        second_copy(step).start()

    def dpre_step(step):
        here = span(step, TILE)
        dhidden = dot(arrived_ref[:, :width], second_ref[here, :], (1, 1))
        dpre_ref[:, here] = (gelu_pair(pre_ref[:, here])[1] * dhidden).astype(jnp.bfloat16)

    def first_step(step):
        here = span(step, TILE)
        first_buf[here, :] = dot(every_ref[:, here], dpre_ref[...], (0, 0)).astype(jnp.bfloat16)
        first_copy(step).start()

    unpack(got_ref, wide_ref)
    arrived_ref[...] = wide_ref[...].astype(jnp.bfloat16)
    steps(across, flat, second_step)
    gate = dot(arrived_ref[:, width:], every_ref[...], (0, 0))
    for task in range(tasks):
        lanes = [at * tasks + task for at in range(3)]
        gate_buf[task] = sum(gate[lane : lane + 1] for lane in lanes)
    gate_copy = pltpu.make_async_copy(gate_buf, grad_gate_ref, sems.at[across + down])
    gate_copy.start()
    steps(units // TILE, flat, dpre_step)
    steps(down, flat, first_step)
    gate_copy.wait()
    steps(across, flat, lambda step: second_copy(step).wait())
    steps(down, flat, lambda step: first_copy(step).wait())


def backward(got, every, hidden, pre, second, tasks):
    rows, width = every.shape
    units = pre.shape[1]
    anywhere = pl.BlockSpec(memory_space=pl.ANY)
    inside = pl.BlockSpec(memory_space=pltpu.VMEM)
    return pl.pallas_call(
        functools.partial(backward_kernel, tasks),
        out_shape=[
            jax.ShapeDtypeStruct((width, units), jnp.bfloat16),
            jax.ShapeDtypeStruct((units, width), jnp.bfloat16),
            jax.ShapeDtypeStruct((tasks, 1, width), jnp.float32),
        ],
        in_specs=[inside] * 5,
        out_specs=[anywhere] * 3,
        scratch_shapes=[
            pltpu.VMEM((rows, units), jnp.bfloat16),
            pltpu.VMEM((width, units), jnp.bfloat16),
            pltpu.VMEM((units, width), jnp.bfloat16),
            pltpu.VMEM((tasks, 1, width), jnp.float32),
            pltpu.VMEM((rows, width + LANES), jnp.bfloat16),
            pltpu.VMEM((rows, width + LANES), jnp.float32),
            pltpu.SemaphoreType.DMA((units // TILE + width // TILE + 1,)),
        ],
        compiler_params=params(),
        cost_estimate=cost(6 * rows * width * units, 6 * width * units),
        name="backward",
    )(got, every, hidden, pre, in_vmem(second))


def per_device(
    events, labels, w_in, w_out, gate_weight, tower_in, tower_bias, tower_out, tower_out_bias
):
    dp = lax.axis_size("dp")
    devices = dp * lax.axis_size("expert")
    tasks = tower_in.shape[0]
    gate = jnp.transpose(gate_weight, (0, 2, 1))

    got = lax.all_to_all(spread(events, devices), BOTH, 0, 0, tiled=True)
    part, every, pre, hidden, prob = forward(got, events, gate, w_in[0], w_out[0])

    parts = lax.all_to_all(part, BOTH, 0, 0, tiled=True)
    message = middle(
        dp, parts, prob, labels, tower_in, tower_bias, tower_out, tower_out_bias[None]
    )

    got = lax.all_to_all(message, BOTH, 0, 0, tiled=True)
    grad_first, grad_second, grad_gate = backward(got, every, hidden, pre, w_out[0], tasks)
    return (grad_first[None], grad_second[None], jnp.transpose(grad_gate, (0, 2, 1)))


def solution(mesh):
    placed = (
        P(BOTH, None),
        P(BOTH, None),
        P("expert", None, "dp"),
        P("expert", "dp", None),
        P(),
        P(),
        P(),
        P(),
        P(),
    )
    return jax.shard_map(
        per_device,
        mesh=mesh,
        in_specs=placed,
        out_specs=(P("expert", None, "dp"), P("expert", "dp", None), P(None, None, "expert")),
        check_vma=False,
    )
```

```python
import functools

import jax
import jax.numpy as jnp
from jax import lax
from jax.experimental import pallas as pl
from jax.experimental.pallas import tpu as pltpu
from jax.sharding import PartitionSpec as P

BOTH = ("dp", "expert")
LANES = 128
TILE = 256
GELU_C = 0.7978845608028654
GELU_A = 0.044715
AHEAD_FLOPS = 1 << 34
VMEM_LIMIT = 32 * 1024 * 1024


def gelu_pair(value):
    square = value * value
    bend = jnp.tanh(GELU_C * (value + GELU_A * value * square))
    inner = GELU_C * (1.0 + 3.0 * GELU_A * square)
    half = 0.5 * (1.0 + bend)
    return value * half, half + 0.5 * value * (1.0 - bend * bend) * inner


def pieces_of(value):
    high = value.astype(jnp.bfloat16)
    rest = value - high.astype(jnp.float32)
    middle = rest.astype(jnp.bfloat16)
    low = (rest - middle.astype(jnp.float32)).astype(jnp.bfloat16)
    return high, middle, low


def dot(left, right, over):
    return lax.dot_general(
        left, right, ((over[:1], over[1:]), ((), ())), preferred_element_type=jnp.float32
    )


def steps(count, flat, body):
    if flat:
        for step in range(count):
            body(step)
    else:
        lax.fori_loop(0, count, lambda step, none: (body(step), none)[1], None)


def span(step, size):
    return pl.ds(pl.multiple_of(step * size, size), size)


def params():
    return pltpu.CompilerParams(vmem_limit_bytes=VMEM_LIMIT)


def cost(flops, moved):
    return pl.CostEstimate(flops=flops, bytes_accessed=moved, transcendentals=0)


def in_vmem(value):
    return pltpu.with_memory_space_constraint(value, pltpu.VMEM)


def spread_kernel(row_ref, out_ref):
    for step in range(out_ref.shape[0]):
        out_ref[step] = row_ref[...]


def spread(value, devices):
    return pl.pallas_call(
        spread_kernel,
        out_shape=pltpu.VMEM((devices, *value.shape), value.dtype),
        compiler_params=params(),
        cost_estimate=cost(AHEAD_FLOPS, 0),
        name="spread",
    )(value)


def unpack(message_ref, rows_ref):
    own = message_ref.shape[1]
    for at in range(message_ref.shape[0]):
        rows_ref[at * own : (at + 1) * own, :] = message_ref[at].astype(jnp.float32)


def iota(shape, axis):
    return lax.broadcasted_iota(jnp.int32, shape, axis)


def by_row(value, count):
    own = value.shape[0]
    row = lax.rem(iota((count, value.shape[1]), 0), own)
    result = jnp.zeros(row.shape, jnp.float32)
    for at in range(own):
        result = jnp.where(row == at, value[at : at + 1].astype(jnp.float32), result)
    return result


def forward_kernel(
    got_ref,
    events_ref,
    gate_ref,
    first_ref,
    second_ref,
    part_ref,
    every_ref,
    pre_ref,
    hidden_ref,
    prob_ref,
    wide_ref,
):
    own = got_ref.shape[1]
    rows, width = every_ref.shape
    chunk = min(rows, 64)
    unpack(got_ref, wide_ref)

    def body(step):
        here = span(step, chunk)
        every = wide_ref[here, :].astype(jnp.bfloat16)
        every_ref[here, :] = every
        pre = dot(every, first_ref[...], (1, 0))
        hidden = gelu_pair(pre)[0].astype(jnp.bfloat16)
        part = dot(hidden, second_ref[...], (1, 0)).astype(jnp.bfloat16)
        for at in range(chunk // own):
            part_ref[step * (chunk // own) + at] = part[at * own : (at + 1) * own]
        pre_ref[here, :] = pre
        hidden_ref[here, :] = hidden

    steps(rows // chunk, rows == chunk, body)

    slots = prob_ref.shape[0]
    experts = slots // own
    tasks = gate_ref.shape[0] // experts
    events = by_row(events_ref[...], slots).astype(jnp.bfloat16)
    mine = iota((slots, experts), 0) // own == iota((slots, experts), 1)
    lane = iota((slots, LANES), 1)
    probs = jnp.zeros((slots, LANES), jnp.float32)
    logits = dot(events, gate_ref[...], (1, 1))
    for task in range(tasks):
        gates = logits[:, task * experts : (task + 1) * experts]
        gates = jnp.exp(gates - jnp.max(gates, -1, keepdims=True))
        prob = jnp.sum(jnp.where(mine, gates, 0.0), -1, keepdims=True)
        probs = jnp.where(lane == task, prob / jnp.sum(gates, -1, keepdims=True), probs)
    prob_ref[...] = probs


def forward(got, events, gate, first, second, experts):
    devices, own, width = got.shape
    rows = devices * own
    units = first.shape[1]
    return pl.pallas_call(
        forward_kernel,
        out_shape=[
            pltpu.VMEM(got.shape, jnp.bfloat16),
            pltpu.VMEM((rows, width), jnp.bfloat16),
            pltpu.VMEM((rows, units), jnp.float32),
            pltpu.VMEM((rows, units), jnp.bfloat16),
            pltpu.VMEM((experts * own, LANES), jnp.float32),
        ],
        scratch_shapes=[pltpu.VMEM((rows, width), jnp.float32)],
        compiler_params=params(),
        cost_estimate=cost(4 * rows * width * units, 4 * width * units),
        name="forward",
    )(got, events, gate, in_vmem(first), in_vmem(second))


def middle_kernel(
    dp,
    parts_ref,
    prob_ref,
    labels_ref,
    tower_in_ref,
    bias_ref,
    weight_ref,
    shift_ref,
    message_ref,
):
    slots, width = parts_ref.shape[0] // dp, parts_ref.shape[1]
    own = labels_ref.shape[0]
    tasks = tower_in_ref.shape[0]
    float32, bfloat16 = jnp.float32, jnp.bfloat16

    total = parts_ref[:slots, :].astype(float32)
    for at in range(1, dp):
        total = total + parts_ref[at * slots : (at + 1) * slots, :].astype(float32)
    outs = total.astype(bfloat16)
    labels = by_row(labels_ref[...], slots)
    lane = iota((slots, LANES), 1)
    lanes = jnp.zeros((slots, LANES), float32)
    dexpert = jnp.zeros((slots, width), float32)
    for task in range(tasks):
        prob = prob_ref[:, task : task + 1]
        weight = weight_ref[task : task + 1, :]
        single = dot(outs, tower_in_ref[task], (1, 0))
        linear = single * prob
        shift = own
        while shift < slots:
            linear = linear + pltpu.roll(linear, shift, 0)
            shift *= 2
        active, slope = gelu_pair(linear + bias_ref[task : task + 1, :])
        logit = jnp.sum(active * weight, -1, keepdims=True) + shift_ref[:, task : task + 1]
        dlogit = jax.nn.sigmoid(logit) - labels[:, task : task + 1]
        dtower = slope * weight * dlogit
        dgate = prob * jnp.sum(dtower * (single - linear), -1, keepdims=True)
        stack = [piece.astype(float32) for piece in pieces_of(dtower)[:2]]
        stack = jnp.concatenate(stack, 0).astype(bfloat16)
        turned = dot(stack, tower_in_ref[task], (1, 1))
        dmixed = (turned[:slots] + turned[slots:]).astype(bfloat16).astype(float32)
        dexpert = dexpert + prob * dmixed
        for at, piece in enumerate(pieces_of(dgate)):
            lanes = jnp.where(lane == at * tasks + task, piece.astype(float32), lanes)
    dexpert = dexpert.astype(bfloat16)
    lanes = lanes.astype(bfloat16)
    for at in range(dp):
        message_ref[at * slots : (at + 1) * slots, :width] = dexpert
        message_ref[at * slots : (at + 1) * slots, width:] = lanes


def middle(dp, parts, prob, labels, tower_in, bias, weight, shift):
    rows, width = parts.shape
    return pl.pallas_call(
        functools.partial(middle_kernel, dp),
        out_shape=pltpu.VMEM((rows, width + LANES), jnp.bfloat16),
        compiler_params=params(),
        cost_estimate=cost(4 * 8 * tower_in.size, 2 * tower_in.size),
        name="middle",
    )(parts, prob, labels, in_vmem(tower_in), bias, weight, shift)


def backward_kernel(
    tasks,
    got_ref,
    every_ref,
    hidden_ref,
    pre_ref,
    second_ref,
    grad_first_ref,
    grad_second_ref,
    grad_gate_ref,
    dpre_ref,
    first_buf,
    second_buf,
    gate_buf,
    arrived_ref,
    wide_ref,
    sems,
):
    rows, width = every_ref.shape
    units = pre_ref.shape[1]
    flat = rows <= 64
    across, down = units // TILE, width // TILE

    def second_copy(step):
        here = span(step, TILE)
        return pltpu.make_async_copy(
            second_buf.at[here, :], grad_second_ref.at[here, :], sems.at[step]
        )

    def first_copy(step):
        here = span(step, TILE)
        return pltpu.make_async_copy(
            first_buf.at[here, :], grad_first_ref.at[here, :], sems.at[across + step]
        )

    def second_step(step):
        here = span(step, TILE)
        second_buf[here, :] = dot(
            hidden_ref[:, here], arrived_ref[:, :width], (0, 0)
        ).astype(jnp.bfloat16)
        second_copy(step).start()

    def dpre_step(step):
        here = span(step, TILE)
        dhidden = dot(arrived_ref[:, :width], second_ref[here, :], (1, 1))
        dpre_ref[:, here] = (gelu_pair(pre_ref[:, here])[1] * dhidden).astype(jnp.bfloat16)

    def first_step(step):
        here = span(step, TILE)
        first_buf[here, :] = dot(every_ref[:, here], dpre_ref[...], (0, 0)).astype(jnp.bfloat16)
        first_copy(step).start()

    unpack(got_ref, wide_ref)
    arrived_ref[...] = wide_ref[...].astype(jnp.bfloat16)
    steps(across, flat, second_step)
    gate = dot(arrived_ref[:, width:], every_ref[...], (0, 0))
    for task in range(tasks):
        lanes = [at * tasks + task for at in range(3)]
        gate_buf[task] = sum(gate[lane : lane + 1] for lane in lanes)
    gate_copy = pltpu.make_async_copy(gate_buf, grad_gate_ref, sems.at[across + down])
    gate_copy.start()
    steps(units // TILE, flat, dpre_step)
    steps(down, flat, first_step)
    gate_copy.wait()
    steps(across, flat, lambda step: second_copy(step).wait())
    steps(down, flat, lambda step: first_copy(step).wait())


def backward(got, every, hidden, pre, second, tasks):
    rows, width = every.shape
    units = pre.shape[1]
    anywhere = pl.BlockSpec(memory_space=pl.ANY)
    inside = pl.BlockSpec(memory_space=pltpu.VMEM)
    return pl.pallas_call(
        functools.partial(backward_kernel, tasks),
        out_shape=[
            jax.ShapeDtypeStruct((width, units), jnp.bfloat16),
            jax.ShapeDtypeStruct((units, width), jnp.bfloat16),
            jax.ShapeDtypeStruct((tasks, 1, width), jnp.float32),
        ],
        in_specs=[inside] * 5,
        out_specs=[anywhere] * 3,
        scratch_shapes=[
            pltpu.VMEM((rows, units), jnp.bfloat16),
            pltpu.VMEM((width, units), jnp.bfloat16),
            pltpu.VMEM((units, width), jnp.bfloat16),
            pltpu.VMEM((tasks, 1, width), jnp.float32),
            pltpu.VMEM((rows, width + LANES), jnp.bfloat16),
            pltpu.VMEM((rows, width + LANES), jnp.float32),
            pltpu.SemaphoreType.DMA((units // TILE + width // TILE + 1,)),
        ],
        compiler_params=params(),
        cost_estimate=cost(6 * rows * width * units, 6 * width * units),
        name="backward",
    )(got, every, hidden, pre, in_vmem(second))


def per_device(
    events, labels, w_in, w_out, gate_weight, tower_in, tower_bias, tower_out, tower_out_bias
):
    dp = lax.axis_size("dp")
    experts = lax.axis_size("expert")
    devices = dp * experts
    tasks = tower_in.shape[0]
    gate = jnp.transpose(gate_weight, (0, 2, 1)).reshape(tasks * experts, events.shape[1])

    got = lax.all_to_all(spread(events, devices), BOTH, 0, 0, tiled=True)
    part, every, pre, hidden, prob = forward(got, events, gate, w_in[0], w_out[0], experts)

    parts = lax.all_to_all(part, BOTH, 0, 0, tiled=True).reshape(-1, events.shape[1])
    message = middle(
        dp, parts, prob, labels, tower_in, tower_bias, tower_out, tower_out_bias[None]
    )

    message = message.reshape(devices, events.shape[0], -1)
    got = lax.all_to_all(message, BOTH, 0, 0, tiled=True)
    grad_first, grad_second, grad_gate = backward(got, every, hidden, pre, w_out[0], tasks)
    return (grad_first[None], grad_second[None], jnp.transpose(grad_gate, (0, 2, 1)))


def solution(mesh):
    placed = (
        P(BOTH, None),
        P(BOTH, None),
        P("expert", None, "dp"),
        P("expert", "dp", None),
        P(),
        P(),
        P(),
        P(),
        P(),
    )
    return jax.shard_map(
        per_device,
        mesh=mesh,
        in_specs=placed,
        out_specs=(P("expert", None, "dp"), P("expert", "dp", None), P(None, None, "expert")),
        check_vma=False,
    )
```

```python
import functools

import jax
import jax.numpy as jnp
from jax import lax
from jax.experimental import pallas as pl
from jax.experimental.pallas import tpu as pltpu
from jax.sharding import PartitionSpec as P

BOTH = ("dp", "expert")
LANES = 128
TILE = 256
GELU_C = 0.7978845608028654
GELU_A = 0.044715
AHEAD_FLOPS = 1 << 34
VMEM_LIMIT = 32 * 1024 * 1024


def gelu_pair(value):
    square = value * value
    bend = jnp.tanh(GELU_C * (value + GELU_A * value * square))
    inner = GELU_C * (1.0 + 3.0 * GELU_A * square)
    half = 0.5 * (1.0 + bend)
    return value * half, half + 0.5 * value * (1.0 - bend * bend) * inner


def pieces_of(value):
    high = value.astype(jnp.bfloat16)
    rest = value - high.astype(jnp.float32)
    middle = rest.astype(jnp.bfloat16)
    low = (rest - middle.astype(jnp.float32)).astype(jnp.bfloat16)
    return high, middle, low


def dot(left, right, over):
    return lax.dot_general(
        left, right, ((over[:1], over[1:]), ((), ())), preferred_element_type=jnp.float32
    )


def steps(count, flat, body):
    if flat:
        for step in range(count):
            body(step)
    else:
        lax.fori_loop(0, count, lambda step, none: (body(step), none)[1], None)


def span(step, size):
    return pl.ds(pl.multiple_of(step * size, size), size)


def params():
    return pltpu.CompilerParams(vmem_limit_bytes=VMEM_LIMIT)


def cost(flops, moved):
    return pl.CostEstimate(flops=flops, bytes_accessed=moved, transcendentals=0)


def in_vmem(value):
    return pltpu.with_memory_space_constraint(value, pltpu.VMEM)


def spread_kernel(row_ref, out_ref):
    for step in range(out_ref.shape[0]):
        out_ref[step] = row_ref[...]


def spread(value, devices):
    return pl.pallas_call(
        spread_kernel,
        out_shape=pltpu.VMEM((devices, *value.shape), value.dtype),
        compiler_params=params(),
        cost_estimate=cost(AHEAD_FLOPS, 0),
        name="spread",
    )(value)


def unpack(message_ref, rows_ref):
    own = message_ref.shape[1]
    for at in range(message_ref.shape[0]):
        rows_ref[at * own : (at + 1) * own, :] = message_ref[at].astype(jnp.float32)


def iota(shape, axis):
    return lax.broadcasted_iota(jnp.int32, shape, axis)


def by_row(value, count):
    own = value.shape[0]
    row = lax.rem(iota((count, value.shape[1]), 0), own)
    result = jnp.zeros(row.shape, jnp.float32)
    for at in range(own):
        result = jnp.where(row == at, value[at : at + 1].astype(jnp.float32), result)
    return result


def forward_kernel(
    got_ref,
    events_ref,
    gate_ref,
    first_ref,
    second_ref,
    part_ref,
    every_ref,
    pre_ref,
    hidden_ref,
    prob_ref,
    wide_ref,
):
    own = got_ref.shape[1]
    rows, width = every_ref.shape
    chunk = min(rows, 64)
    slots = prob_ref.shape[0]
    experts = slots // own
    tasks = gate_ref.shape[0] // experts
    events = by_row(events_ref[...], slots).astype(jnp.bfloat16)
    mine = iota((slots, experts), 0) // own == iota((slots, experts), 1)
    lane = iota((slots, LANES), 1)
    probs = jnp.zeros((slots, LANES), jnp.float32)
    logits = dot(events, gate_ref[...], (1, 1))
    for task in range(tasks):
        gates = logits[:, task * experts : (task + 1) * experts]
        gates = jnp.exp(gates - jnp.max(gates, -1, keepdims=True))
        prob = jnp.sum(jnp.where(mine, gates, 0.0), -1, keepdims=True)
        probs = jnp.where(lane == task, prob / jnp.sum(gates, -1, keepdims=True), probs)
    prob_ref[...] = probs

    unpack(got_ref, wide_ref)

    def body(step):
        here = span(step, chunk)
        every = wide_ref[here, :].astype(jnp.bfloat16)
        every_ref[here, :] = every
        pre = dot(every, first_ref[...], (1, 0))
        hidden = gelu_pair(pre)[0].astype(jnp.bfloat16)
        part = dot(hidden, second_ref[...], (1, 0)).astype(jnp.bfloat16)
        for at in range(chunk // own):
            part_ref[step * (chunk // own) + at] = part[at * own : (at + 1) * own]
        pre_ref[here, :] = pre
        hidden_ref[here, :] = hidden

    steps(rows // chunk, rows == chunk, body)


def forward(got, events, gate, first, second, experts):
    devices, own, width = got.shape
    rows = devices * own
    units = first.shape[1]
    return pl.pallas_call(
        forward_kernel,
        out_shape=[
            pltpu.VMEM(got.shape, jnp.bfloat16),
            pltpu.VMEM((rows, width), jnp.bfloat16),
            pltpu.VMEM((rows, units), jnp.float32),
            pltpu.VMEM((rows, units), jnp.bfloat16),
            pltpu.VMEM((experts * own, LANES), jnp.float32),
        ],
        scratch_shapes=[pltpu.VMEM((rows, width), jnp.float32)],
        compiler_params=params(),
        cost_estimate=cost(4 * rows * width * units, 4 * width * units),
        name="forward",
    )(got, events, gate, in_vmem(first), in_vmem(second))


def middle_kernel(
    dp,
    parts_ref,
    prob_ref,
    labels_ref,
    tower_in_ref,
    bias_ref,
    weight_ref,
    shift_ref,
    message_ref,
    outs_ref,
):
    devices, own, width = parts_ref.shape
    experts = devices // dp
    slots = experts * own
    tasks = tower_in_ref.shape[0]
    float32, bfloat16 = jnp.float32, jnp.bfloat16

    for expert in range(experts):
        total = parts_ref[expert].astype(float32)
        for at in range(1, dp):
            total = total + parts_ref[at * experts + expert].astype(float32)
        outs_ref[expert * own : (expert + 1) * own, :] = total
    outs = outs_ref[...].astype(bfloat16)
    labels = by_row(labels_ref[...], slots)
    lane = iota((slots, LANES), 1)
    units = tower_in_ref.shape[2]

    def wide(ref):
        return jnp.concatenate([ref[task : task + 1, :] for task in range(tasks)], 1)

    def lanes_of(value, task):
        return value[:, task * units : (task + 1) * units]

    def each(columns):
        return jnp.concatenate(
            [jnp.broadcast_to(column, (slots, units)) for column in columns], 1
        )

    probs = [prob_ref[:, task : task + 1] for task in range(tasks)]
    single = jnp.concatenate(
        [dot(outs, tower_in_ref[task], (1, 0)) for task in range(tasks)], 1
    )
    linear = single * each(probs)
    shift = own
    while shift < slots:
        linear = linear + pltpu.roll(linear, shift, 0)
        shift *= 2
    active, slope = gelu_pair(linear + wide(bias_ref))
    weight = wide(weight_ref)
    active, slope = active * weight, slope * weight
    dlogit = []
    for task in range(tasks):
        logit = jnp.sum(lanes_of(active, task), -1, keepdims=True) + shift_ref[:, task : task + 1]
        dlogit.append(jax.nn.sigmoid(logit) - labels[:, task : task + 1])
    dtower = slope * each(dlogit)
    stack = [piece.astype(float32) for piece in pieces_of(dtower)[:2]]
    stack = jnp.concatenate(stack, 0).astype(bfloat16)
    turned = [
        dot(lanes_of(stack, task), tower_in_ref[task], (1, 1)) for task in range(tasks)
    ]
    rest = dtower * (single - linear)
    lanes = jnp.zeros((slots, LANES), float32)
    dexpert = jnp.zeros((slots, width), float32)
    for task in range(tasks):
        dgate = probs[task] * jnp.sum(lanes_of(rest, task), -1, keepdims=True)
        for at, piece in enumerate(pieces_of(dgate)):
            lanes = jnp.where(lane == at * tasks + task, piece.astype(float32), lanes)
        dmixed = (turned[task][:slots] + turned[task][slots:]).astype(bfloat16)
        dexpert = dexpert + probs[task] * dmixed.astype(float32)
    dexpert = dexpert.astype(bfloat16)
    lanes = lanes.astype(bfloat16)
    for expert in range(experts):
        here = slice(expert * own, (expert + 1) * own)
        for at in range(dp):
            message_ref[at * experts + expert, :, :width] = dexpert[here]
            message_ref[at * experts + expert, :, width:] = lanes[here]


def middle(dp, parts, prob, labels, tower_in, bias, weight, shift):
    devices, own, width = parts.shape
    return pl.pallas_call(
        functools.partial(middle_kernel, dp),
        out_shape=pltpu.VMEM((devices, own, width + LANES), jnp.bfloat16),
        scratch_shapes=[pltpu.VMEM((devices // dp * own, width), jnp.float32)],
        compiler_params=params(),
        cost_estimate=cost(4 * 8 * tower_in.size, 2 * tower_in.size),
        name="middle",
    )(parts, prob, labels, in_vmem(tower_in), bias, weight, shift)


def backward_kernel(
    tasks,
    got_ref,
    every_ref,
    hidden_ref,
    pre_ref,
    second_ref,
    grad_first_ref,
    grad_second_ref,
    grad_gate_ref,
    dpre_ref,
    first_buf,
    second_buf,
    gate_buf,
    arrived_ref,
    wide_ref,
    sems,
):
    rows, width = every_ref.shape
    units = pre_ref.shape[1]
    flat = rows <= 64
    across, down = units // TILE, width // TILE

    def second_copy(step):
        here = span(step, TILE)
        return pltpu.make_async_copy(
            second_buf.at[here, :], grad_second_ref.at[here, :], sems.at[step]
        )

    def first_copy(step):
        here = span(step, TILE)
        return pltpu.make_async_copy(
            first_buf.at[here, :], grad_first_ref.at[here, :], sems.at[across + step]
        )

    def second_step(step):
        here = span(step, TILE)
        second_buf[here, :] = dot(
            hidden_ref[:, here], arrived_ref[:, :width], (0, 0)
        ).astype(jnp.bfloat16)
        second_copy(step).start()

    def dpre_step(step):
        here = span(step, TILE)
        dhidden = dot(arrived_ref[:, :width], second_ref[here, :], (1, 1))
        dpre_ref[:, here] = (gelu_pair(pre_ref[:, here])[1] * dhidden).astype(jnp.bfloat16)

    def first_step(step):
        here = span(step, TILE)
        first_buf[here, :] = dot(every_ref[:, here], dpre_ref[...], (0, 0)).astype(jnp.bfloat16)
        first_copy(step).start()

    unpack(got_ref, wide_ref)
    arrived_ref[...] = wide_ref[...].astype(jnp.bfloat16)
    steps(across, flat, second_step)
    gate = dot(arrived_ref[:, width:], every_ref[...], (0, 0))
    for task in range(tasks):
        lanes = [at * tasks + task for at in range(3)]
        gate_buf[task] = sum(gate[lane : lane + 1] for lane in lanes)
    gate_copy = pltpu.make_async_copy(gate_buf, grad_gate_ref, sems.at[across + down])
    gate_copy.start()
    steps(units // TILE, flat, dpre_step)
    steps(down, flat, first_step)
    gate_copy.wait()
    steps(across, flat, lambda step: second_copy(step).wait())
    steps(down, flat, lambda step: first_copy(step).wait())


def backward(got, every, hidden, pre, second, tasks):
    rows, width = every.shape
    units = pre.shape[1]
    anywhere = pl.BlockSpec(memory_space=pl.ANY)
    inside = pl.BlockSpec(memory_space=pltpu.VMEM)
    return pl.pallas_call(
        functools.partial(backward_kernel, tasks),
        out_shape=[
            jax.ShapeDtypeStruct((width, units), jnp.bfloat16),
            jax.ShapeDtypeStruct((units, width), jnp.bfloat16),
            jax.ShapeDtypeStruct((tasks, 1, width), jnp.float32),
        ],
        in_specs=[inside] * 5,
        out_specs=[anywhere] * 3,
        scratch_shapes=[
            pltpu.VMEM((rows, units), jnp.bfloat16),
            pltpu.VMEM((width, units), jnp.bfloat16),
            pltpu.VMEM((units, width), jnp.bfloat16),
            pltpu.VMEM((tasks, 1, width), jnp.float32),
            pltpu.VMEM((rows, width + LANES), jnp.bfloat16),
            pltpu.VMEM((rows, width + LANES), jnp.float32),
            pltpu.SemaphoreType.DMA((units // TILE + width // TILE + 1,)),
        ],
        compiler_params=params(),
        cost_estimate=cost(6 * rows * width * units, 6 * width * units),
        name="backward",
    )(got, every, hidden, pre, in_vmem(second))


def per_device(
    events, labels, w_in, w_out, gate_weight, tower_in, tower_bias, tower_out, tower_out_bias
):
    dp = lax.axis_size("dp")
    experts = lax.axis_size("expert")
    devices = dp * experts
    tasks = tower_in.shape[0]
    gate = jnp.transpose(gate_weight, (0, 2, 1)).reshape(tasks * experts, events.shape[1])

    got = lax.all_to_all(spread(events, devices), BOTH, 0, 0, tiled=True)
    part, every, pre, hidden, prob = forward(got, events, gate, w_in[0], w_out[0], experts)

    parts = lax.all_to_all(part, BOTH, 0, 0, tiled=True)
    message = middle(
        dp, parts, prob, labels, tower_in, tower_bias, tower_out, tower_out_bias[None]
    )

    got = lax.all_to_all(message, BOTH, 0, 0, tiled=True)
    grad_first, grad_second, grad_gate = backward(got, every, hidden, pre, w_out[0], tasks)
    return (grad_first[None], grad_second[None], jnp.transpose(grad_gate, (0, 2, 1)))


def solution(mesh):
    placed = (
        P(BOTH, None),
        P(BOTH, None),
        P("expert", None, "dp"),
        P("expert", "dp", None),
        P(),
        P(),
        P(),
        P(),
        P(),
    )
    return jax.shard_map(
        per_device,
        mesh=mesh,
        in_specs=placed,
        out_specs=(P("expert", None, "dp"), P("expert", "dp", None), P(None, None, "expert")),
        check_vma=False,
    )
```

```python
import functools

import jax
import jax.numpy as jnp
from jax import lax
from jax.experimental import pallas as pl
from jax.experimental.pallas import tpu as pltpu
from jax.sharding import PartitionSpec as P

BOTH = ("dp", "expert")
LANES = 128
TILE = 256
GELU_C = 0.7978845608028654
GELU_A = 0.044715
AHEAD_FLOPS = 1 << 34
VMEM_LIMIT = 32 * 1024 * 1024


def gelu_pair(value):
    square = value * value
    bend = jnp.tanh(GELU_C * (value + GELU_A * value * square))
    inner = GELU_C * (1.0 + 3.0 * GELU_A * square)
    half = 0.5 * (1.0 + bend)
    return value * half, half + 0.5 * value * (1.0 - bend * bend) * inner


def pieces_of(value):
    high = value.astype(jnp.bfloat16)
    rest = value - high.astype(jnp.float32)
    middle = rest.astype(jnp.bfloat16)
    low = (rest - middle.astype(jnp.float32)).astype(jnp.bfloat16)
    return high, middle, low


def dot(left, right, over):
    return lax.dot_general(
        left, right, ((over[:1], over[1:]), ((), ())), preferred_element_type=jnp.float32
    )


def steps(count, flat, body):
    if flat:
        for step in range(count):
            body(step)
    else:
        lax.fori_loop(0, count, lambda step, none: (body(step), none)[1], None)


def span(step, size):
    return pl.ds(pl.multiple_of(step * size, size), size)


def params():
    return pltpu.CompilerParams(vmem_limit_bytes=VMEM_LIMIT)


def cost(flops, moved):
    return pl.CostEstimate(flops=flops, bytes_accessed=moved, transcendentals=0)


def in_vmem(value):
    return pltpu.with_memory_space_constraint(value, pltpu.VMEM)


def spread_kernel(row_ref, out_ref):
    for step in range(out_ref.shape[0]):
        out_ref[step] = row_ref[...]


def spread(value, devices):
    return pl.pallas_call(
        spread_kernel,
        out_shape=pltpu.VMEM((devices, *value.shape), value.dtype),
        compiler_params=params(),
        name="spread",
    )(value)


def ahead_kernel(value_ref, same_ref):
    del value_ref, same_ref


def ahead(value):
    return pl.pallas_call(
        ahead_kernel,
        in_specs=[pl.BlockSpec(memory_space=pl.ANY)],
        out_specs=pl.BlockSpec(memory_space=pl.ANY),
        out_shape=pltpu.VMEM(value.shape, value.dtype),
        input_output_aliases={0: 0},
        compiler_params=params(),
        cost_estimate=cost(AHEAD_FLOPS, 0),
        name="ahead",
    )(value)


def unpack(message_ref, rows_ref):
    own = message_ref.shape[1]
    for at in range(message_ref.shape[0]):
        rows_ref[at * own : (at + 1) * own, :] = message_ref[at].astype(jnp.float32)


def iota(shape, axis):
    return lax.broadcasted_iota(jnp.int32, shape, axis)


def by_row(value, count):
    own = value.shape[0]
    row = lax.rem(iota((count, value.shape[1]), 0), own)
    result = jnp.zeros(row.shape, jnp.float32)
    for at in range(own):
        result = jnp.where(row == at, value[at : at + 1].astype(jnp.float32), result)
    return result


def forward_kernel(
    got_ref,
    events_ref,
    gate_ref,
    first_ref,
    second_ref,
    part_ref,
    every_ref,
    pre_ref,
    hidden_ref,
    prob_ref,
    wide_ref,
):
    own = got_ref.shape[1]
    rows, width = every_ref.shape
    chunk = min(rows, 64)
    slots = prob_ref.shape[0]
    experts = slots // own
    tasks = gate_ref.shape[0] // experts
    events = by_row(events_ref[...], slots).astype(jnp.bfloat16)
    mine = iota((slots, experts), 0) // own == iota((slots, experts), 1)
    lane = iota((slots, LANES), 1)
    probs = jnp.zeros((slots, LANES), jnp.float32)
    logits = dot(events, gate_ref[...], (1, 1))
    for task in range(tasks):
        gates = logits[:, task * experts : (task + 1) * experts]
        gates = jnp.exp(gates - jnp.max(gates, -1, keepdims=True))
        prob = jnp.sum(jnp.where(mine, gates, 0.0), -1, keepdims=True)
        probs = jnp.where(lane == task, prob / jnp.sum(gates, -1, keepdims=True), probs)
    prob_ref[...] = probs

    unpack(got_ref, wide_ref)

    def body(step):
        here = span(step, chunk)
        every = wide_ref[here, :].astype(jnp.bfloat16)
        every_ref[here, :] = every
        blocks = [slice(at, at + TILE) for at in range(0, first_ref.shape[1], TILE)]
        pre = [dot(every, first_ref[:, block], (1, 0)) for block in blocks]
        part = 0.0
        for block, value in zip(blocks, pre):
            hidden = gelu_pair(value)[0].astype(jnp.bfloat16)
            part = part + dot(hidden, second_ref[block, :], (1, 0))
            pre_ref[here, block] = value
            hidden_ref[here, block] = hidden
        part = part.astype(jnp.bfloat16)
        for at in range(chunk // own):
            part_ref[step * (chunk // own) + at] = part[at * own : (at + 1) * own]

    steps(rows // chunk, rows == chunk, body)


def forward(got, events, gate, first, second, experts):
    devices, own, width = got.shape
    rows = devices * own
    units = first.shape[1]
    return pl.pallas_call(
        forward_kernel,
        out_shape=[
            pltpu.VMEM(got.shape, jnp.bfloat16),
            pltpu.VMEM((rows, width), jnp.bfloat16),
            pltpu.VMEM((rows, units), jnp.float32),
            pltpu.VMEM((rows, units), jnp.bfloat16),
            pltpu.VMEM((experts * own, LANES), jnp.float32),
        ],
        scratch_shapes=[pltpu.VMEM((rows, width), jnp.float32)],
        compiler_params=params(),
        cost_estimate=cost(4 * rows * width * units, 4 * width * units),
        name="forward",
    )(got, events, gate, in_vmem(first), in_vmem(second))


def middle_kernel(
    dp,
    parts_ref,
    prob_ref,
    labels_ref,
    tower_in_ref,
    bias_ref,
    weight_ref,
    shift_ref,
    message_ref,
    outs_ref,
):
    devices, own, width = parts_ref.shape
    experts = devices // dp
    slots = experts * own
    tasks = tower_in_ref.shape[0]
    float32, bfloat16 = jnp.float32, jnp.bfloat16

    for expert in range(experts):
        total = parts_ref[expert].astype(float32)
        for at in range(1, dp):
            total = total + parts_ref[at * experts + expert].astype(float32)
        outs_ref[expert * own : (expert + 1) * own, :] = total
    outs = outs_ref[...].astype(bfloat16)
    labels = by_row(labels_ref[...], slots)
    lane = iota((slots, LANES), 1)
    units = tower_in_ref.shape[2]

    def wide(ref):
        return jnp.concatenate([ref[task : task + 1, :] for task in range(tasks)], 1)

    def lanes_of(value, task):
        return value[:, task * units : (task + 1) * units]

    def each(columns):
        return jnp.concatenate(
            [jnp.broadcast_to(column, (slots, units)) for column in columns], 1
        )

    probs = [prob_ref[:, task : task + 1] for task in range(tasks)]
    single = jnp.concatenate(
        [dot(outs, tower_in_ref[task], (1, 0)) for task in range(tasks)], 1
    )
    linear = single * each(probs)
    shift = own
    while shift < slots:
        linear = linear + pltpu.roll(linear, shift, 0)
        shift *= 2
    active, slope = gelu_pair(linear + wide(bias_ref))
    weight = wide(weight_ref)
    active, slope = active * weight, slope * weight
    dlogit = []
    for task in range(tasks):
        logit = jnp.sum(lanes_of(active, task), -1, keepdims=True) + shift_ref[:, task : task + 1]
        dlogit.append(jax.nn.sigmoid(logit) - labels[:, task : task + 1])
    dtower = slope * each(dlogit)
    stack = [piece.astype(float32) for piece in pieces_of(dtower)[:2]]
    stack = jnp.concatenate(stack, 0).astype(bfloat16)
    turned = [
        dot(lanes_of(stack, task), tower_in_ref[task], (1, 1)) for task in range(tasks)
    ]
    rest = dtower * (single - linear)
    lanes = jnp.zeros((slots, LANES), float32)
    dexpert = jnp.zeros((slots, width), float32)
    for task in range(tasks):
        dgate = probs[task] * jnp.sum(lanes_of(rest, task), -1, keepdims=True)
        for at, piece in enumerate(pieces_of(dgate)):
            lanes = jnp.where(lane == at * tasks + task, piece.astype(float32), lanes)
        dmixed = (turned[task][:slots] + turned[task][slots:]).astype(bfloat16)
        dexpert = dexpert + probs[task] * dmixed.astype(float32)
    dexpert = dexpert.astype(bfloat16)
    lanes = lanes.astype(bfloat16)
    for expert in range(experts):
        here = slice(expert * own, (expert + 1) * own)
        for at in range(dp):
            message_ref[at * experts + expert, :, :width] = dexpert[here]
            message_ref[at * experts + expert, :, width:] = lanes[here]


def middle(dp, parts, prob, labels, tower_in, bias, weight, shift):
    devices, own, width = parts.shape
    return pl.pallas_call(
        functools.partial(middle_kernel, dp),
        out_shape=pltpu.VMEM((devices, own, width + LANES), jnp.bfloat16),
        scratch_shapes=[pltpu.VMEM((devices // dp * own, width), jnp.float32)],
        compiler_params=params(),
        cost_estimate=cost(4 * 8 * tower_in.size, 2 * tower_in.size),
        name="middle",
    )(parts, prob, labels, in_vmem(tower_in), bias, weight, shift)


def backward_kernel(
    tasks,
    got_ref,
    every_ref,
    hidden_ref,
    pre_ref,
    second_ref,
    grad_first_ref,
    grad_second_ref,
    grad_gate_ref,
    dpre_ref,
    first_buf,
    second_buf,
    gate_buf,
    arrived_ref,
    wide_ref,
    sems,
):
    rows, width = every_ref.shape
    units = pre_ref.shape[1]
    flat = rows <= 64
    blocks = units // TILE
    tops = width // TILE
    second_cuts = [1, blocks - 1]
    first_cuts = [tops - tops // 2, tops // 2 - tops // 4, tops // 4]

    def second_step(step):
        here = span(step, TILE)
        second_buf[here, :] = dot(
            hidden_ref[:, here], arrived_ref[:, :width], (0, 0)
        ).astype(jnp.bfloat16)

    def dpre_step(step):
        here = span(step, TILE)
        dhidden = dot(arrived_ref[:, :width], second_ref[here, :], (1, 1))
        dpre_ref[:, here] = (gelu_pair(pre_ref[:, here])[1] * dhidden).astype(jnp.bfloat16)

    def first_step(step):
        here = span(step, TILE)
        first_buf[here, :] = dot(every_ref[:, here], dpre_ref[...], (0, 0)).astype(jnp.bfloat16)

    copies = []

    def send(source, target):
        copies.append(pltpu.make_async_copy(source, target, sems.at[len(copies)]))
        copies[-1].start()

    def gradient(make, buf, target, cuts, at):
        for cut in filter(None, cuts):
            steps(cut, flat, lambda step: make(step + at))
            here = pl.ds(at * TILE, cut * TILE)
            send(buf.at[here, :], target.at[here, :])
            at += cut

    unpack(got_ref, wide_ref)
    arrived_ref[...] = wide_ref[...].astype(jnp.bfloat16)
    gradient(second_step, second_buf, grad_second_ref, second_cuts[:1], 0)
    steps(blocks, flat, dpre_step)
    gradient(second_step, second_buf, grad_second_ref, second_cuts[1:], second_cuts[0])
    gate = dot(arrived_ref[:, width:], every_ref[...], (0, 0))
    for task in range(tasks):
        lanes = [at * tasks + task for at in range(3)]
        gate_buf[task] = sum(gate[lane : lane + 1] for lane in lanes)
    send(gate_buf, grad_gate_ref)
    gradient(first_step, first_buf, grad_first_ref, first_cuts, 0)
    for copy in copies:
        copy.wait()


def backward(got, every, hidden, pre, second, tasks):
    rows, width = every.shape
    units = pre.shape[1]
    anywhere = pl.BlockSpec(memory_space=pl.ANY)
    inside = pl.BlockSpec(memory_space=pltpu.VMEM)
    return pl.pallas_call(
        functools.partial(backward_kernel, tasks),
        out_shape=[
            jax.ShapeDtypeStruct((width, units), jnp.bfloat16),
            jax.ShapeDtypeStruct((units, width), jnp.bfloat16),
            jax.ShapeDtypeStruct((tasks, 1, width), jnp.float32),
        ],
        in_specs=[inside] * 5,
        out_specs=[anywhere] * 3,
        scratch_shapes=[
            pltpu.VMEM((rows, units), jnp.bfloat16),
            pltpu.VMEM((width, units), jnp.bfloat16),
            pltpu.VMEM((units, width), jnp.bfloat16),
            pltpu.VMEM((tasks, 1, width), jnp.float32),
            pltpu.VMEM((rows, width + LANES), jnp.bfloat16),
            pltpu.VMEM((rows, width + LANES), jnp.float32),
            pltpu.SemaphoreType.DMA((6,)),
        ],
        compiler_params=params(),
        cost_estimate=cost(6 * rows * width * units, 6 * width * units),
        name="backward",
    )(got, every, hidden, pre, in_vmem(second))


def per_device(
    events, labels, w_in, w_out, gate_weight, tower_in, tower_bias, tower_out, tower_out_bias
):
    dp = lax.axis_size("dp")
    experts = lax.axis_size("expert")
    devices = dp * experts
    tasks = tower_in.shape[0]
    gate = jnp.transpose(gate_weight, (0, 2, 1)).reshape(tasks * experts, events.shape[1])

    got = lax.all_to_all(ahead(spread(events, devices)), BOTH, 0, 0, tiled=True)
    part, every, pre, hidden, prob = forward(got, events, gate, w_in[0], w_out[0], experts)

    parts = lax.all_to_all(part, BOTH, 0, 0, tiled=True)
    message = middle(
        dp, parts, prob, labels, tower_in, tower_bias, tower_out, tower_out_bias[None]
    )

    got = lax.all_to_all(message, BOTH, 0, 0, tiled=True)
    grad_first, grad_second, grad_gate = backward(got, every, hidden, pre, w_out[0], tasks)
    return (grad_first[None], grad_second[None], jnp.transpose(grad_gate, (0, 2, 1)))


def solution(mesh):
    placed = (
        P(BOTH, None),
        P(BOTH, None),
        P("expert", None, "dp"),
        P("expert", "dp", None),
        P(),
        P(),
        P(),
        P(),
        P(),
    )
    return jax.shard_map(
        per_device,
        mesh=mesh,
        in_specs=placed,
        out_specs=(P("expert", None, "dp"), P("expert", "dp", None), P(None, None, "expert")),
        check_vma=False,
    )
```

```python
import functools

import jax
import jax.numpy as jnp
from jax import lax
from jax.experimental import pallas as pl
from jax.experimental.pallas import tpu as pltpu
from jax.sharding import PartitionSpec as P

BOTH = ("dp", "expert")
LANES = 128
TILE = 256
GELU_C = 0.7978845608028654
GELU_A = 0.044715
AHEAD_FLOPS = 1 << 34
VMEM_LIMIT = 32 * 1024 * 1024


def gelu_pair(value):
    square = value * value
    bend = jnp.tanh(GELU_C * (value + GELU_A * value * square))
    inner = GELU_C * (1.0 + 3.0 * GELU_A * square)
    half = 0.5 * (1.0 + bend)
    return value * half, half + 0.5 * value * (1.0 - bend * bend) * inner


def pieces_of(value):
    high = value.astype(jnp.bfloat16)
    rest = value - high.astype(jnp.float32)
    middle = rest.astype(jnp.bfloat16)
    low = (rest - middle.astype(jnp.float32)).astype(jnp.bfloat16)
    return high, middle, low


def dot(left, right, over):
    return lax.dot_general(
        left, right, ((over[:1], over[1:]), ((), ())), preferred_element_type=jnp.float32
    )


def steps(count, flat, body):
    if flat:
        for step in range(count):
            body(step)
    else:
        lax.fori_loop(0, count, lambda step, none: (body(step), none)[1], None)


def span(step, size):
    return pl.ds(pl.multiple_of(step * size, size), size)


def params():
    return pltpu.CompilerParams(vmem_limit_bytes=VMEM_LIMIT)


def cost(flops, moved):
    return pl.CostEstimate(flops=flops, bytes_accessed=moved, transcendentals=0)


def in_vmem(value):
    return pltpu.with_memory_space_constraint(value, pltpu.VMEM)


def spread_kernel(row_ref, out_ref):
    for step in range(out_ref.shape[0]):
        out_ref[step] = row_ref[...]


def spread(value, devices):
    return pl.pallas_call(
        spread_kernel,
        out_shape=pltpu.VMEM((devices, *value.shape), value.dtype),
        compiler_params=params(),
        name="spread",
    )(value)


def ahead_kernel(value_ref, same_ref):
    del value_ref, same_ref


def ahead(value):
    return pl.pallas_call(
        ahead_kernel,
        in_specs=[pl.BlockSpec(memory_space=pl.ANY)],
        out_specs=pl.BlockSpec(memory_space=pl.ANY),
        out_shape=pltpu.VMEM(value.shape, value.dtype),
        input_output_aliases={0: 0},
        compiler_params=params(),
        cost_estimate=cost(AHEAD_FLOPS, 0),
        name="ahead",
    )(value)


def unpack(message_ref, rows_ref):
    own = message_ref.shape[1]
    for at in range(message_ref.shape[0]):
        rows_ref[at * own : (at + 1) * own, :] = message_ref[at].astype(jnp.float32)


def iota(shape, axis):
    return lax.broadcasted_iota(jnp.int32, shape, axis)


def by_row(value, count):
    own = value.shape[0]
    row = lax.rem(iota((count, value.shape[1]), 0), own)
    result = jnp.zeros(row.shape, jnp.float32)
    for at in range(own):
        result = jnp.where(row == at, value[at : at + 1].astype(jnp.float32), result)
    return result


def forward_kernel(
    got_ref,
    events_ref,
    gate_ref,
    first_ref,
    second_ref,
    part_ref,
    every_ref,
    pre_ref,
    hidden_ref,
    prob_ref,
    wide_ref,
):
    own = got_ref.shape[1]
    rows, width = every_ref.shape
    chunk = min(rows, 64)
    slots = prob_ref.shape[0]
    experts = slots // own
    tasks = gate_ref.shape[0] // experts
    events = by_row(events_ref[...], slots).astype(jnp.bfloat16)
    mine = iota((slots, experts), 0) // own == iota((slots, experts), 1)
    lane = iota((slots, LANES), 1)
    probs = jnp.zeros((slots, LANES), jnp.float32)
    logits = dot(events, gate_ref[...], (1, 1))
    for task in range(tasks):
        gates = logits[:, task * experts : (task + 1) * experts]
        gates = jnp.exp(gates - jnp.max(gates, -1, keepdims=True))
        prob = jnp.sum(jnp.where(mine, gates, 0.0), -1, keepdims=True)
        probs = jnp.where(lane == task, prob / jnp.sum(gates, -1, keepdims=True), probs)
    prob_ref[...] = probs

    unpack(got_ref, wide_ref)

    def body(step):
        here = span(step, chunk)
        every = wide_ref[here, :].astype(jnp.bfloat16)
        every_ref[here, :] = every
        blocks = [slice(at, at + TILE) for at in range(0, first_ref.shape[1], TILE)]
        pre = [dot(every, first_ref[:, block], (1, 0)) for block in blocks]
        part = 0.0
        for block, value in zip(blocks, pre):
            hidden = gelu_pair(value)[0].astype(jnp.bfloat16)
            part = part + dot(hidden, second_ref[block, :], (1, 0))
            pre_ref[here, block] = value
            hidden_ref[here, block] = hidden
        part = part.astype(jnp.bfloat16)
        for at in range(chunk // own):
            part_ref[step * (chunk // own) + at] = part[at * own : (at + 1) * own]

    steps(rows // chunk, rows == chunk, body)


def forward(got, events, gate, first, second, experts):
    devices, own, width = got.shape
    rows = devices * own
    units = first.shape[1]
    return pl.pallas_call(
        forward_kernel,
        out_shape=[
            pltpu.VMEM(got.shape, jnp.bfloat16),
            pltpu.VMEM((rows, width), jnp.bfloat16),
            pltpu.VMEM((rows, units), jnp.float32),
            pltpu.VMEM((rows, units), jnp.bfloat16),
            pltpu.VMEM((experts * own, LANES), jnp.float32),
        ],
        scratch_shapes=[pltpu.VMEM((rows, width), jnp.float32)],
        compiler_params=params(),
        cost_estimate=cost(4 * rows * width * units, 4 * width * units),
        name="forward",
    )(got, events, gate, in_vmem(first), in_vmem(second))


def middle_kernel(
    dp,
    parts_ref,
    prob_ref,
    labels_ref,
    tower_in_ref,
    bias_ref,
    weight_ref,
    shift_ref,
    message_ref,
    outs_ref,
):
    devices, own, width = parts_ref.shape
    experts = devices // dp
    slots = experts * own
    tasks = tower_in_ref.shape[0]
    float32, bfloat16 = jnp.float32, jnp.bfloat16

    for expert in range(experts):
        total = parts_ref[expert].astype(float32)
        for at in range(1, dp):
            total = total + parts_ref[at * experts + expert].astype(float32)
        outs_ref[expert * own : (expert + 1) * own, :] = total
    outs = outs_ref[...].astype(bfloat16)
    labels = by_row(labels_ref[...], slots)
    lane = iota((slots, LANES), 1)
    units = tower_in_ref.shape[2]

    def wide(ref):
        return jnp.concatenate([ref[task : task + 1, :] for task in range(tasks)], 1)

    def lanes_of(value, task):
        return value[:, task * units : (task + 1) * units]

    def each(columns):
        return jnp.concatenate(
            [jnp.broadcast_to(column, (slots, units)) for column in columns], 1
        )

    probs = [prob_ref[:, task : task + 1] for task in range(tasks)]
    single = jnp.concatenate(
        [dot(outs, tower_in_ref[task], (1, 0)) for task in range(tasks)], 1
    )
    linear = single * each(probs)
    shift = own
    while shift < slots:
        linear = linear + pltpu.roll(linear, shift, 0)
        shift *= 2
    active, slope = gelu_pair(linear + wide(bias_ref))
    weight = wide(weight_ref)
    active, slope = active * weight, slope * weight
    dlogit = []
    for task in range(tasks):
        logit = jnp.sum(lanes_of(active, task), -1, keepdims=True) + shift_ref[:, task : task + 1]
        dlogit.append(jax.nn.sigmoid(logit) - labels[:, task : task + 1])
    dtower = slope * each(dlogit)
    stack = [piece.astype(float32) for piece in pieces_of(dtower)[:2]]
    stack = jnp.concatenate(stack, 0).astype(bfloat16)
    turned = [
        dot(lanes_of(stack, task), tower_in_ref[task], (1, 1)) for task in range(tasks)
    ]
    rest = dtower * (single - linear)
    lanes = jnp.zeros((slots, LANES), float32)
    dexpert = jnp.zeros((slots, width), float32)
    for task in range(tasks):
        dgate = probs[task] * jnp.sum(lanes_of(rest, task), -1, keepdims=True)
        for at, piece in enumerate(pieces_of(dgate)):
            lanes = jnp.where(lane == at * tasks + task, piece.astype(float32), lanes)
        dmixed = (turned[task][:slots] + turned[task][slots:]).astype(bfloat16)
        dexpert = dexpert + probs[task] * dmixed.astype(float32)
    dexpert = dexpert.astype(bfloat16)
    lanes = lanes.astype(bfloat16)
    for expert in range(experts):
        here = slice(expert * own, (expert + 1) * own)
        for at in range(dp):
            message_ref[at * experts + expert, :, :width] = dexpert[here]
            message_ref[at * experts + expert, :, width:] = lanes[here]


def middle(dp, parts, prob, labels, tower_in, bias, weight, shift):
    devices, own, width = parts.shape
    return pl.pallas_call(
        functools.partial(middle_kernel, dp),
        out_shape=pltpu.VMEM((devices, own, width + LANES), jnp.bfloat16),
        scratch_shapes=[pltpu.VMEM((devices // dp * own, width), jnp.float32)],
        compiler_params=params(),
        cost_estimate=cost(4 * 8 * tower_in.size, 2 * tower_in.size),
        name="middle",
    )(parts, prob, labels, in_vmem(tower_in), bias, weight, shift)


def backward_kernel(
    tasks,
    got_ref,
    every_ref,
    hidden_ref,
    pre_ref,
    second_ref,
    grad_first_ref,
    grad_second_ref,
    grad_gate_ref,
    dpre_ref,
    first_buf,
    second_buf,
    gate_buf,
    hidden_turned,
    every_turned,
    arrived_ref,
    wide_ref,
    sems,
):
    rows, width = every_ref.shape
    units = pre_ref.shape[1]
    flat = rows <= 64
    blocks = units // TILE
    copies = []

    def turn(source, target):
        def block(step):
            here = span(step, LANES)
            target[here, :] = source[:, here].astype(jnp.float32).T.astype(jnp.bfloat16)

        steps(source.shape[1] // LANES, flat, block)

    def gradient(left, right, buf, target, cuts):
        at = 0
        for cut in cuts:

            def block(step, at=at):
                here = span(step + at, LANES)
                for across in range(buf.shape[1] // TILE):
                    there = span(across, TILE)
                    buf[here, there] = dot(left[here, :], right[:, there], (1, 0)).astype(
                        jnp.bfloat16
                    )

            steps(cut, flat, block)
            here = pl.ds(at * LANES, cut * LANES)
            send(buf.at[here, :], target.at[here, :])
            at += cut

    def send(source, target):
        copies.append(pltpu.make_async_copy(source, target, sems.at[len(copies)]))
        copies[-1].start()

    def dpre_step(step):
        here = span(step, TILE)
        dhidden = dot(arrived_ref[:, :width], second_ref[here, :], (1, 1))
        dpre_ref[:, here] = (gelu_pair(pre_ref[:, here])[1] * dhidden).astype(jnp.bfloat16)

    turn(hidden_ref, hidden_turned)
    unpack(got_ref, wide_ref)
    arrived_ref[...] = wide_ref[...].astype(jnp.bfloat16)
    gradient(
        hidden_turned, arrived_ref, second_buf, grad_second_ref, [2] * (units // LANES // 2)
    )
    turn(every_ref, every_turned)
    gate = dot(arrived_ref[:, width:], every_ref[...], (0, 0))
    for task in range(tasks):
        lanes = [at * tasks + task for at in range(3)]
        gate_buf[task] = sum(gate[lane : lane + 1] for lane in lanes)
    send(gate_buf, grad_gate_ref)
    steps(blocks, flat, dpre_step)
    gradient(
        every_turned,
        dpre_ref,
        first_buf,
        grad_first_ref,
        [2] * (width // LANES // 2 - 1) + [1, 1],
    )
    for copy in copies:
        copy.wait()


def backward(got, every, hidden, pre, second, tasks):
    rows, width = every.shape
    units = pre.shape[1]
    anywhere = pl.BlockSpec(memory_space=pl.ANY)
    inside = pl.BlockSpec(memory_space=pltpu.VMEM)
    return pl.pallas_call(
        functools.partial(backward_kernel, tasks),
        out_shape=[
            jax.ShapeDtypeStruct((width, units), jnp.bfloat16),
            jax.ShapeDtypeStruct((units, width), jnp.bfloat16),
            jax.ShapeDtypeStruct((tasks, 1, width), jnp.float32),
        ],
        in_specs=[inside] * 5,
        out_specs=[anywhere] * 3,
        scratch_shapes=[
            pltpu.VMEM((rows, units), jnp.bfloat16),
            pltpu.VMEM((width, units), jnp.bfloat16),
            pltpu.VMEM((units, width), jnp.bfloat16),
            pltpu.VMEM((tasks, 1, width), jnp.float32),
            pltpu.VMEM((units, rows), jnp.bfloat16),
            pltpu.VMEM((width, rows), jnp.bfloat16),
            pltpu.VMEM((rows, width + LANES), jnp.bfloat16),
            pltpu.VMEM((rows, width + LANES), jnp.float32),
            pltpu.SemaphoreType.DMA((units // TILE + width // TILE + 2,)),
        ],
        compiler_params=params(),
        cost_estimate=cost(6 * rows * width * units, 6 * width * units),
        name="backward",
    )(got, every, hidden, pre, in_vmem(second))


def per_device(
    events, labels, w_in, w_out, gate_weight, tower_in, tower_bias, tower_out, tower_out_bias
):
    dp = lax.axis_size("dp")
    experts = lax.axis_size("expert")
    devices = dp * experts
    tasks = tower_in.shape[0]
    gate = jnp.transpose(gate_weight, (0, 2, 1)).reshape(tasks * experts, events.shape[1])

    got = lax.all_to_all(ahead(spread(events, devices)), BOTH, 0, 0, tiled=True)
    part, every, pre, hidden, prob = forward(got, events, gate, w_in[0], w_out[0], experts)

    parts = lax.all_to_all(part, BOTH, 0, 0, tiled=True)
    message = middle(
        dp, parts, prob, labels, tower_in, tower_bias, tower_out, tower_out_bias[None]
    )

    got = lax.all_to_all(message, BOTH, 0, 0, tiled=True)
    grad_first, grad_second, grad_gate = backward(got, every, hidden, pre, w_out[0], tasks)
    return (grad_first[None], grad_second[None], jnp.transpose(grad_gate, (0, 2, 1)))


def solution(mesh):
    placed = (
        P(BOTH, None),
        P(BOTH, None),
        P("expert", None, "dp"),
        P("expert", "dp", None),
        P(),
        P(),
        P(),
        P(),
        P(),
    )
    return jax.shard_map(
        per_device,
        mesh=mesh,
        in_specs=placed,
        out_specs=(P("expert", None, "dp"), P("expert", "dp", None), P(None, None, "expert")),
        check_vma=False,
    )
```

```python
import functools

import jax
import jax.numpy as jnp
from jax import lax
from jax.experimental import pallas as pl
from jax.experimental.pallas import tpu as pltpu
from jax.sharding import PartitionSpec as P

BOTH = ("dp", "expert")
LANES = 128
TILE = 256
GELU_C = 0.7978845608028654
GELU_A = 0.044715
AHEAD_FLOPS = 1 << 34
VMEM_LIMIT = 32 * 1024 * 1024


def gelu_pair(value):
    square = value * value
    bend = jnp.tanh(GELU_C * (value + GELU_A * value * square))
    inner = GELU_C * (1.0 + 3.0 * GELU_A * square)
    half = 0.5 * (1.0 + bend)
    return value * half, half + 0.5 * value * (1.0 - bend * bend) * inner


def pieces_of(value):
    high = value.astype(jnp.bfloat16)
    rest = value - high.astype(jnp.float32)
    middle = rest.astype(jnp.bfloat16)
    low = (rest - middle.astype(jnp.float32)).astype(jnp.bfloat16)
    return high, middle, low


def dot(left, right, over):
    return lax.dot_general(
        left, right, ((over[:1], over[1:]), ((), ())), preferred_element_type=jnp.float32
    )


def steps(count, flat, body):
    if flat:
        for step in range(count):
            body(step)
    else:
        lax.fori_loop(0, count, lambda step, none: (body(step), none)[1], None)


def span(step, size):
    return pl.ds(pl.multiple_of(step * size, size), size)


def params():
    return pltpu.CompilerParams(vmem_limit_bytes=VMEM_LIMIT)


def cost(flops, moved):
    return pl.CostEstimate(flops=flops, bytes_accessed=moved, transcendentals=0)


def in_vmem(value):
    return pltpu.with_memory_space_constraint(value, pltpu.VMEM)


def spread_kernel(row_ref, out_ref):
    for step in range(out_ref.shape[0]):
        out_ref[step] = row_ref[...]


def spread(value, devices):
    return pl.pallas_call(
        spread_kernel,
        out_shape=pltpu.VMEM((devices, *value.shape), value.dtype),
        compiler_params=params(),
        name="spread",
    )(value)


def ahead_kernel(value_ref, same_ref):
    del value_ref, same_ref


def ahead(value):
    return pl.pallas_call(
        ahead_kernel,
        in_specs=[pl.BlockSpec(memory_space=pl.ANY)],
        out_specs=pl.BlockSpec(memory_space=pl.ANY),
        out_shape=pltpu.VMEM(value.shape, value.dtype),
        input_output_aliases={0: 0},
        compiler_params=params(),
        cost_estimate=cost(AHEAD_FLOPS, 0),
        name="ahead",
    )(value)


def unpack(message_ref, rows_ref):
    own = message_ref.shape[1]
    for at in range(message_ref.shape[0]):
        rows_ref[at * own : (at + 1) * own, :] = message_ref[at].astype(jnp.float32)


def iota(shape, axis):
    return lax.broadcasted_iota(jnp.int32, shape, axis)


def by_row(value, count):
    own = value.shape[0]
    row = lax.rem(iota((count, value.shape[1]), 0), own)
    result = jnp.zeros(row.shape, jnp.float32)
    for at in range(own):
        result = jnp.where(row == at, value[at : at + 1].astype(jnp.float32), result)
    return result


def forward_kernel(
    got_ref,
    events_ref,
    gate_ref,
    first_ref,
    second_ref,
    part_ref,
    every_ref,
    pre_ref,
    hidden_ref,
    prob_ref,
    wide_ref,
):
    own = got_ref.shape[1]
    rows, width = every_ref.shape
    chunk = min(rows, 64)
    slots = prob_ref.shape[0]
    experts = slots // own
    tasks = gate_ref.shape[0] // experts
    events = by_row(events_ref[...], slots).astype(jnp.bfloat16)
    mine = iota((slots, experts), 0) // own == iota((slots, experts), 1)
    lane = iota((slots, LANES), 1)
    probs = jnp.zeros((slots, LANES), jnp.float32)
    logits = dot(events, gate_ref[...], (1, 1))
    for task in range(tasks):
        gates = logits[:, task * experts : (task + 1) * experts]
        gates = jnp.exp(gates - jnp.max(gates, -1, keepdims=True))
        prob = jnp.sum(jnp.where(mine, gates, 0.0), -1, keepdims=True)
        probs = jnp.where(lane == task, prob / jnp.sum(gates, -1, keepdims=True), probs)
    prob_ref[...] = probs

    unpack(got_ref, wide_ref)

    def body(step):
        here = span(step, chunk)
        every = wide_ref[here, :].astype(jnp.bfloat16)
        every_ref[here, :] = every
        blocks = [slice(at, at + TILE) for at in range(0, first_ref.shape[1], TILE)]
        pre = [dot(every, first_ref[:, block], (1, 0)) for block in blocks]
        part = 0.0
        for block, value in zip(blocks, pre):
            hidden = gelu_pair(value)[0].astype(jnp.bfloat16)
            part = part + dot(hidden, second_ref[block, :], (1, 0))
            pre_ref[here, block] = value
            hidden_ref[here, block] = hidden
        part = part.astype(jnp.bfloat16)
        for at in range(chunk // own):
            part_ref[step * (chunk // own) + at] = part[at * own : (at + 1) * own]

    steps(rows // chunk, rows == chunk, body)


def forward(got, events, gate, first, second, experts):
    devices, own, width = got.shape
    rows = devices * own
    units = first.shape[1]
    return pl.pallas_call(
        forward_kernel,
        out_shape=[
            pltpu.VMEM(got.shape, jnp.bfloat16),
            pltpu.VMEM((rows, width), jnp.bfloat16),
            pltpu.VMEM((rows, units), jnp.float32),
            pltpu.VMEM((rows, units), jnp.bfloat16),
            pltpu.VMEM((experts * own, LANES), jnp.float32),
        ],
        scratch_shapes=[pltpu.VMEM((rows, width), jnp.float32)],
        compiler_params=params(),
        cost_estimate=cost(4 * rows * width * units, 4 * width * units),
        name="forward",
    )(got, events, gate, in_vmem(first), in_vmem(second))


def middle_kernel(
    dp,
    parts_ref,
    prob_ref,
    labels_ref,
    tower_in_ref,
    bias_ref,
    weight_ref,
    shift_ref,
    message_ref,
    outs_ref,
):
    devices, own, width = parts_ref.shape
    experts = devices // dp
    slots = experts * own
    tasks = tower_in_ref.shape[0]
    float32, bfloat16 = jnp.float32, jnp.bfloat16

    features = [slice(at, at + TILE) for at in range(0, width, TILE)]
    singles = [0.0] * tasks
    for block in features:
        for expert in range(experts):
            total = parts_ref[expert, :, block].astype(float32)
            for at in range(1, dp):
                total = total + parts_ref[at * experts + expert, :, block].astype(float32)
            outs_ref[expert * own : (expert + 1) * own, block] = total
        outs = outs_ref[:, block].astype(bfloat16)
        for task in range(tasks):
            singles[task] = singles[task] + dot(outs, tower_in_ref[task, block, :], (1, 0))

    labels = by_row(labels_ref[...], slots)
    lane = iota((slots, LANES), 1)
    units = tower_in_ref.shape[2]

    def store(value, block):
        for expert in range(experts):
            here = slice(expert * own, (expert + 1) * own)
            for at in range(dp):
                message_ref[at * experts + expert, :, block] = value[here]

    def wide(ref):
        return jnp.concatenate([ref[task : task + 1, :] for task in range(tasks)], 1)

    def lanes_of(value, task):
        return value[:, task * units : (task + 1) * units]

    def each(columns):
        return jnp.concatenate(
            [jnp.broadcast_to(column, (slots, units)) for column in columns], 1
        )

    probs = [prob_ref[:, task : task + 1] for task in range(tasks)]
    single = jnp.concatenate(singles, 1)
    linear = single * each(probs)
    shift = own
    while shift < slots:
        linear = linear + pltpu.roll(linear, shift, 0)
        shift *= 2
    active, slope = gelu_pair(linear + wide(bias_ref))
    weight = wide(weight_ref)
    active, slope = active * weight, slope * weight
    dlogit = []
    for task in range(tasks):
        logit = jnp.sum(lanes_of(active, task), -1, keepdims=True) + shift_ref[:, task : task + 1]
        dlogit.append(jax.nn.sigmoid(logit) - labels[:, task : task + 1])
    dtower = slope * each(dlogit)
    stack = [piece.astype(float32) for piece in pieces_of(dtower)[:2]]
    stack = jnp.concatenate(stack, 0).astype(bfloat16)
    rest = dtower * (single - linear)
    lanes = jnp.zeros((slots, LANES), float32)
    for task in range(tasks):
        dgate = probs[task] * jnp.sum(lanes_of(rest, task), -1, keepdims=True)
        for at, piece in enumerate(pieces_of(dgate)):
            lanes = jnp.where(lane == at * tasks + task, piece.astype(float32), lanes)
    store(lanes.astype(bfloat16), slice(width, width + LANES))
    for block in features:
        dexpert = jnp.zeros((slots, TILE), float32)
        for task in range(tasks):
            turned = dot(lanes_of(stack, task), tower_in_ref[task, block, :], (1, 1))
            dmixed = (turned[:slots] + turned[slots:]).astype(bfloat16)
            dexpert = dexpert + probs[task] * dmixed.astype(float32)
        store(dexpert.astype(bfloat16), block)


def middle(dp, parts, prob, labels, tower_in, bias, weight, shift):
    devices, own, width = parts.shape
    return pl.pallas_call(
        functools.partial(middle_kernel, dp),
        out_shape=pltpu.VMEM((devices, own, width + LANES), jnp.bfloat16),
        scratch_shapes=[pltpu.VMEM((devices // dp * own, width), jnp.float32)],
        compiler_params=params(),
        cost_estimate=cost(4 * 8 * tower_in.size, 2 * tower_in.size),
        name="middle",
    )(parts, prob, labels, in_vmem(tower_in), bias, weight, shift)


def backward_kernel(
    tasks,
    got_ref,
    every_ref,
    hidden_ref,
    pre_ref,
    second_ref,
    grad_first_ref,
    grad_second_ref,
    grad_gate_ref,
    dpre_ref,
    first_buf,
    second_buf,
    gate_buf,
    arrived_ref,
    wide_ref,
    sems,
):
    rows, width = every_ref.shape
    units = pre_ref.shape[1]
    flat = rows <= 64
    blocks = units // TILE
    copies = []

    def gradient(left, right, buf, target, cuts):
        at = 0
        for cut in cuts:
            here = pl.ds(at * LANES, cut * LANES)
            buf[here, :] = dot(left[:, here], right(), (0, 0)).astype(jnp.bfloat16)
            send(buf.at[here, :], target.at[here, :])
            at += cut

    def send(source, target):
        copies.append(pltpu.make_async_copy(source, target, sems.at[len(copies)]))
        copies[-1].start()

    def dpre_step(step):
        here = span(step, TILE)
        dhidden = dot(arrived_ref[:, :width], second_ref[here, :], (1, 1))
        dpre_ref[:, here] = (gelu_pair(pre_ref[:, here])[1] * dhidden).astype(jnp.bfloat16)

    unpack(got_ref, wide_ref)
    arrived_ref[...] = wide_ref[...].astype(jnp.bfloat16)
    pairs = units // LANES // 2 - 1
    gradient(
        hidden_ref,
        lambda: arrived_ref[:, :width],
        second_buf,
        grad_second_ref,
        [1] + [2] * pairs + [1],
    )
    gate = dot(arrived_ref[:, width:], every_ref[...], (0, 0))
    for task in range(tasks):
        lanes = [at * tasks + task for at in range(3)]
        gate_buf[task] = sum(gate[lane : lane + 1] for lane in lanes)
    send(gate_buf, grad_gate_ref)
    steps(blocks, flat, dpre_step)
    pairs = width // LANES // 2 - 1
    gradient(
        every_ref, lambda: dpre_ref[...], first_buf, grad_first_ref, [2] * pairs + [1, 1]
    )
    for copy in copies:
        copy.wait()


def backward(got, every, hidden, pre, second, tasks):
    rows, width = every.shape
    units = pre.shape[1]
    anywhere = pl.BlockSpec(memory_space=pl.ANY)
    inside = pl.BlockSpec(memory_space=pltpu.VMEM)
    return pl.pallas_call(
        functools.partial(backward_kernel, tasks),
        out_shape=[
            jax.ShapeDtypeStruct((width, units), jnp.bfloat16),
            jax.ShapeDtypeStruct((units, width), jnp.bfloat16),
            jax.ShapeDtypeStruct((tasks, 1, width), jnp.float32),
        ],
        in_specs=[inside] * 5,
        out_specs=[anywhere] * 3,
        scratch_shapes=[
            pltpu.VMEM((rows, units), jnp.bfloat16),
            pltpu.VMEM((width, units), jnp.bfloat16),
            pltpu.VMEM((units, width), jnp.bfloat16),
            pltpu.VMEM((tasks, 1, width), jnp.float32),
            pltpu.VMEM((rows, width + LANES), jnp.bfloat16),
            pltpu.VMEM((rows, width + LANES), jnp.float32),
            pltpu.SemaphoreType.DMA((units // TILE + width // TILE + 3,)),
        ],
        compiler_params=params(),
        cost_estimate=cost(6 * rows * width * units, 6 * width * units),
        name="backward",
    )(got, every, hidden, pre, in_vmem(second))


def per_device(
    events, labels, w_in, w_out, gate_weight, tower_in, tower_bias, tower_out, tower_out_bias
):
    dp = lax.axis_size("dp")
    experts = lax.axis_size("expert")
    devices = dp * experts
    tasks = tower_in.shape[0]
    gate = jnp.transpose(gate_weight, (0, 2, 1)).reshape(tasks * experts, events.shape[1])

    got = lax.all_to_all(ahead(spread(events, devices)), BOTH, 0, 0, tiled=True)
    part, every, pre, hidden, prob = forward(got, events, gate, w_in[0], w_out[0], experts)

    parts = lax.all_to_all(part, BOTH, 0, 0, tiled=True)
    message = middle(
        dp, parts, prob, labels, tower_in, tower_bias, tower_out, tower_out_bias[None]
    )

    got = lax.all_to_all(message, BOTH, 0, 0, tiled=True)
    grad_first, grad_second, grad_gate = backward(got, every, hidden, pre, w_out[0], tasks)
    return (grad_first[None], grad_second[None], jnp.transpose(grad_gate, (0, 2, 1)))


def solution(mesh):
    placed = (
        P(BOTH, None),
        P(BOTH, None),
        P("expert", None, "dp"),
        P("expert", "dp", None),
        P(),
        P(),
        P(),
        P(),
        P(),
    )
    return jax.shard_map(
        per_device,
        mesh=mesh,
        in_specs=placed,
        out_specs=(P("expert", None, "dp"), P("expert", "dp", None), P(None, None, "expert")),
        check_vma=False,
    )
```

```python
import functools

import jax
import jax.numpy as jnp
from jax import lax
from jax.experimental import pallas as pl
from jax.experimental.pallas import tpu as pltpu
from jax.sharding import PartitionSpec as P

BOTH = ("dp", "expert")
SLOTS = ("expert", "dp")
LANES = 128
TILE = 256
GELU_C = 0.7978845608028654
GELU_A = 0.044715
AHEAD_FLOPS = 1 << 34
VMEM_LIMIT = 32 * 1024 * 1024


def gelu_pair(value):
    square = value * value
    bend = jnp.tanh(GELU_C * (value + GELU_A * value * square))
    inner = GELU_C * (1.0 + 3.0 * GELU_A * square)
    half = 0.5 * (1.0 + bend)
    return value * half, half + 0.5 * value * (1.0 - bend * bend) * inner


def pieces_of(value):
    high = value.astype(jnp.bfloat16)
    rest = value - high.astype(jnp.float32)
    middle = rest.astype(jnp.bfloat16)
    low = (rest - middle.astype(jnp.float32)).astype(jnp.bfloat16)
    return high, middle, low


def dot(left, right, over):
    return lax.dot_general(
        left, right, ((over[:1], over[1:]), ((), ())), preferred_element_type=jnp.float32
    )


def steps(count, flat, body):
    if flat:
        for step in range(count):
            body(step)
    else:
        lax.fori_loop(0, count, lambda step, none: (body(step), none)[1], None)


def span(step, size):
    return pl.ds(pl.multiple_of(step * size, size), size)


def params():
    return pltpu.CompilerParams(vmem_limit_bytes=VMEM_LIMIT)


def cost(flops, moved):
    return pl.CostEstimate(flops=flops, bytes_accessed=moved, transcendentals=0)


def in_vmem(value):
    return pltpu.with_memory_space_constraint(value, pltpu.VMEM)


def spread_kernel(row_ref, out_ref):
    for step in range(out_ref.shape[0]):
        out_ref[step] = row_ref[...]


def spread(value, devices):
    return pl.pallas_call(
        spread_kernel,
        out_shape=pltpu.VMEM((devices, *value.shape), value.dtype),
        compiler_params=params(),
        name="spread",
    )(value)


def ahead_kernel(value_ref, same_ref):
    del value_ref, same_ref


def ahead(value):
    return pl.pallas_call(
        ahead_kernel,
        in_specs=[pl.BlockSpec(memory_space=pl.ANY)],
        out_specs=pl.BlockSpec(memory_space=pl.ANY),
        out_shape=pltpu.VMEM(value.shape, value.dtype),
        input_output_aliases={0: 0},
        compiler_params=params(),
        cost_estimate=cost(AHEAD_FLOPS, 0),
        name="ahead",
    )(value)


def unpack(message_ref, rows_ref):
    own = message_ref.shape[1]
    for at in range(message_ref.shape[0]):
        rows_ref[at * own : (at + 1) * own, :] = message_ref[at].astype(jnp.float32)


def iota(shape, axis):
    return lax.broadcasted_iota(jnp.int32, shape, axis)


def by_row(value, count):
    own = value.shape[0]
    row = lax.rem(iota((count, value.shape[1]), 0), own)
    result = jnp.zeros(row.shape, jnp.float32)
    for at in range(own):
        result = jnp.where(row == at, value[at : at + 1].astype(jnp.float32), result)
    return result


def forward_kernel(
    got_ref,
    events_ref,
    gate_ref,
    first_ref,
    second_ref,
    part_ref,
    every_ref,
    pre_ref,
    hidden_ref,
    prob_ref,
    wide_ref,
):
    own = got_ref.shape[1]
    rows, width = every_ref.shape
    chunk = min(rows, 64)
    slots = prob_ref.shape[0]
    experts = slots // own
    tasks = gate_ref.shape[0] // experts
    events = by_row(events_ref[...], slots).astype(jnp.bfloat16)
    mine = iota((slots, experts), 0) // own == iota((slots, experts), 1)
    lane = iota((slots, LANES), 1)
    probs = jnp.zeros((slots, LANES), jnp.float32)
    logits = dot(events, gate_ref[...], (1, 1))
    for task in range(tasks):
        gates = logits[:, task * experts : (task + 1) * experts]
        gates = jnp.exp(gates - jnp.max(gates, -1, keepdims=True))
        prob = jnp.sum(jnp.where(mine, gates, 0.0), -1, keepdims=True)
        probs = jnp.where(lane == task, prob / jnp.sum(gates, -1, keepdims=True), probs)
    prob_ref[...] = probs

    unpack(got_ref, wide_ref)

    def body(step):
        here = span(step, chunk)
        every = wide_ref[here, :].astype(jnp.bfloat16)
        every_ref[here, :] = every
        blocks = [slice(at, at + TILE) for at in range(0, first_ref.shape[1], TILE)]
        pre = [dot(every, first_ref[:, block], (1, 0)) for block in blocks]
        part = 0.0
        for block, value in zip(blocks, pre):
            hidden = gelu_pair(value)[0].astype(jnp.bfloat16)
            part = part + dot(hidden, second_ref[block, :], (1, 0))
            pre_ref[here, block] = value
            hidden_ref[here, block] = hidden
        part = part.astype(jnp.bfloat16)
        for at in range(chunk // own):
            part_ref[step * (chunk // own) + at] = part[at * own : (at + 1) * own]

    steps(rows // chunk, rows == chunk, body)


def forward(got, events, gate, first, second, experts):
    devices, own, width = got.shape
    rows = devices * own
    units = first.shape[1]
    return pl.pallas_call(
        forward_kernel,
        out_shape=[
            pltpu.VMEM(got.shape, jnp.bfloat16),
            pltpu.VMEM((rows, width), jnp.bfloat16),
            pltpu.VMEM((rows, units), jnp.float32),
            pltpu.VMEM((rows, units), jnp.bfloat16),
            pltpu.VMEM((experts * own, LANES), jnp.float32),
        ],
        scratch_shapes=[pltpu.VMEM((rows, width), jnp.float32)],
        compiler_params=params(),
        cost_estimate=cost(4 * rows * width * units, 4 * width * units),
        name="forward",
    )(got, events, gate, in_vmem(first), in_vmem(second))


def middle_kernel(
    dp,
    parts_ref,
    prob_ref,
    labels_ref,
    tower_in_ref,
    bias_ref,
    weight_ref,
    shift_ref,
    message_ref,
    outs_ref,
):
    devices, own, width = parts_ref.shape
    experts = devices // dp
    slots = experts * own
    tasks = tower_in_ref.shape[0]
    float32, bfloat16 = jnp.float32, jnp.bfloat16

    features = [slice(at, at + TILE) for at in range(0, width, TILE)]
    singles = [0.0] * tasks
    for block in features:
        for expert in range(experts):
            total = parts_ref[expert * dp, :, block].astype(float32)
            for at in range(1, dp):
                total = total + parts_ref[expert * dp + at, :, block].astype(float32)
            outs_ref[expert * own : (expert + 1) * own, block] = total
        outs = outs_ref[:, block].astype(bfloat16)
        for task in range(tasks):
            singles[task] = singles[task] + dot(outs, tower_in_ref[task, block, :], (1, 0))

    labels = by_row(labels_ref[...], slots)
    lane = iota((slots, LANES), 1)
    units = tower_in_ref.shape[2]

    def store(value, block):
        for expert in range(experts):
            here = slice(expert * own, (expert + 1) * own)
            for at in range(dp):
                message_ref[expert * dp + at, :, block] = value[here]

    def wide(ref):
        return jnp.concatenate([ref[task : task + 1, :] for task in range(tasks)], 1)

    def lanes_of(value, task):
        return value[:, task * units : (task + 1) * units]

    def each(columns):
        return jnp.concatenate(
            [jnp.broadcast_to(column, (slots, units)) for column in columns], 1
        )

    probs = [prob_ref[:, task : task + 1] for task in range(tasks)]
    single = jnp.concatenate(singles, 1)
    linear = single * each(probs)
    shift = own
    while shift < slots:
        linear = linear + pltpu.roll(linear, shift, 0)
        shift *= 2
    active, slope = gelu_pair(linear + wide(bias_ref))
    weight = wide(weight_ref)
    active, slope = active * weight, slope * weight
    dlogit = []
    for task in range(tasks):
        logit = jnp.sum(lanes_of(active, task), -1, keepdims=True) + shift_ref[:, task : task + 1]
        dlogit.append(jax.nn.sigmoid(logit) - labels[:, task : task + 1])
    dtower = slope * each(dlogit)
    stack = [piece.astype(float32) for piece in pieces_of(dtower)[:2]]
    stack = jnp.concatenate(stack, 0).astype(bfloat16)
    rest = dtower * (single - linear)
    lanes = jnp.zeros((slots, LANES), float32)
    for task in range(tasks):
        dgate = probs[task] * jnp.sum(lanes_of(rest, task), -1, keepdims=True)
        for at, piece in enumerate(pieces_of(dgate)):
            lanes = jnp.where(lane == at * tasks + task, piece.astype(float32), lanes)
    store(lanes.astype(bfloat16), slice(width, width + LANES))
    for block in features:
        dexpert = jnp.zeros((slots, TILE), float32)
        for task in range(tasks):
            turned = dot(lanes_of(stack, task), tower_in_ref[task, block, :], (1, 1))
            dmixed = (turned[:slots] + turned[slots:]).astype(bfloat16)
            dexpert = dexpert + probs[task] * dmixed.astype(float32)
        store(dexpert.astype(bfloat16), block)


def middle(dp, parts, prob, labels, tower_in, bias, weight, shift):
    devices, own, width = parts.shape
    return pl.pallas_call(
        functools.partial(middle_kernel, dp),
        out_shape=pltpu.VMEM((devices, own, width + LANES), jnp.bfloat16),
        scratch_shapes=[pltpu.VMEM((devices // dp * own, width), jnp.float32)],
        compiler_params=params(),
        cost_estimate=cost(4 * 8 * tower_in.size, 2 * tower_in.size),
        name="middle",
    )(parts, prob, labels, in_vmem(tower_in), bias, weight, shift)


def backward_kernel(
    tasks,
    got_ref,
    every_ref,
    hidden_ref,
    pre_ref,
    second_ref,
    grad_first_ref,
    grad_second_ref,
    grad_gate_ref,
    dpre_ref,
    first_buf,
    second_buf,
    gate_buf,
    arrived_ref,
    wide_ref,
    sems,
):
    rows, width = every_ref.shape
    units = pre_ref.shape[1]
    flat = rows <= 64
    blocks = units // TILE
    copies = []

    def gradient(left, right, buf, target, cuts):
        at = 0
        for cut in cuts:
            here = pl.ds(at * LANES, cut * LANES)
            buf[here, :] = dot(left[:, here], right(), (0, 0)).astype(jnp.bfloat16)
            send(buf.at[here, :], target.at[here, :])
            at += cut

    def send(source, target):
        copies.append(pltpu.make_async_copy(source, target, sems.at[len(copies)]))
        copies[-1].start()

    def dpre_step(step):
        here = span(step, TILE)
        dhidden = dot(arrived_ref[:, :width], second_ref[here, :], (1, 1))
        dpre_ref[:, here] = (gelu_pair(pre_ref[:, here])[1] * dhidden).astype(jnp.bfloat16)

    unpack(got_ref, wide_ref)
    arrived_ref[...] = wide_ref[...].astype(jnp.bfloat16)
    pairs = units // LANES // 2 - 1
    gradient(
        hidden_ref,
        lambda: arrived_ref[:, :width],
        second_buf,
        grad_second_ref,
        [1] + [2] * pairs + [1],
    )
    gate = dot(arrived_ref[:, width:], every_ref[...], (0, 0))
    for task in range(tasks):
        lanes = [at * tasks + task for at in range(3)]
        gate_buf[task] = sum(gate[lane : lane + 1] for lane in lanes)
    send(gate_buf, grad_gate_ref)
    steps(blocks, flat, dpre_step)
    pairs = width // LANES // 2 - 1
    gradient(
        every_ref, lambda: dpre_ref[...], first_buf, grad_first_ref, [2] * pairs + [1, 1]
    )
    for copy in copies:
        copy.wait()


def backward(got, every, hidden, pre, second, tasks):
    rows, width = every.shape
    units = pre.shape[1]
    anywhere = pl.BlockSpec(memory_space=pl.ANY)
    inside = pl.BlockSpec(memory_space=pltpu.VMEM)
    return pl.pallas_call(
        functools.partial(backward_kernel, tasks),
        out_shape=[
            jax.ShapeDtypeStruct((width, units), jnp.bfloat16),
            jax.ShapeDtypeStruct((units, width), jnp.bfloat16),
            jax.ShapeDtypeStruct((tasks, 1, width), jnp.float32),
        ],
        in_specs=[inside] * 5,
        out_specs=[anywhere] * 3,
        scratch_shapes=[
            pltpu.VMEM((rows, units), jnp.bfloat16),
            pltpu.VMEM((width, units), jnp.bfloat16),
            pltpu.VMEM((units, width), jnp.bfloat16),
            pltpu.VMEM((tasks, 1, width), jnp.float32),
            pltpu.VMEM((rows, width + LANES), jnp.bfloat16),
            pltpu.VMEM((rows, width + LANES), jnp.float32),
            pltpu.SemaphoreType.DMA((units // TILE + width // TILE + 3,)),
        ],
        compiler_params=params(),
        cost_estimate=cost(6 * rows * width * units, 6 * width * units),
        name="backward",
    )(got, every, hidden, pre, in_vmem(second))


def per_device(
    events, labels, w_in, w_out, gate_weight, tower_in, tower_bias, tower_out, tower_out_bias
):
    dp = lax.axis_size("dp")
    experts = lax.axis_size("expert")
    devices = dp * experts
    tasks = tower_in.shape[0]
    gate = jnp.transpose(gate_weight, (0, 2, 1)).reshape(tasks * experts, events.shape[1])

    got = lax.all_to_all(ahead(spread(events, devices)), SLOTS, 0, 0, tiled=True)
    part, every, pre, hidden, prob = forward(got, events, gate, w_in[0], w_out[0], experts)

    parts = lax.all_to_all(part, SLOTS, 0, 0, tiled=True)
    message = middle(
        dp, parts, prob, labels, tower_in, tower_bias, tower_out, tower_out_bias[None]
    )

    got = lax.all_to_all(message, SLOTS, 0, 0, tiled=True)
    grad_first, grad_second, grad_gate = backward(got, every, hidden, pre, w_out[0], tasks)
    return (grad_first[None], grad_second[None], jnp.transpose(grad_gate, (0, 2, 1)))


def solution(mesh):
    placed = (
        P(BOTH, None),
        P(BOTH, None),
        P("expert", None, "dp"),
        P("expert", "dp", None),
        P(),
        P(),
        P(),
        P(),
        P(),
    )
    return jax.shard_map(
        per_device,
        mesh=mesh,
        in_specs=placed,
        out_specs=(P("expert", None, "dp"), P("expert", "dp", None), P(None, None, "expert")),
        check_vma=False,
    )
```

```python
import functools

import jax
import jax.numpy as jnp
from jax import lax
from jax.experimental import pallas as pl
from jax.experimental.pallas import tpu as pltpu
from jax.sharding import PartitionSpec as P

BOTH = ("dp", "expert")
LANES = 128
TILE = 256
GELU_C = 0.7978845608028654
GELU_A = 0.044715
AHEAD_FLOPS = 1 << 34
VMEM_LIMIT = 32 * 1024 * 1024


def gelu_pair(value):
    square = value * value
    bend = jnp.tanh(GELU_C * (value + GELU_A * value * square))
    inner = GELU_C * (1.0 + 3.0 * GELU_A * square)
    half = 0.5 * (1.0 + bend)
    return value * half, half + 0.5 * value * (1.0 - bend * bend) * inner


def pieces_of(value):
    high = value.astype(jnp.bfloat16)
    rest = value - high.astype(jnp.float32)
    middle = rest.astype(jnp.bfloat16)
    low = (rest - middle.astype(jnp.float32)).astype(jnp.bfloat16)
    return high, middle, low


def dot(left, right, over):
    return lax.dot_general(
        left, right, ((over[:1], over[1:]), ((), ())), preferred_element_type=jnp.float32
    )


def steps(count, flat, body):
    if flat:
        for step in range(count):
            body(step)
    else:
        lax.fori_loop(0, count, lambda step, none: (body(step), none)[1], None)


def span(step, size):
    return pl.ds(pl.multiple_of(step * size, size), size)


def params():
    return pltpu.CompilerParams(vmem_limit_bytes=VMEM_LIMIT)


def cost(flops, moved):
    return pl.CostEstimate(flops=flops, bytes_accessed=moved, transcendentals=0)


def in_vmem(value):
    return pltpu.with_memory_space_constraint(value, pltpu.VMEM)


def spread_kernel(row_ref, out_ref):
    for step in range(out_ref.shape[0]):
        out_ref[step] = row_ref[...]


def spread(value, devices):
    return pl.pallas_call(
        spread_kernel,
        out_shape=pltpu.VMEM((devices, *value.shape), value.dtype),
        compiler_params=params(),
        name="spread",
    )(value)


def ahead_kernel(value_ref, same_ref):
    del value_ref, same_ref


def ahead(value):
    return pl.pallas_call(
        ahead_kernel,
        in_specs=[pl.BlockSpec(memory_space=pl.ANY)],
        out_specs=pl.BlockSpec(memory_space=pl.ANY),
        out_shape=pltpu.VMEM(value.shape, value.dtype),
        input_output_aliases={0: 0},
        compiler_params=params(),
        cost_estimate=cost(AHEAD_FLOPS, 0),
        name="ahead",
    )(value)


def unpack(message_ref, rows_ref, block):
    own = message_ref.shape[1]
    for at in range(message_ref.shape[0]):
        here = slice(at * own, (at + 1) * own)
        rows_ref[here, block] = message_ref[at, :, block].astype(jnp.float32)


def blocks_of(count, size):
    return [slice(at, at + size) for at in range(0, count, size)]


def iota(shape, axis):
    return lax.broadcasted_iota(jnp.int32, shape, axis)


def by_row(value, count):
    own = value.shape[0]
    row = lax.rem(iota((count, value.shape[1]), 0), own)
    result = jnp.zeros(row.shape, jnp.float32)
    for at in range(own):
        result = jnp.where(row == at, value[at : at + 1].astype(jnp.float32), result)
    return result


def forward_kernel(
    got_ref,
    events_ref,
    gate_ref,
    first_ref,
    second_ref,
    part_ref,
    every_ref,
    pre_ref,
    hidden_ref,
    prob_ref,
    wide_ref,
):
    own = got_ref.shape[1]
    rows, width = every_ref.shape
    chunk = min(rows, 64)
    slots = prob_ref.shape[0]
    experts = slots // own
    tasks = gate_ref.shape[0] // experts
    events = by_row(events_ref[...], slots).astype(jnp.bfloat16)
    mine = iota((slots, experts), 0) // own == iota((slots, experts), 1)
    lane = iota((slots, LANES), 1)
    probs = jnp.zeros((slots, LANES), jnp.float32)
    logits = dot(events, gate_ref[...], (1, 1))
    for task in range(tasks):
        gates = logits[:, task * experts : (task + 1) * experts]
        gates = jnp.exp(gates - jnp.max(gates, -1, keepdims=True))
        prob = jnp.sum(jnp.where(mine, gates, 0.0), -1, keepdims=True)
        probs = jnp.where(lane == task, prob / jnp.sum(gates, -1, keepdims=True), probs)
    prob_ref[...] = probs

    halves = blocks_of(every_ref.shape[1], every_ref.shape[1] // 2)
    if rows != chunk:
        unpack(got_ref, wide_ref, slice(None))

    def body(step):
        here = span(step, chunk)
        blocks = blocks_of(first_ref.shape[1], TILE)
        pre = [0.0] * len(blocks)
        for half in halves:
            if rows == chunk:
                unpack(got_ref, wide_ref, half)
            every = wide_ref[here, half].astype(jnp.bfloat16)
            every_ref[here, half] = every
            for at, block in enumerate(blocks):
                pre[at] = pre[at] + dot(every, first_ref[half, block], (1, 0))
        part = 0.0
        for block, value in zip(blocks, pre):
            hidden = gelu_pair(value)[0].astype(jnp.bfloat16)
            part = part + dot(hidden, second_ref[block, :], (1, 0))
            pre_ref[here, block] = value
            hidden_ref[here, block] = hidden
        part = part.astype(jnp.bfloat16)
        for at in range(chunk // own):
            part_ref[step * (chunk // own) + at] = part[at * own : (at + 1) * own]

    steps(rows // chunk, rows == chunk, body)


def forward(got, events, gate, first, second, experts):
    devices, own, width = got.shape
    rows = devices * own
    units = first.shape[1]
    return pl.pallas_call(
        forward_kernel,
        out_shape=[
            pltpu.VMEM(got.shape, jnp.bfloat16),
            pltpu.VMEM((rows, width), jnp.bfloat16),
            pltpu.VMEM((rows, units), jnp.float32),
            pltpu.VMEM((rows, units), jnp.bfloat16),
            pltpu.VMEM((experts * own, LANES), jnp.float32),
        ],
        scratch_shapes=[pltpu.VMEM((rows, width), jnp.float32)],
        compiler_params=params(),
        cost_estimate=cost(4 * rows * width * units, 4 * width * units),
        name="forward",
    )(got, events, gate, in_vmem(first), in_vmem(second))


def middle_kernel(
    dp,
    parts_ref,
    prob_ref,
    labels_ref,
    tower_in_ref,
    bias_ref,
    weight_ref,
    shift_ref,
    message_ref,
    outs_ref,
):
    devices, own, width = parts_ref.shape
    experts = devices // dp
    slots = experts * own
    tasks = tower_in_ref.shape[0]
    float32, bfloat16 = jnp.float32, jnp.bfloat16

    features = blocks_of(width, TILE)
    singles = [0.0] * tasks
    for block in features:
        for expert in range(experts):
            total = parts_ref[expert, :, block].astype(float32)
            for at in range(1, dp):
                total = total + parts_ref[at * experts + expert, :, block].astype(float32)
            outs_ref[expert * own : (expert + 1) * own, block] = total
        outs = outs_ref[:, block].astype(bfloat16)
        for task in range(tasks):
            singles[task] = singles[task] + dot(outs, tower_in_ref[task, block, :], (1, 0))

    labels = by_row(labels_ref[...], slots)
    lane = iota((slots, LANES), 1)
    units = tower_in_ref.shape[2]

    def store(value, block):
        for expert in range(experts):
            here = slice(expert * own, (expert + 1) * own)
            for at in range(dp):
                message_ref[at * experts + expert, :, block] = value[here]

    def wide(ref):
        return jnp.concatenate([ref[task : task + 1, :] for task in range(tasks)], 1)

    def lanes_of(value, task):
        return value[:, task * units : (task + 1) * units]

    def each(columns):
        return jnp.concatenate(
            [jnp.broadcast_to(column, (slots, units)) for column in columns], 1
        )

    probs = [prob_ref[:, task : task + 1] for task in range(tasks)]
    single = jnp.concatenate(singles, 1)
    linear = single * each(probs)
    shift = own
    while shift < slots:
        linear = linear + pltpu.roll(linear, shift, 0)
        shift *= 2
    active, slope = gelu_pair(linear + wide(bias_ref))
    weight = wide(weight_ref)
    active, slope = active * weight, slope * weight
    dlogit = []
    for task in range(tasks):
        logit = jnp.sum(lanes_of(active, task), -1, keepdims=True) + shift_ref[:, task : task + 1]
        dlogit.append(jax.nn.sigmoid(logit) - labels[:, task : task + 1])
    dtower = slope * each(dlogit)
    stack = [piece.astype(float32) for piece in pieces_of(dtower)[:2]]
    stack = jnp.concatenate(stack, 0).astype(bfloat16)
    rest = dtower * (single - linear)
    lanes = jnp.zeros((slots, LANES), float32)
    for task in range(tasks):
        dgate = probs[task] * jnp.sum(lanes_of(rest, task), -1, keepdims=True)
        for at, piece in enumerate(pieces_of(dgate)):
            lanes = jnp.where(lane == at * tasks + task, piece.astype(float32), lanes)
    store(lanes.astype(bfloat16), slice(width, width + LANES))
    for block in features:
        dexpert = jnp.zeros((slots, TILE), float32)
        for task in range(tasks):
            turned = dot(lanes_of(stack, task), tower_in_ref[task, block, :], (1, 1))
            dmixed = (turned[:slots] + turned[slots:]).astype(bfloat16)
            dexpert = dexpert + probs[task] * dmixed.astype(float32)
        store(dexpert.astype(bfloat16), block)


def middle(dp, parts, prob, labels, tower_in, bias, weight, shift):
    devices, own, width = parts.shape
    return pl.pallas_call(
        functools.partial(middle_kernel, dp),
        out_shape=pltpu.VMEM((devices, own, width + LANES), jnp.bfloat16),
        scratch_shapes=[pltpu.VMEM((devices // dp * own, width), jnp.float32)],
        compiler_params=params(),
        cost_estimate=cost(4 * 8 * tower_in.size, 2 * tower_in.size),
        name="middle",
    )(parts, prob, labels, in_vmem(tower_in), bias, weight, shift)


def backward_kernel(
    tasks,
    got_ref,
    every_ref,
    hidden_ref,
    pre_ref,
    second_ref,
    grad_first_ref,
    grad_second_ref,
    grad_gate_ref,
    dpre_ref,
    first_buf,
    second_buf,
    gate_buf,
    arrived_ref,
    wide_ref,
    sems,
):
    rows, width = every_ref.shape
    units = pre_ref.shape[1]
    flat = rows <= 64
    blocks = units // TILE
    copies = []

    def gradient(left, right, buf, target, cuts, at=0):
        for cut in cuts:
            here = pl.ds(at * LANES, cut * LANES)
            buf[here, :] = dot(left[:, here], right(), (0, 0)).astype(jnp.bfloat16)
            send(buf.at[here, :], target.at[here, :])
            at += cut

    def send(source, target):
        copies.append(pltpu.make_async_copy(source, target, sems.at[len(copies)]))
        copies[-1].start()

    def dpre_step(step):
        here = span(step, TILE)
        dhidden = dot(arrived_ref[:, :width], second_ref[here, :], (1, 1))
        dpre_ref[:, here] = (gelu_pair(pre_ref[:, here])[1] * dhidden).astype(jnp.bfloat16)

    top = slice(0, TILE)
    for block in blocks_of(width, TILE) + [slice(width, width + LANES)]:
        unpack(got_ref, wide_ref, block)
        arrived_ref[:, block] = wide_ref[:, block].astype(jnp.bfloat16)
        if block.stop <= width:
            second_buf[top, block] = dot(
                hidden_ref[:, top], arrived_ref[:, block], (0, 0)
            ).astype(jnp.bfloat16)
    send(second_buf.at[top, :], grad_second_ref.at[top, :])
    gradient(
        hidden_ref,
        lambda: arrived_ref[:, :width],
        second_buf,
        grad_second_ref,
        [2] * (units // TILE - 1),
        TILE // LANES,
    )
    gate = dot(arrived_ref[:, width:], every_ref[...], (0, 0))
    for task in range(tasks):
        lanes = [at * tasks + task for at in range(3)]
        gate_buf[task] = sum(gate[lane : lane + 1] for lane in lanes)
    send(gate_buf, grad_gate_ref)
    steps(blocks, flat, dpre_step)
    pairs = width // LANES // 2 - 1
    gradient(
        every_ref, lambda: dpre_ref[...], first_buf, grad_first_ref, [2] * pairs + [1, 1]
    )
    for copy in copies:
        copy.wait()


def backward(got, every, hidden, pre, second, tasks):
    rows, width = every.shape
    units = pre.shape[1]
    anywhere = pl.BlockSpec(memory_space=pl.ANY)
    inside = pl.BlockSpec(memory_space=pltpu.VMEM)
    return pl.pallas_call(
        functools.partial(backward_kernel, tasks),
        out_shape=[
            jax.ShapeDtypeStruct((width, units), jnp.bfloat16),
            jax.ShapeDtypeStruct((units, width), jnp.bfloat16),
            jax.ShapeDtypeStruct((tasks, 1, width), jnp.float32),
        ],
        in_specs=[inside] * 5,
        out_specs=[anywhere] * 3,
        scratch_shapes=[
            pltpu.VMEM((rows, units), jnp.bfloat16),
            pltpu.VMEM((width, units), jnp.bfloat16),
            pltpu.VMEM((units, width), jnp.bfloat16),
            pltpu.VMEM((tasks, 1, width), jnp.float32),
            pltpu.VMEM((rows, width + LANES), jnp.bfloat16),
            pltpu.VMEM((rows, width + LANES), jnp.float32),
            pltpu.SemaphoreType.DMA((units // TILE + width // TILE + 3,)),
        ],
        compiler_params=params(),
        cost_estimate=cost(6 * rows * width * units, 6 * width * units),
        name="backward",
    )(got, every, hidden, pre, in_vmem(second))


def per_device(
    events, labels, w_in, w_out, gate_weight, tower_in, tower_bias, tower_out, tower_out_bias
):
    dp = lax.axis_size("dp")
    experts = lax.axis_size("expert")
    devices = dp * experts
    tasks = tower_in.shape[0]
    gate = jnp.transpose(gate_weight, (0, 2, 1)).reshape(tasks * experts, events.shape[1])

    got = lax.all_to_all(ahead(spread(events, devices)), BOTH, 0, 0, tiled=True)
    part, every, pre, hidden, prob = forward(got, events, gate, w_in[0], w_out[0], experts)

    parts = lax.all_to_all(part, BOTH, 0, 0, tiled=True)
    message = middle(
        dp, parts, prob, labels, tower_in, tower_bias, tower_out, tower_out_bias[None]
    )

    got = lax.all_to_all(message, BOTH, 0, 0, tiled=True)
    grad_first, grad_second, grad_gate = backward(got, every, hidden, pre, w_out[0], tasks)
    return (grad_first[None], grad_second[None], jnp.transpose(grad_gate, (0, 2, 1)))


def solution(mesh):
    placed = (
        P(BOTH, None),
        P(BOTH, None),
        P("expert", None, "dp"),
        P("expert", "dp", None),
        P(),
        P(),
        P(),
        P(),
        P(),
    )
    return jax.shard_map(
        per_device,
        mesh=mesh,
        in_specs=placed,
        out_specs=(P("expert", None, "dp"), P("expert", "dp", None), P(None, None, "expert")),
        check_vma=False,
    )
```

```python
import functools

import jax
import jax.numpy as jnp
from jax import lax
from jax.experimental import pallas as pl
from jax.experimental.pallas import tpu as pltpu
from jax.sharding import PartitionSpec as P

BOTH = ("dp", "expert")
LANES = 128
TILE = 256
GELU_C = 0.7978845608028654
GELU_A = 0.044715
AHEAD_FLOPS = 1 << 34
VMEM_LIMIT = 32 * 1024 * 1024


def gelu_pair(value):
    square = value * value
    bend = jnp.tanh(GELU_C * (value + GELU_A * value * square))
    inner = GELU_C * (1.0 + 3.0 * GELU_A * square)
    half = 0.5 * (1.0 + bend)
    return value * half, half + 0.5 * value * (1.0 - bend * bend) * inner


def pieces_of(value):
    high = value.astype(jnp.bfloat16)
    rest = value - high.astype(jnp.float32)
    middle = rest.astype(jnp.bfloat16)
    low = (rest - middle.astype(jnp.float32)).astype(jnp.bfloat16)
    return high, middle, low


def dot(left, right, over):
    return lax.dot_general(
        left, right, ((over[:1], over[1:]), ((), ())), preferred_element_type=jnp.float32
    )


def steps(count, flat, body):
    if flat:
        for step in range(count):
            body(step)
    else:
        lax.fori_loop(0, count, lambda step, none: (body(step), none)[1], None)


def span(step, size):
    return pl.ds(pl.multiple_of(step * size, size), size)


def params():
    return pltpu.CompilerParams(vmem_limit_bytes=VMEM_LIMIT)


def cost(flops, moved):
    return pl.CostEstimate(flops=flops, bytes_accessed=moved, transcendentals=0)


def in_vmem(value):
    return pltpu.with_memory_space_constraint(value, pltpu.VMEM)


def spread_kernel(row_ref, out_ref):
    for step in range(out_ref.shape[0]):
        out_ref[step] = row_ref[...]


def spread(value, devices):
    return pl.pallas_call(
        spread_kernel,
        out_shape=pltpu.VMEM((devices, *value.shape), value.dtype),
        compiler_params=params(),
        name="spread",
    )(value)


def ahead_kernel(value_ref, same_ref):
    del value_ref, same_ref


def ahead(value):
    return pl.pallas_call(
        ahead_kernel,
        in_specs=[pl.BlockSpec(memory_space=pl.ANY)],
        out_specs=pl.BlockSpec(memory_space=pl.ANY),
        out_shape=pltpu.VMEM(value.shape, value.dtype),
        input_output_aliases={0: 0},
        compiler_params=params(),
        cost_estimate=cost(AHEAD_FLOPS, 0),
        name="ahead",
    )(value)


def unpack(message_ref, rows_ref, block):
    own = message_ref.shape[1]
    for at in range(message_ref.shape[0]):
        here = slice(at * own, (at + 1) * own)
        rows_ref[here, block] = message_ref[at, :, block].astype(jnp.float32)


def blocks_of(count, size):
    return [slice(at, at + size) for at in range(0, count, size)]


def iota(shape, axis):
    return lax.broadcasted_iota(jnp.int32, shape, axis)


def by_row(value, count):
    own = value.shape[0]
    row = lax.rem(iota((count, value.shape[1]), 0), own)
    result = jnp.zeros(row.shape, jnp.float32)
    for at in range(own):
        result = jnp.where(row == at, value[at : at + 1].astype(jnp.float32), result)
    return result


def forward_kernel(
    got_ref,
    events_ref,
    gate_ref,
    first_ref,
    second_ref,
    part_ref,
    every_ref,
    pre_ref,
    hidden_ref,
    prob_ref,
    wide_ref,
):
    own = got_ref.shape[1]
    rows, width = every_ref.shape
    chunk = min(rows, 64)
    slots = prob_ref.shape[0]
    experts = slots // own
    tasks = gate_ref.shape[0] // experts
    events = by_row(events_ref[...], slots).astype(jnp.bfloat16)
    mine = iota((slots, experts), 0) // own == iota((slots, experts), 1)
    lane = iota((slots, LANES), 1)
    probs = jnp.zeros((slots, LANES), jnp.float32)
    logits = dot(events, gate_ref[...], (1, 1))
    for task in range(tasks):
        gates = logits[:, task * experts : (task + 1) * experts]
        gates = jnp.exp(gates - jnp.max(gates, -1, keepdims=True))
        prob = jnp.sum(jnp.where(mine, gates, 0.0), -1, keepdims=True)
        probs = jnp.where(lane == task, prob / jnp.sum(gates, -1, keepdims=True), probs)
    prob_ref[...] = probs

    halves = blocks_of(every_ref.shape[1], every_ref.shape[1] // 2)
    if rows != chunk:
        unpack(got_ref, wide_ref, slice(None))

    def body(step):
        here = span(step, chunk)
        blocks = blocks_of(first_ref.shape[1], TILE)
        pre = [0.0] * len(blocks)
        for half in halves:
            if rows == chunk:
                unpack(got_ref, wide_ref, half)
            every = wide_ref[here, half].astype(jnp.bfloat16)
            every_ref[here, half] = every
            for at, block in enumerate(blocks):
                pre[at] = pre[at] + dot(every, first_ref[half, block], (1, 0))
        part = 0.0
        for block, value in zip(blocks, pre):
            hidden = gelu_pair(value)[0].astype(jnp.bfloat16)
            part = part + dot(hidden, second_ref[block, :], (1, 0))
            pre_ref[here, block] = value
            hidden_ref[here, block] = hidden
        part = part.astype(jnp.bfloat16)
        for at in range(chunk // own):
            part_ref[step * (chunk // own) + at] = part[at * own : (at + 1) * own]

    steps(rows // chunk, rows == chunk, body)


def forward(got, events, gate, first, second, experts):
    devices, own, width = got.shape
    rows = devices * own
    units = first.shape[1]
    return pl.pallas_call(
        forward_kernel,
        out_shape=[
            pltpu.VMEM(got.shape, jnp.bfloat16),
            pltpu.VMEM((rows, width), jnp.bfloat16),
            pltpu.VMEM((rows, units), jnp.float32),
            pltpu.VMEM((rows, units), jnp.bfloat16),
            pltpu.VMEM((experts * own, LANES), jnp.float32),
        ],
        scratch_shapes=[pltpu.VMEM((rows, width), jnp.float32)],
        compiler_params=params(),
        cost_estimate=cost(4 * rows * width * units, 4 * width * units),
        name="forward",
    )(got, events, gate, in_vmem(first), in_vmem(second))


def middle_kernel(
    dp,
    parts_ref,
    prob_ref,
    labels_ref,
    tower_in_ref,
    bias_ref,
    weight_ref,
    shift_ref,
    message_ref,
    outs_ref,
):
    devices, own, width = parts_ref.shape
    experts = devices // dp
    slots = experts * own
    tasks = tower_in_ref.shape[0]
    float32, bfloat16 = jnp.float32, jnp.bfloat16

    features = blocks_of(width, TILE)
    singles = [0.0] * tasks
    for block in features:
        for expert in range(experts):
            total = parts_ref[expert, :, block].astype(float32)
            for at in range(1, dp):
                total = total + parts_ref[at * experts + expert, :, block].astype(float32)
            outs_ref[expert * own : (expert + 1) * own, block] = total
        outs = outs_ref[:, block].astype(bfloat16)
        for task in range(tasks):
            singles[task] = singles[task] + dot(outs, tower_in_ref[task, block, :], (1, 0))

    labels = by_row(labels_ref[...], slots)
    lane = iota((slots, LANES), 1)
    units = tower_in_ref.shape[2]

    def store(value, block):
        for expert in range(experts):
            here = slice(expert * own, (expert + 1) * own)
            for at in range(dp):
                message_ref[at * experts + expert, :, block] = value[here]

    def wide(ref):
        return jnp.concatenate([ref[task : task + 1, :] for task in range(tasks)], 1)

    def lanes_of(value, task):
        return value[:, task * units : (task + 1) * units]

    def each(columns):
        return jnp.concatenate(
            [jnp.broadcast_to(column, (slots, units)) for column in columns], 1
        )

    probs = [prob_ref[:, task : task + 1] for task in range(tasks)]
    single = jnp.concatenate(singles, 1)
    linear = single * each(probs)
    shift = own
    while shift < slots:
        linear = linear + pltpu.roll(linear, shift, 0)
        shift *= 2
    active, slope = gelu_pair(linear + wide(bias_ref))
    weight = wide(weight_ref)
    active, slope = active * weight, slope * weight
    dlogit = []
    for task in range(tasks):
        logit = jnp.sum(lanes_of(active, task), -1, keepdims=True) + shift_ref[:, task : task + 1]
        dlogit.append(jax.nn.sigmoid(logit) - labels[:, task : task + 1])
    dtower = slope * each(dlogit)
    stack = [piece.astype(float32) for piece in pieces_of(dtower)[:2]]
    stack = jnp.concatenate(stack, 0).astype(bfloat16)
    rest = dtower * (single - linear)
    lanes = jnp.zeros((slots, LANES), float32)
    for task in range(tasks):
        dgate = probs[task] * jnp.sum(lanes_of(rest, task), -1, keepdims=True)
        for at, piece in enumerate(pieces_of(dgate)):
            lanes = jnp.where(lane == at * tasks + task, piece.astype(float32), lanes)
    store(lanes.astype(bfloat16), slice(width, width + LANES))
    for block in features:
        dexpert = jnp.zeros((slots, TILE), float32)
        for task in range(tasks):
            turned = dot(lanes_of(stack, task), tower_in_ref[task, block, :], (1, 1))
            dmixed = (turned[:slots] + turned[slots:]).astype(bfloat16)
            dexpert = dexpert + probs[task] * dmixed.astype(float32)
        store(dexpert.astype(bfloat16), block)


def middle(dp, parts, prob, labels, tower_in, bias, weight, shift):
    devices, own, width = parts.shape
    return pl.pallas_call(
        functools.partial(middle_kernel, dp),
        out_shape=pltpu.VMEM((devices, own, width + LANES), jnp.bfloat16),
        scratch_shapes=[pltpu.VMEM((devices // dp * own, width), jnp.float32)],
        compiler_params=params(),
        cost_estimate=cost(4 * 8 * tower_in.size, 2 * tower_in.size),
        name="middle",
    )(parts, prob, labels, in_vmem(tower_in), bias, weight, shift)


def backward_kernel(
    tasks,
    got_ref,
    every_ref,
    hidden_ref,
    pre_ref,
    second_ref,
    grad_first_ref,
    grad_second_ref,
    grad_gate_ref,
    dpre_ref,
    first_buf,
    second_buf,
    gate_buf,
    arrived_ref,
    wide_ref,
    sems,
):
    rows, width = every_ref.shape
    units = pre_ref.shape[1]
    flat = rows <= 64
    blocks = units // TILE
    copies = []

    def gradient(left, right, buf, target, cuts, at=0):
        for cut in cuts:
            here = pl.ds(at * LANES, cut * LANES)
            buf[here, :] = dot(left[:, here], right(), (0, 0)).astype(jnp.bfloat16)
            send(buf.at[here, :], target.at[here, :])
            at += cut

    def send(source, target):
        copies.append(pltpu.make_async_copy(source, target, sems.at[len(copies)]))
        copies[-1].start()

    def dpre_step(step):
        here = span(step, TILE)
        dhidden = dot(arrived_ref[:, :width], second_ref[here, :], (1, 1))
        dpre_ref[:, here] = (gelu_pair(pre_ref[:, here])[1] * dhidden).astype(jnp.bfloat16)

    top = slice(0, TILE)
    for block in blocks_of(width, TILE) + [slice(width, width + LANES)]:
        unpack(got_ref, wide_ref, block)
        arrived_ref[:, block] = wide_ref[:, block].astype(jnp.bfloat16)
        if block.stop <= width:
            second_buf[top, block] = dot(
                hidden_ref[:, top], arrived_ref[:, block], (0, 0)
            ).astype(jnp.bfloat16)
    send(second_buf.at[top, :], grad_second_ref.at[top, :])
    gradient(
        hidden_ref,
        lambda: arrived_ref[:, :width],
        second_buf,
        grad_second_ref,
        [2] * (units // TILE - 1),
        TILE // LANES,
    )
    steps(blocks, flat, dpre_step)
    pairs = width // LANES // 2 - 1
    gradient(every_ref, lambda: dpre_ref[...], first_buf, grad_first_ref, [2])
    gate = dot(arrived_ref[:, width:], every_ref[...], (0, 0))
    for task in range(tasks):
        lanes = [at * tasks + task for at in range(3)]
        gate_buf[task] = sum(gate[lane : lane + 1] for lane in lanes)
    send(gate_buf, grad_gate_ref)
    gradient(
        every_ref,
        lambda: dpre_ref[...],
        first_buf,
        grad_first_ref,
        [2] * (pairs - 1) + [1, 1],
        TILE // LANES,
    )
    for copy in copies:
        copy.wait()


def backward(got, every, hidden, pre, second, tasks):
    rows, width = every.shape
    units = pre.shape[1]
    anywhere = pl.BlockSpec(memory_space=pl.ANY)
    inside = pl.BlockSpec(memory_space=pltpu.VMEM)
    return pl.pallas_call(
        functools.partial(backward_kernel, tasks),
        out_shape=[
            jax.ShapeDtypeStruct((width, units), jnp.bfloat16),
            jax.ShapeDtypeStruct((units, width), jnp.bfloat16),
            jax.ShapeDtypeStruct((tasks, 1, width), jnp.float32),
        ],
        in_specs=[inside] * 5,
        out_specs=[anywhere] * 3,
        scratch_shapes=[
            pltpu.VMEM((rows, units), jnp.bfloat16),
            pltpu.VMEM((width, units), jnp.bfloat16),
            pltpu.VMEM((units, width), jnp.bfloat16),
            pltpu.VMEM((tasks, 1, width), jnp.float32),
            pltpu.VMEM((rows, width + LANES), jnp.bfloat16),
            pltpu.VMEM((rows, width + LANES), jnp.float32),
            pltpu.SemaphoreType.DMA((units // TILE + width // TILE + 3,)),
        ],
        compiler_params=params(),
        cost_estimate=cost(6 * rows * width * units, 6 * width * units),
        name="backward",
    )(got, every, hidden, pre, in_vmem(second))


def per_device(
    events, labels, w_in, w_out, gate_weight, tower_in, tower_bias, tower_out, tower_out_bias
):
    dp = lax.axis_size("dp")
    experts = lax.axis_size("expert")
    devices = dp * experts
    tasks = tower_in.shape[0]
    gate = jnp.transpose(gate_weight, (0, 2, 1)).reshape(tasks * experts, events.shape[1])

    got = lax.all_to_all(ahead(spread(events, devices)), BOTH, 0, 0, tiled=True)
    part, every, pre, hidden, prob = forward(got, events, gate, w_in[0], w_out[0], experts)

    parts = lax.all_to_all(part, BOTH, 0, 0, tiled=True)
    message = middle(
        dp, parts, prob, labels, tower_in, tower_bias, tower_out, tower_out_bias[None]
    )

    got = lax.all_to_all(message, BOTH, 0, 0, tiled=True)
    grad_first, grad_second, grad_gate = backward(got, every, hidden, pre, w_out[0], tasks)
    return (grad_first[None], grad_second[None], jnp.transpose(grad_gate, (0, 2, 1)))


def solution(mesh):
    placed = (
        P(BOTH, None),
        P(BOTH, None),
        P("expert", None, "dp"),
        P("expert", "dp", None),
        P(),
        P(),
        P(),
        P(),
        P(),
    )
    return jax.shard_map(
        per_device,
        mesh=mesh,
        in_specs=placed,
        out_specs=(P("expert", None, "dp"), P("expert", "dp", None), P(None, None, "expert")),
        check_vma=False,
    )
```
